32 devices in a mesh: seq: 2 (over y), dp: 16 (over z, x, core).
Axes of the slice: x: 2, y: 2, z: 4, core: 2. Of those that a mesh axis runs over, the one named last changes fastest.
Arguments:
- tokens: bfloat16 [16, 2560, 768], P('dp', 'seq'), may hold values from -6 to 6
- cotangent: bfloat16 [16, 2560, 768], P('dp', 'seq'), may hold values from -6 to 6
- lengths: int32 [16, 5], P('dp'), may hold values from 0 to 2048, as said below
- threshold: int32 [1], replicated, may hold values from 0 to 1023
- attn_gain: float32 [768], replicated, may hold values from 0.25 to 1.75
- qkv_weight: bfloat16 [768, 2304], replicated, may hold values from -0.21875 to 0.21875
- out_weight: bfloat16 [768, 768], replicated, may hold values from -1 to 1
- mlp_gain: float32 [768], replicated, may hold values from 0.25 to 1.75
- up_weight: bfloat16 [768, 3072], replicated, may hold values from -0.21875 to 0.21875
- down_weight: bfloat16 [3072, 768], replicated, may hold values from -0.109375 to 0.109375
Outputs:
- output: bfloat16 [16, 2560, 768], P('dp', 'seq')
- input_grad: bfloat16 [16, 2560, 768], P('dp', 'seq')
- attn_gain_grad: float32 [768], P('dp')
- qkv_weight_grad: float32 [768, 2304], P('dp')
- out_weight_grad: float32 [768, 768], P('dp')
- mlp_gain_grad: float32 [768], P('dp')
- up_weight_grad: float32 [768, 3072], P('dp')
- down_weight_grad: float32 [3072, 768], P('dp')
- excess: float32 [1], replicated
The draws below stay inside these ranges and needn't reach their ends.
Inputs may be any that keep to these rules, and one draw needn't show every extreme that they name: `lengths`: each row is either 2048 and 512 in some order followed by three zeros, or 512 five times; every row sums to 2560; row 0 holds a sequence of 2048.
All inputs are finite; a program needn't handle non-finite values.
Results may differ from the reference program's by a relative error of at most 0.014.
Values may be sent and summed in bfloat16 or wider, within the bound.
No kernel may reach another device: no remote copies, remote signals or barrier semaphores. Data moves between devices by JAX's collectives and lax.ppermute only.
A program may use at most 448 MiB of HBM per device.

```python
import jax
import jax.numpy as jnp
from jax import lax

D = 768
HEADS = 12
HEAD_DIM = 64
FF = 3072
SHORT = 512
LONG = 2048
PACK = 2560
PACKS = 16


def draw_lengths(key, part):
    layout = jax.random.randint(key, (PACKS,), 0, 3)
    first_kind = jax.random.randint(jax.random.fold_in(key, 11), (), 0, 2)
    layout = jnp.where(jnp.arange(PACKS) == 0, first_kind, layout)
    layouts = jnp.array([[LONG, SHORT, 0, 0, 0], [SHORT, LONG, 0, 0, 0], [SHORT, SHORT, SHORT, SHORT, SHORT]], dtype=jnp.int32)
    picked = jnp.sum(jnp.where(layout[:, None, None] == jnp.arange(3)[None, :, None], layouts[None, :, :], 0), axis=1)
    return picked.astype(jnp.int32)


def block_scale(key, shape, split, smallest, top_value):
    factor_of, own = 1.0, jax.random.fold_in(key, 6)
    for position, parts in split:
        steps = jnp.exp(jax.random.uniform(jax.random.fold_in(own, position), (parts,), jnp.float32, smallest / len(split), top_value / len(split)))
        factor_of = factor_of * jnp.repeat(steps, shape[position] // parts).reshape([-1 if axis == position else 1 for axis in range(len(shape))])
    return factor_of


def gaussian(rng, dims, deviation, bound, cuts=(), kind=jnp.bfloat16):
    loudness = block_scale(rng, dims, cuts, -0.22, 0.18) if cuts else 1.0
    values = jax.random.normal(rng, dims, jnp.float32) * deviation * loudness
    return jnp.minimum(jnp.maximum(values, -bound), bound).astype(kind)


def setup_inputs(seed: int = 0) -> dict:
    streams_of = jax.random.split(jax.random.key(seed), 11)
    return {
        "tokens": gaussian(streams_of[0], (PACKS, PACK, D), 1.0, 6.0, ((0, 16), (1, 2))),
        "cotangent": gaussian(streams_of[1], (PACKS, PACK, D), 1.0, 6.0, ((0, 16), (1, 2))),
        "lengths": draw_lengths(jax.random.fold_in(streams_of[10], 71), 0),
        "threshold": jax.random.randint(streams_of[3], (1,), 0, 1024).astype(jnp.int32),
        "attn_gain": jnp.clip(1.0 + 0.15 * jax.random.normal(streams_of[4], (D,), jnp.float32), 0.25, 1.75),
        "qkv_weight": gaussian(streams_of[5], (D, 3 * D), D ** -0.5, 0.21875),
        "out_weight": gaussian(streams_of[6], (D, D), (D // 24) ** -0.5, 1.0),
        "mlp_gain": jnp.clip(1.0 + 0.15 * jax.random.normal(streams_of[7], (D,), jnp.float32), 0.25, 1.75),
        "up_weight": gaussian(streams_of[8], (D, FF), D ** -0.5, 0.21875),
        "down_weight": gaussian(streams_of[9], (FF, D), FF ** -0.5, 0.109375),
    }


LN_EPS = 1e-05
GELU_C = 0.7978845608028654
PRECISE = lax.Precision.HIGHEST

@jax.custom_vjp
def low(v):
    return lax.optimization_barrier(v.astype(jnp.bfloat16)).astype(jnp.float32)

@jax.custom_vjp
def low_back(v):
    return v

def low_keep(v):
    return (low(v), None)

def low_pass(kept, grad):
    return (grad,)

def back_keep(v):
    return (v, None)

def back_low(kept, grad):
    return (low(grad),)
low.defvjp(low_keep, low_pass)
low_back.defvjp(back_keep, back_low)

def matmul_hi(left, right):
    return jnp.dot(left, right, precision=PRECISE)

def layer_norm(values, gain):
    centre = lax.optimization_barrier(jnp.mean(values, axis=-1, keepdims=True))
    shifted = values - centre
    spread = lax.optimization_barrier(jnp.mean(shifted * shifted, axis=-1, keepdims=True))
    return shifted * lax.rsqrt(spread + LN_EPS) * gain

def gelu_tanh(values):
    return 0.5 * values * (1.0 + jnp.tanh(GELU_C * (values + 0.044715 * values * values * values)))

def seg_info(length_row, positions):
    seg_ends = jnp.cumsum(length_row)
    segment = lax.optimization_barrier(jnp.sum((positions[:, None] >= seg_ends[None, :]).astype(jnp.int32), axis=1))
    slot_ids = jnp.arange(length_row.shape[0], dtype=jnp.int32)
    seg_len = lax.optimization_barrier(jnp.sum(jnp.where(segment[:, None] == slot_ids[None, :], length_row[None, :], 0), axis=1))
    return (segment, 4.0 / seg_len.astype(jnp.float32))

def head_from_scores(scores, values, penalty, allowed):
    numerators = jnp.where(allowed, jnp.exp(scores - penalty), 0.0)
    totals = lax.optimization_barrier(jnp.sum(numerators, axis=1, keepdims=True))
    return matmul_hi(low(numerators), values) / totals

def head_direct(queries, key_rows, values, penalty, allowed):
    scores = low_back(matmul_hi(queries, key_rows.T) * HEAD_DIM ** (-0.5))
    return head_from_scores(scores, values, penalty, allowed)

def pack_forward(tokens, attn_gain, qkv_weight, out_weight, mlp_gain, up_weight, down_weight, segment, rate, limit):
    width = tokens.shape[1]
    positions = jnp.arange(tokens.shape[0], dtype=jnp.int32)
    normed = low(layer_norm(tokens, attn_gain))
    qkv = low(low_back(matmul_hi(normed, qkv_weight)))
    same_seg = segment[:, None] == segment[None, :]
    allowed = same_seg & (positions[None, :] <= positions[:, None])
    strict = same_seg & (positions[None, :] < positions[:, None])
    first_scores = low_back(matmul_hi(qkv[:, 0:HEAD_DIM], qkv[:, width:width + HEAD_DIM].T) * HEAD_DIM ** (-0.5))
    chosen = jnp.where(strict, jnp.maximum(first_scores, 0.0), 0.0)
    penalty = rate[:, None] * (jnp.cumsum(chosen, axis=0) - chosen)
    outputs = [jax.checkpoint(head_from_scores)(first_scores, qkv[:, 2 * width:2 * width + HEAD_DIM], penalty, allowed)]
    for head in range(1, HEADS):
        lo_col = head * HEAD_DIM
        outputs.append(jax.checkpoint(head_direct)(qkv[:, lo_col:lo_col + HEAD_DIM], qkv[:, width + lo_col:width + lo_col + HEAD_DIM], qkv[:, 2 * width + lo_col:2 * width + lo_col + HEAD_DIM], penalty, allowed))
    attended = jnp.concatenate(outputs, axis=1)
    branch = low_back(matmul_hi(low(low_back(attended)), out_weight))
    residual = tokens + branch
    pre = low_back(matmul_hi(low(layer_norm(residual, mlp_gain)), up_weight))
    hidden = low(gelu_tanh(pre))
    result = residual + low_back(matmul_hi(hidden, down_weight))
    column_sums = lax.optimization_barrier(jnp.sum(chosen, axis=0))
    excess_part = jnp.sum(jnp.maximum(rate * column_sums - limit, 0.0))
    return (result, excess_part)

def reference(tokens, cotangent, lengths, threshold, attn_gain, qkv_weight, out_weight, mlp_gain, up_weight, down_weight):
    params = (attn_gain.astype(jnp.float32), qkv_weight.astype(jnp.float32), out_weight.astype(jnp.float32), mlp_gain.astype(jnp.float32), up_weight.astype(jnp.float32), down_weight.astype(jnp.float32))
    limit = threshold[0].astype(jnp.float32) / 1024.0
    positions = jnp.arange(tokens.shape[1], dtype=jnp.int32)

    def per_pack(totals, pack_in):
        pack_tokens, pack_cot, length_row = pack_in
        segment, rate = seg_info(length_row, positions)

        def forward(token_vals, *weights):
            return pack_forward(token_vals, *weights, segment, rate, limit)
        result, pullback, excess_part = jax.vjp(forward, pack_tokens.astype(jnp.float32), *params, has_aux=True)
        grads = pullback(pack_cot.astype(jnp.float32))
        summed = tuple((old + new for old, new in zip(totals[0], grads[1:])))
        return ((summed, totals[1] + excess_part), (result.astype(jnp.bfloat16), grads[0].astype(jnp.bfloat16)))
    init = (tuple((jnp.zeros_like(p) for p in params)), jnp.zeros((), jnp.float32))
    (grads, excess_sum), (outputs, input_grads) = lax.scan(per_pack, init, (tokens, cotangent, lengths))
    excess = (excess_sum / (tokens.shape[0] * tokens.shape[1])).reshape(1)
    return (outputs, input_grads, grads[0], grads[1], grads[2], grads[3], grads[4], grads[5], excess)
```

```python
import functools

import jax
import jax.numpy as jnp
from jax import lax
from jax.experimental import pallas as pl
from jax.experimental.pallas import tpu as pltpu
from jax.sharding import PartitionSpec as P

HEADS = 12
HEAD_DIM = 64
PAIRS = HEADS // 2
PAIR = 2 * HEAD_DIM

LN_EPS = 1e-05
GELU_C = 0.7978845608028654
LOG2E = 1.4426950408889634
FAR = 1e30
VMEM_LIMIT = 56 * 2**20

BF16 = jnp.bfloat16
F32 = jnp.float32
NN = (((1,), (0,)), ((), ()))
NT = (((1,), (1,)), ((), ()))
TN = (((0,), (0,)), ((), ()))


def mm(left, right, dims):
    return lax.dot_general(left, right, dims, preferred_element_type=F32)


def pick_tile(block_len):
    return 256 if block_len % 256 == 0 else block_len


def layer_norm(values, gain):
    centre = jnp.mean(values, axis=-1, keepdims=True)
    shifted = values - centre
    spread = jnp.mean(shifted * shifted, axis=-1, keepdims=True)
    return shifted * lax.rsqrt(spread + LN_EPS) * gain


def gelu_tanh(values):
    return 0.5 * values * (1.0 + jnp.tanh(GELU_C * (values + 0.044715 * values * values * values)))


def split2(values):
    high = values.astype(BF16)
    return high, (values - high.astype(F32)).astype(BF16)


def half_masks(rows):
    lane = lax.broadcasted_iota(jnp.int32, (rows, PAIR), 1)
    return (lane < HEAD_DIM, lane >= HEAD_DIM)


def tile_marks(tile, row_tile, key_tile, start):
    rows = row_tile * tile + lax.broadcasted_iota(jnp.int32, (tile, tile), 0)
    keys = key_tile * tile + lax.broadcasted_iota(jnp.int32, (tile, tile), 1)
    inside = keys >= start
    return inside & (keys < rows), inside & (keys <= rows)


def head0_scores(q_pair, k_pair, tile):
    first, _ = half_masks(tile)
    return mm(jnp.where(first, q_pair, 0), k_pair, NT) * HEAD_DIM**-0.5


def before_sum(chosen, tile):
    rows = lax.broadcasted_iota(jnp.int32, (tile, tile), 0)
    cols = lax.broadcasted_iota(jnp.int32, (tile, tile), 1)
    lower = (cols < rows).astype(F32).astype(BF16)
    high, low = split2(chosen)
    above = mm(lower, high, NN) + mm(lower, low, NN)
    return above, above[tile - 1 :, :] + chosen[tile - 1 :, :]


def after_sum(values, tile):
    rows = lax.broadcasted_iota(jnp.int32, (tile, tile), 0)
    cols = lax.broadcasted_iota(jnp.int32, (tile, tile), 1)
    upper = (cols > rows).astype(F32).astype(BF16)
    high, low = split2(values)
    below = mm(upper, high, NN) + mm(upper, low, NN)
    return below, below[:1, :] + values[:1, :]


def forward_kernel(
    tile, tiles,
    slot_ref, low_ref, q_ref, q0_ref, k_ref, v_ref, start_ref, rate_ref,
    att_ref, den_ref, kept_ref, sums_ref,
    acc, pen,
):
    halves = half_masks(tile)
    sums_ref[...] = jnp.zeros_like(sums_ref)

    def row_step(i, carry):
        slot = slot_ref[i]
        start = start_ref[i]
        rate = rate_ref[i]

        @pl.when(slot < 0)
        def _():
            def key_step(j, c):
                strict, _ = tile_marks(tile, i, j, start)
                scores = head0_scores(q0_ref[i], k_ref[j, :, :PAIR], tile)
                chosen = jnp.where(strict, jnp.maximum(scores, 0.0), 0.0)
                sums_ref[j] += jnp.sum(chosen, axis=0, keepdims=True)
                return c

            lax.fori_loop(low_ref[i], i + 1, key_step, 0)

        @pl.when(slot >= 0)
        def _():
            acc[...] = jnp.zeros_like(acc)

            def key_step(j, c):
                kept = sums_ref[j]
                kept_ref[slot, j] = kept
                strict, allowed = tile_marks(tile, i, j, start)
                scores = head0_scores(q0_ref[i], k_ref[j, :, :PAIR], tile)
                chosen = jnp.where(strict, jnp.maximum(scores, 0.0), 0.0)
                above, total = before_sum(chosen, tile)
                pen[...] = jnp.where(allowed, (rate * LOG2E) * (kept + above), FAR)
                sums_ref[j] = kept + total
                for pair in range(PAIRS):
                    at = slice(pair * PAIR, (pair + 1) * PAIR)
                    for half in range(2):
                        q_one = jnp.where(halves[half], q_ref[slot, :, at], 0)
                        logits = mm(q_one, k_ref[j, :, at], NT) * (HEAD_DIM**-0.5 * LOG2E) - pen[...]
                        numer = jnp.exp2(logits).astype(BF16)
                        v_one = jnp.where(halves[half], v_ref[j, :, at], 1)
                        acc[2 * pair + half] += mm(numer, v_one, NN)
                return c

            lax.fori_loop(low_ref[i], i + 1, key_step, 0)
            for pair in range(PAIRS):
                at = slice(pair * PAIR, (pair + 1) * PAIR)
                low, high = acc[2 * pair], acc[2 * pair + 1]
                numer = jnp.where(halves[0], low, high)
                denom = pltpu.roll(jnp.where(halves[0], high, low), HEAD_DIM, 1)
                att_ref[slot, :, at] = numer / denom
                den_ref[slot, :, at] = denom

        return carry

    lax.fori_loop(0, tiles, row_step, 0)


def backward_kernel(
    tile, owned,
    own_ref, low_ref, q_ref, k_ref, v_ref, dx_ref, start_ref, rate_ref, kept_ref,
    dq_ref, dk_ref, dv_ref, later_ref,
    acc_q, acc_k, acc_v, pen, dpen, later,
):
    halves = half_masks(tile)
    acc_k[...] = jnp.zeros_like(acc_k)
    acc_v[...] = jnp.zeros_like(acc_v)
    later[...] = jnp.zeros_like(later)
    later_ref[...] = jnp.zeros_like(later_ref)

    def row_step(step, carry):
        slot = owned - 1 - step
        i = own_ref[slot]
        start = start_ref[i]
        rate = rate_ref[i]
        acc_q[...] = jnp.zeros_like(acc_q)

        def key_step(j, c):
            strict, allowed = tile_marks(tile, i, j, start)
            scores0 = head0_scores(q_ref[slot, :, :PAIR], k_ref[j, :, :PAIR], tile)
            chosen = jnp.where(strict, jnp.maximum(scores0, 0.0), 0.0)
            above, _ = before_sum(chosen, tile)
            pen[...] = jnp.where(allowed, (rate * LOG2E) * (kept_ref[slot, j] + above), FAR)
            dpen[...] = jnp.zeros_like(dpen)
            for head in range(HEADS - 1, -1, -1):
                pair, half = divmod(head, 2)
                at = slice(pair * PAIR, (pair + 1) * PAIR)
                rows_at = slice(half * HEAD_DIM, (half + 1) * HEAD_DIM)
                head_at = slice(head * HEAD_DIM, (head + 1) * HEAD_DIM)
                k_one = k_ref[j, :, at]
                q_pair = q_ref[slot, :, at]
                if head == 0:
                    logits = scores0 * LOG2E - pen[...]
                else:
                    q_one = jnp.where(halves[half], q_pair, 0)
                    logits = mm(q_one, k_one, NT) * (HEAD_DIM**-0.5 * LOG2E) - pen[...]
                numer = jnp.exp2(logits)
                dx = dx_ref[slot, :, head * PAIR : (head + 1) * PAIR]
                v_one = jnp.where(halves[half], v_ref[j, :, at], 1)
                d_logit = numer * mm(dx, v_one, NT)
                total_pen = dpen[...] + d_logit
                if head == 0:
                    below, total = after_sum(total_pen, tile)
                    picked = strict & (scores0 > 0.0)
                    d_logit = d_logit + jnp.where(picked, -rate * (later[j] + below), 0.0)
                    later[j] = later[j] + total
                    later_ref[slot, j] = total
                else:
                    dpen[...] = total_pen
                d_low = d_logit.astype(BF16)
                acc_v[j, head_at, :] += mm(dx, numer.astype(BF16), TN)[rows_at]
                acc_k[j, head_at, :] += mm(q_pair, d_low, TN)[rows_at]
                acc_q[:, at] += mm(d_low, jnp.where(halves[half], k_one, 0), NN)
            return c

        lax.fori_loop(low_ref[i], i + 1, key_step, 0)
        dq_ref[slot] = (acc_q[...] * HEAD_DIM**-0.5).astype(BF16)
        return carry

    lax.fori_loop(0, owned, row_step, 0)

    def finish(j, c):
        dk_ref[j] = (acc_k[j] * HEAD_DIM**-0.5).astype(BF16)
        dv_ref[j] = acc_v[j].astype(BF16)
        return c

    lax.fori_loop(0, dk_ref.shape[0], finish, 0)


def late_kernel(tile, owned, own_ref, low_ref, q_ref, k_ref, start_ref, rate_ref, later_ref, dq_ref, dk_ref):
    first, _ = half_masks(tile)
    dk_ref[...] = jnp.zeros_like(dk_ref)
    dq_ref[...] = jnp.zeros_like(dq_ref)

    def row_step(slot, carry):
        i = own_ref[slot]
        start = start_ref[i]
        rate = rate_ref[i]

        def key_step(j, c):
            strict, _ = tile_marks(tile, i, j, start)
            scores = head0_scores(q_ref[slot], k_ref[j], tile)
            d_low = jnp.where(strict & (scores > 0.0), -rate * later_ref[slot, j], 0.0).astype(BF16)
            dk_ref[j] += mm(q_ref[slot], d_low, TN)[:HEAD_DIM] * HEAD_DIM**-0.5
            dq_ref[slot] += mm(d_low, jnp.where(first, k_ref[j], 0), NN) * HEAD_DIM**-0.5
            return c

        lax.fori_loop(low_ref[i], i + 1, key_step, 0)
        return carry

    lax.fori_loop(0, owned, row_step, 0)


def call(kernel, outs, scratch, scalars, operands, cost):
    smem = pl.BlockSpec(memory_space=pltpu.SMEM)
    vmem = pl.BlockSpec(memory_space=pltpu.VMEM)
    return pl.pallas_call(
        kernel,
        out_shape=tuple(jax.ShapeDtypeStruct(shape, dtype) for shape, dtype in outs),
        in_specs=[smem] * len(scalars) + [vmem] * len(operands),
        out_specs=tuple(vmem for _ in outs),
        scratch_shapes=[pltpu.VMEM(shape, dtype) for shape, dtype in scratch],
        compiler_params=pltpu.CompilerParams(vmem_limit_bytes=VMEM_LIMIT),
        cost_estimate=pl.CostEstimate(flops=cost, bytes_accessed=cost // 600, transcendentals=0),
    )(*scalars, *operands)


def on_device(
    tokens, cotangent, lengths, threshold, attn_gain, qkv_weight, out_weight, mlp_gain, up_weight, down_weight
):
    _, block_len, width = tokens.shape
    blocks = lax.axis_size("seq")
    dp_count = lax.axis_size("dp")
    me = lax.axis_index("seq")
    tile = pick_tile(block_len)
    owned = block_len // tile
    tiles = owned * blocks
    rows = blocks * block_len
    hid = up_weight.shape[1]

    ends = jnp.cumsum(lengths[0])
    positions = jnp.arange(rows, dtype=jnp.int32)
    passed = positions[:, None] >= ends[None, :]
    segment = jnp.sum(passed.astype(jnp.int32), axis=1)
    start = jnp.max(jnp.where(passed, ends[None, :], 0), axis=1)
    slots = jnp.arange(lengths.shape[1], dtype=jnp.int32)
    seg_len = jnp.sum(jnp.where(segment[:, None] == slots[None, :], lengths[0][None, :], 0), axis=1)
    rate = 4.0 / seg_len.astype(F32)
    tile_ids = jnp.arange(tiles, dtype=jnp.int32)
    low = start[::tile] // tile
    slot_of = jnp.where(tile_ids // owned == me, tile_ids % owned, -1).astype(jnp.int32)
    own_ids = (me * owned + jnp.arange(owned)).astype(jnp.int32)
    start3 = start.reshape(tiles, tile, 1)
    rate3 = rate.reshape(tiles, tile, 1)

    token_own = tokens[0]
    if blocks == 2:
        other = lax.ppermute(token_own, "seq", [(0, 1), (1, 0)])
        both = jnp.stack([token_own, other])
        pack = jnp.where(me == 0, both, both[::-1]).reshape(rows, width)
    else:
        pack = lax.all_gather(token_own, "seq", axis=0, tiled=True)
    token_vals = token_own.astype(F32)
    normed_low = layer_norm(pack.astype(F32), attn_gain).astype(BF16)
    normed_own = layer_norm(token_vals, attn_gain).astype(BF16)
    q_own = mm(normed_own, qkv_weight[:, :width], NN).astype(BF16).reshape(owned, tile, width)
    q_first = mm(normed_low, qkv_weight[:, :PAIR], NN).astype(BF16).reshape(tiles, tile, PAIR)
    k_all = mm(normed_low, qkv_weight[:, width : 2 * width], NN).astype(BF16).reshape(tiles, tile, width)
    v_all = mm(normed_low, qkv_weight[:, 2 * width :], NN).astype(BF16).reshape(tiles, tile, width)

    pairs_cost = rows * block_len * HEADS * HEAD_DIM
    attended4, denom4, kept, sums = call(
        functools.partial(forward_kernel, tile, tiles),
        [
            ((owned, tile, width), F32),
            ((owned, tile, width), F32),
            ((owned, tiles, 1, tile), F32),
            ((tiles, 1, tile), F32),
        ],
        [((HEADS, tile, PAIR), F32), ((tile, tile), F32)],
        [slot_of, low.astype(jnp.int32)],
        [q_own, q_first, k_all, v_all, start3, rate3],
        4 * pairs_cost,
    )
    limit = threshold[0].astype(F32) / 1024.0
    own_sums = lax.dynamic_slice_in_dim(sums.reshape(rows), me * block_len, block_len)
    own_rate = lax.dynamic_slice_in_dim(rate, me * block_len, block_len)
    excess_part = jnp.sum(jnp.maximum(own_rate * own_sums - limit, 0.0))
    attended = attended4.reshape(block_len, width)
    denom = denom4.reshape(block_len, width)

    cot = cotangent[0]
    attended_low = attended.astype(BF16)
    residual = token_vals + mm(attended_low, out_weight, NN)
    normed_mlp = layer_norm(residual, mlp_gain).astype(BF16)
    pre = mm(normed_mlp, up_weight, NN)
    hidden = gelu_tanh(pre).astype(BF16)
    output = (residual + mm(hidden, down_weight, NN)).astype(BF16)
    down_grad = mm(hidden, cot, TN).astype(BF16)
    d_hidden = mm(cot, down_weight, NT)
    _, gelu_pull = jax.vjp(gelu_tanh, pre)
    d_pre = gelu_pull(d_hidden)[0].astype(BF16)
    up_grad = mm(normed_mlp, d_pre, TN).astype(BF16)
    d_normed_mlp = mm(d_pre, up_weight, NT)
    _, mlp_pull = jax.vjp(layer_norm, residual, mlp_gain)
    d_res_norm, mlp_gain_grad = mlp_pull(d_normed_mlp)
    d_residual = cot.astype(F32) + d_res_norm
    d_branch = d_residual.astype(BF16)
    out_grad = mm(attended_low, d_branch, TN).astype(BF16)
    d_attended = mm(d_branch, out_weight, NT).astype(BF16)

    def scatter(grad):
        return lax.psum_scatter(grad, "dp", scatter_dimension=0, tiled=True)

    early = [scatter(g) for g in (down_grad, up_grad, out_grad)]

    by_head = (block_len, HEADS, HEAD_DIM)
    scaled = (d_attended.astype(F32) / denom).astype(BF16)
    row_dot = jnp.sum((scaled.astype(F32) * attended).reshape(by_head), axis=2, keepdims=True)
    dot_high, dot_low = split2(-row_dot)
    side = jnp.concatenate(
        [dot_high, dot_low, jnp.zeros((block_len, HEADS, HEAD_DIM - 2), BF16)], axis=2
    )
    scaled3 = scaled.reshape(by_head)
    even = (jnp.arange(HEADS) % 2 == 0)[None, :, None]
    dx = jnp.concatenate([jnp.where(even, scaled3, side), jnp.where(even, side, scaled3)], axis=2)
    dx = dx.reshape(owned, tile, HEADS * PAIR)
    dq, dk, dv, totals = call(
        functools.partial(backward_kernel, tile, owned),
        [
            ((owned, tile, width), BF16),
            ((tiles, width, tile), BF16),
            ((tiles, width, tile), BF16),
            ((owned, tiles, 1, tile), F32),
        ],
        [
            ((tile, width), F32),
            ((tiles, width, tile), F32),
            ((tiles, width, tile), F32),
            ((tile, tile), F32),
            ((tile, tile), F32),
            ((tiles, 1, tile), F32),
        ],
        [own_ids, low.astype(jnp.int32)],
        [q_own, k_all, v_all, dx, start3, rate3, kept],
        10 * pairs_cost,
    )
    all_totals = lax.all_gather(jnp.sum(totals, axis=0), "seq", axis=0)
    from_later = jnp.sum(
        jnp.where((jnp.arange(blocks) > me)[:, None, None, None], all_totals, 0.0), axis=0
    )
    late_q, late_k = call(
        functools.partial(late_kernel, tile, owned),
        [((owned, tile, PAIR), F32), ((tiles, HEAD_DIM, tile), F32)],
        [],
        [own_ids, low.astype(jnp.int32)],
        [
            q_own[:, :, :PAIR],
            k_all[:, :, :PAIR],
            start3,
            rate3,
            jnp.broadcast_to(from_later, (owned,) + from_later.shape),
        ],
        pairs_cost,
    )
    dq = jnp.concatenate(
        [(dq[:, :, :PAIR].astype(F32) + late_q).astype(BF16), dq[:, :, PAIR:]], axis=2
    ).reshape(block_len, width)
    dk = jnp.concatenate(
        [(dk[:, :HEAD_DIM].astype(F32) + late_k).astype(BF16), dk[:, HEAD_DIM:]], axis=1
    )
    dkv = jnp.concatenate([dk, dv], axis=1)
    d_normed = lax.dot_general(
        dkv, qkv_weight[:, width:], (((1,), (1,)), ((), ())), preferred_element_type=F32
    ).reshape(rows, width)
    kv_grad = jnp.einsum(
        "rtd,rct->dc", normed_low.reshape(tiles, tile, width), dkv, preferred_element_type=F32
    )
    q_grad = mm(normed_own, dq, TN)
    late = scatter(jnp.concatenate([q_grad, kv_grad], axis=1).astype(BF16))
    d_own = mm(dq, qkv_weight[:, :width], NT)
    d_blocks = d_normed.reshape(blocks, block_len, width)
    if blocks == 2:
        away = lax.dynamic_index_in_dim(d_blocks, 1 - me, 0, keepdims=False).astype(BF16)
        back = lax.ppermute(away, "seq", [(0, 1), (1, 0)]).astype(F32)
        d_own += lax.dynamic_index_in_dim(d_blocks, me, 0, keepdims=False) + back
    else:
        d_own += lax.psum_scatter(
            d_blocks.astype(BF16), "seq", scatter_dimension=0, tiled=False
        ).astype(F32)
    _, attn_pull = jax.vjp(layer_norm, token_vals, attn_gain)
    d_tok_norm, attn_gain_grad = attn_pull(d_own)
    input_grad = (d_residual + d_tok_norm).astype(BF16)

    def over_seq(piece):
        if blocks == 2:
            return piece.astype(F32) + lax.ppermute(piece, "seq", [(0, 1), (1, 0)]).astype(F32)
        return lax.psum(piece, "seq").astype(F32)

    down_piece, up_piece, out_piece = [over_seq(piece) for piece in early]
    qkv_piece = over_seq(late)
    gains = jnp.concatenate([attn_gain_grad, mlp_gain_grad, excess_part.reshape(1)])
    gains = lax.psum(gains, ("seq", "dp"))
    part = width // dp_count
    at = lax.axis_index("dp") * part
    attn_piece = lax.dynamic_slice_in_dim(gains, at, part)
    mlp_piece = lax.dynamic_slice_in_dim(gains, width + at, part)
    excess = (gains[2 * width :] / (dp_count * rows)).reshape(1)
    return (
        output[None],
        input_grad[None],
        attn_piece,
        qkv_piece,
        out_piece,
        mlp_piece,
        up_piece,
        down_piece,
        excess,
    )


def solution(mesh):
    return jax.shard_map(
        on_device,
        mesh=mesh,
        in_specs=(
            P("dp", "seq", None),
            P("dp", "seq", None),
            P("dp", None),
            P(),
            P(),
            P(),
            P(),
            P(),
            P(),
            P(),
        ),
        out_specs=(
            P("dp", "seq", None),
            P("dp", "seq", None),
            P("dp"),
            P("dp", None),
            P("dp", None),
            P("dp"),
            P("dp", None),
            P("dp", None),
            P(),
        ),
        check_vma=False,
    )
```

```python
import functools
import itertools

import jax
import jax.numpy as jnp
import numpy as np
from jax import lax
from jax.experimental import pallas as pl
from jax.experimental.pallas import tpu as pltpu
from jax.sharding import PartitionSpec as P

HEADS = 12
HEAD_DIM = 64
PAIRS = HEADS // 2
PAIR = 2 * HEAD_DIM

LONG = 2048
SHORT = 512

LN_EPS = 1e-05
GELU_C = 0.7978845608028654
LOG2E = 1.4426950408889634
FAR = 1e30
VMEM_LIMIT = 60 * 2**20

BF16 = jnp.bfloat16
F32 = jnp.float32
NN = (((1,), (0,)), ((), ()))
NT = (((1,), (1,)), ((), ()))
TN = (((0,), (0,)), ((), ()))


def mm(left, right, dims):
    return lax.dot_general(left, right, dims, preferred_element_type=F32)


def pick_tile(block_len):
    return 256 if block_len % 256 == 0 else block_len


def layer_norm(values, gain):
    centre = jnp.mean(values, axis=-1, keepdims=True)
    shifted = values - centre
    spread = jnp.mean(shifted * shifted, axis=-1, keepdims=True)
    return shifted * lax.rsqrt(spread + LN_EPS) * gain


def gelu_tanh(values):
    return 0.5 * values * (1.0 + jnp.tanh(GELU_C * (values + 0.044715 * values * values * values)))


def split2(values):
    high = values.astype(BF16)
    return high, (values - high.astype(F32)).astype(BF16)


def half_masks(rows):
    lane = lax.broadcasted_iota(jnp.int32, (rows, PAIR), 1)
    return (lane < HEAD_DIM, lane >= HEAD_DIM)


class Layout:
    def __init__(self, rows, slots, tile, owned, blocks):
        self.tile, self.owned, self.blocks, self.tiles = tile, owned, blocks, owned * blocks
        self.aligned = SHORT % tile == 0
        self.count = 2 if blocks == 2 and owned >= 4 else 0
        ways = [[LONG, SHORT], [SHORT, LONG], [SHORT] * (rows // SHORT)]
        made = [self.plan(way + [0] * (slots - len(way)), me) for way in ways for me in range(blocks)]
        self.at, at, columns = {}, 0, []
        for name in made[0]:
            size = max(len(m[name]) for m in made)
            self.at[name] = (at, size)
            at += size
            columns.append([m[name] + m[name][-1:] * (size - len(m[name])) for m in made])
        self.table = np.array([sum((c[n] for c in columns), []) for n in range(len(made))], np.int32)

    def plan(self, lengths, me):
        tile, owned, blocks, tiles = self.tile, self.owned, self.blocks, self.tiles
        ends = [int(e) for e in np.cumsum(lengths)]
        low = [max([e for e in ends if e <= t * tile], default=0) // tile for t in range(tiles)]
        last = [min(e for e in ends if e > t * tile) for t in range(tiles)]
        length = [e - max([f for f in ends if f < e], default=0) for e in last]
        cost = [t - low[t] + 1 for t in range(tiles)]
        homes = [[b * owned + t for t in range(owned)] for b in range(blocks)]
        works = [list(h) for h in homes]
        given = [[0], [0]]
        if self.count:
            options = list(itertools.combinations(range(owned), self.count))

            def apart(choice):
                a, b = choice
                gain = sum(cost[owned + t] for t in b) - sum(cost[t] for t in a)
                return abs(sum(cost[:owned]) - sum(cost[owned:]) + 2 * gain), -sum(a), sum(b)

            given = list(min(itertools.product(options, options), key=apart))
            for side in range(2):
                for t, u in zip(given[side], given[1 - side]):
                    works[side][t] = (1 - side) * owned + u
        own = works[me]
        slot = [own.index(t) if t in own else -1 for t in range(tiles)]
        loc = [((t // owned - me) % blocks) * owned + t % owned for t in range(tiles)]
        far = works[1 - me] if blocks == 2 else [t if t not in own else -1 for t in range(tiles)]
        pairs = [(i, j) for i in range(tiles) for j in range(low[i], i + 1)]
        forward = [(i, j) for i, j in pairs if slot[i] >= 0]
        backward, flags = [], []
        for j in range(tiles):
            mine = [(i, j) for i in reversed(range(j, tiles)) if slot[i] >= 0 and low[i] <= j]
            marks = [1] * len(mine)
            if not mine:
                mine, marks = [(j, j)], [0]
            marks[0] += 2
            marks[-1] += 4
            backward += mine
            flags += marks
        late = [(i, j) for i, j in forward if any(f > i and low[f] <= j for f in far)]
        return {
            "ends": ends,
            "length": length,
            "loc": loc,
            "slot": slot,
            "own": own,
            "own_at": [loc[t] for t in own],
            "slot_loc": [slot[loc.index(t)] for t in range(tiles)],
            "far": far,
            "given": list(given[me]) if self.count else [0],
            "taken": list(given[1 - me]) if self.count else [0],
            "all_n": [len(pairs)],
            "all_i": [i for i, _ in pairs],
            "all_j": [j for _, j in pairs],
            "fwd_i": [i for i, _ in forward],
            "fwd_j": [j for _, j in forward],
            "fwd_f": [1 + 2 * (j == low[i]) for i, j in forward] + [0],
            "bwd_i": [i for i, _ in backward],
            "bwd_j": [j for _, j in backward],
            "bwd_f": flags + [0],
            "late_n": [len(late)],
            "late_i": [i for i, _ in late] + [0],
            "late_j": [j for _, j in late] + [0],
        }

    def chosen(self, lengths, me):
        way = jnp.where(lengths[0] == LONG, 0, jnp.where(lengths[1] == LONG, 1, 2))
        return lax.dynamic_index_in_dim(jnp.array(self.table), way * self.blocks + me, 0, keepdims=False)

    def get(self, numbers, name, index):
        return numbers[self.at[name][0] + index]

    def part(self, numbers, name):
        at, size = self.at[name]
        return numbers[at : at + size]

    def size(self, name):
        return self.at[name][1]


def tile_marks(layout, numbers, i, j):
    tile = layout.tile
    row = lax.broadcasted_iota(jnp.int32, (tile, tile), 0)
    key = lax.broadcasted_iota(jnp.int32, (tile, tile), 1)
    if layout.aligned:
        apart = key - row
        ahead = jnp.where(i == j, 0, tile)
        length = jnp.full((1, 1), layout.get(numbers, "length", i), jnp.int32)
        return apart < ahead, apart <= ahead, 4.0 / length.astype(F32)
    places = i * tile + lax.broadcasted_iota(jnp.int32, (tile, 1), 0)
    start = jnp.zeros((tile, 1), jnp.int32)
    end = jnp.full((tile, 1), 2**30, jnp.int32)
    for n in range(layout.size("ends")):
        edge = layout.get(numbers, "ends", n)
        start = jnp.maximum(start, jnp.where(places >= edge, edge, 0))
        end = jnp.minimum(end, jnp.where(places < edge, edge, 2**30))
    inside = j * tile + key >= start
    apart = (j - i) * tile + key - row
    return inside & (apart < 0), inside & (apart <= 0), 4.0 / (end - start).astype(F32)


def head0_scores(q_pair, k_pair, tile):
    first, _ = half_masks(tile)
    return mm(jnp.where(first, q_pair, 0), k_pair, NT) * HEAD_DIM**-0.5


def before_sum(chosen, tile):
    rows = lax.broadcasted_iota(jnp.int32, (tile, tile), 0)
    cols = lax.broadcasted_iota(jnp.int32, (tile, tile), 1)
    lower = (cols < rows).astype(F32).astype(BF16)
    high, low = split2(chosen)
    above = mm(lower, high, NN) + mm(lower, low, NN)
    return above, above[tile - 1 :, :] + chosen[tile - 1 :, :]


def after_sum(values, tile):
    rows = lax.broadcasted_iota(jnp.int32, (tile, tile), 0)
    cols = lax.broadcasted_iota(jnp.int32, (tile, tile), 1)
    upper = (cols > rows).astype(F32).astype(BF16)
    high, low = split2(values)
    below = mm(upper, high, NN) + mm(upper, low, NN)
    return below, below[:1, :] + values[:1, :]


def project_kernel(x_ref, w_ref, gain_ref, *refs):
    q_ref, k_ref, v_ref, normed_ref = refs[-4:]
    width = x_ref.shape[2]
    normed = layer_norm(x_ref[0].astype(F32), gain_ref[...]).astype(BF16)
    normed_ref[0] = normed
    for part, ref in enumerate((q_ref, k_ref, v_ref)):
        ref[0] = mm(normed, w_ref[:, part * width : (part + 1) * width], NN).astype(BF16)


UNROLL = 4


def sums_kernel(layout, numbers, q_ref, k_ref, kept_ref, sums_ref, column):
    tile = layout.tile
    last = layout.size("all_i") - 1

    def group_step(group, carry):
        for n in range(UNROLL):
            at = jnp.minimum(group * UNROLL + n, last)
            i, j = layout.get(numbers, "all_i", at), layout.get(numbers, "all_j", at)
            at_i, at_j = layout.get(numbers, "loc", i), layout.get(numbers, "loc", j)
            strict, _, _ = tile_marks(layout, numbers, i, j)
            scores = head0_scores(q_ref[at_i], k_ref[at_j], tile)
            chosen = jnp.where(strict, jnp.maximum(scores, 0.0), 0.0)
            column[group * UNROLL + n] = jnp.sum(chosen, axis=0, keepdims=True)
        return carry

    count = layout.get(numbers, "all_n", 0)
    lax.fori_loop(0, lax.div(count + (UNROLL - 1), jnp.int32(UNROLL)), group_step, 0)
    sums_ref[...] = jnp.zeros_like(sums_ref)

    def add_step(n, carry):
        i, j = layout.get(numbers, "all_i", n), layout.get(numbers, "all_j", n)
        kept_ref[i, j] = sums_ref[j]
        sums_ref[j] += column[n]
        return carry

    lax.fori_loop(0, count, add_step, 0)


def forward_kernel(layout, numbers, q_ref, k_ref, v_ref, kept_ref, att_ref, inv_ref, acc, pen):
    tile = layout.tile
    step = pl.program_id(0)
    i, j = layout.get(numbers, "fwd_i", step), layout.get(numbers, "fwd_j", step)
    flag = layout.get(numbers, "fwd_f", step)
    halves = half_masks(tile)

    @pl.when((flag & 2) != 0)
    def _():
        acc[...] = jnp.zeros_like(acc)

    @pl.when((flag & 1) != 0)
    def _():
        def logits_of(head):
            pair, half = divmod(head, 2)
            at = slice(pair * PAIR, (pair + 1) * PAIR)
            return mm(jnp.where(halves[half], q_ref[0, :, at], 0), k_ref[0, :, at], NT)

        def gather(head, numer):
            pair, half = divmod(head, 2)
            at = slice(pair * PAIR, (pair + 1) * PAIR)
            acc[head] += mm(numer, jnp.where(halves[half], v_ref[0, :, at], 1), NN)

        raw = {head: logits_of(head) for head in range(3)}
        strict, allowed, rate = tile_marks(layout, numbers, i, j)
        chosen = jnp.where(strict, jnp.maximum(raw[0] * HEAD_DIM**-0.5, 0.0), 0.0)
        above, _ = before_sum(chosen, tile)
        pen[...] = jnp.where(allowed, (rate * LOG2E) * (kept_ref[i, j] + above), FAR)
        waiting = {}
        for head in range(HEADS + 2):
            if 3 <= head + 3 < HEADS:
                raw[head + 3] = logits_of(head + 3)
            if head < HEADS:
                waiting[head] = jnp.exp2(raw.pop(head) * (HEAD_DIM**-0.5 * LOG2E) - pen[...]).astype(BF16)
            if head >= 2:
                gather(head - 2, waiting.pop(head - 2))

        @pl.when(i == j)
        def _():
            for pair in range(PAIRS):
                at = slice(pair * PAIR, (pair + 1) * PAIR)
                low, high = acc[2 * pair], acc[2 * pair + 1]
                numer = jnp.where(halves[0], low, high)
                inverse = 1.0 / pltpu.roll(jnp.where(halves[0], high, low), HEAD_DIM, 1)
                att_ref[0, :, at] = numer * inverse
                inv_ref[0, :, at] = inverse


def middle_kernel(
    tile, owned, chunk,
    att_ref, inv_ref, x_ref, cot_ref, wo_ref, wu_ref, wd_ref, gain_ref,
    out_ref, branch_ref, dx_ref, gain_grad_ref, grads_ref,
    hid_s, dpre_s, low_s, normed_s, branch_s, stage_down, stage_rest, sems,
):
    step = pl.program_id(0)
    width = x_ref.shape[2]
    hid = wu_ref.shape[1]
    parts = hid // width
    joined = len(stage_rest.shape) == 4

    def shipment(n):
        source = stage_down.at[n] if n < parts else stage_rest.at[n - parts]
        if not joined:
            target = grads_ref.at[n]
        elif n < parts:
            some, long = stage_down.shape[1:3]
            target = grads_ref.at[pl.ds(n * some, some), pl.ds(0, long), :]
        else:
            share = stage_rest.shape[2]
            target = grads_ref.at[:, pl.ds(share * n, share), :]
        return pltpu.make_async_copy(source, target, sems.at[n])

    def ship(n, block):
        stage, at = (stage_down, n) if n < parts else (stage_rest, n - parts)
        stage[at] = block.astype(BF16).reshape(stage.shape[1:])
        shipment(n).start()

    @pl.when(step == 0)
    def _():
        gain_grad_ref[...] = jnp.zeros_like(gain_grad_ref)

    @pl.when(step < owned)
    def _():
        at = pl.ds(pl.multiple_of(step * tile, tile), tile)
        attended = att_ref[0]
        cot = cot_ref[at, :]
        gain = gain_ref[...]
        low = attended.astype(BF16)
        low_s[at, :] = low
        residual = x_ref[0].astype(F32) + mm(low, wo_ref[...], NN)
        centre = jnp.mean(residual, axis=1, keepdims=True)
        shifted = residual - centre
        scale = lax.rsqrt(jnp.mean(shifted * shifted, axis=1, keepdims=True) + LN_EPS)
        xhat = shifted * scale
        normed = (xhat * gain).astype(BF16)
        normed_s[at, :] = normed
        result = residual
        d_normed = jnp.zeros((tile, width), F32)
        for c in range(hid // chunk):
            cols = slice(c * chunk, (c + 1) * chunk)
            pre = mm(normed, wu_ref[:, cols], NN)
            square = pre * pre
            wave = jnp.tanh(GELU_C * pre * (1.0 + 0.044715 * square))
            rising = 0.5 * (1.0 + wave)
            hidden = (pre * rising).astype(BF16)
            slope = rising + (0.5 * GELU_C) * pre * (1.0 - wave * wave) * (1.0 + (3 * 0.044715) * square)
            d_pre = (mm(cot, wd_ref[cols, :], NT) * slope).astype(BF16)
            hid_s[at, cols] = hidden
            dpre_s[at, cols] = d_pre
            result = result + mm(hidden, wd_ref[cols, :], NN)
            d_normed = d_normed + mm(d_pre, wu_ref[:, cols], NT)
        out_ref[0] = result.astype(BF16)
        gain_grad_ref[...] += jnp.sum(d_normed * xhat, axis=0, keepdims=True)
        grown = d_normed * gain
        mean_grown = jnp.mean(grown, axis=1, keepdims=True)
        mean_both = jnp.mean(grown * xhat, axis=1, keepdims=True)
        branch = (cot.astype(F32) + scale * (grown - mean_grown - xhat * mean_both)).astype(BF16)
        branch_ref[0] = branch
        branch_s[at, :] = branch
        d_attended = mm(branch, wo_ref[...], NT).astype(BF16).astype(F32)
        scaled = (d_attended * inv_ref[0]).astype(BF16)
        product = scaled.astype(F32) * attended
        rows = lax.broadcasted_iota(jnp.int32, (PAIR, 2 * PAIR), 0)
        cols = lax.broadcasted_iota(jnp.int32, (PAIR, 2 * PAIR), 1)
        block = cols // HEAD_DIM
        spread = jnp.where(block == jnp.where(rows < HEAD_DIM, 1, 2), -1.0, 0.0).astype(BF16)
        lane = lax.broadcasted_iota(jnp.int32, (tile, 2 * PAIR), 1) % HEAD_DIM
        first, _ = half_masks(tile)
        for pair in range(PAIRS):
            here = slice(pair * PAIR, (pair + 1) * PAIR)
            high, rest = split2(product[:, here])
            minus_dot = mm(high, spread, NN) + mm(rest, spread, NN)
            dot_high, dot_low = split2(minus_dot)
            side = jnp.where(lane == 0, dot_high, jnp.where(lane == 1, dot_low, 0))
            mine = scaled[:, here]
            base = 2 * pair * PAIR
            dx_ref[0, :, base : base + PAIR] = jnp.where(first, mine, side[:, :PAIR])
            dx_ref[0, :, base + PAIR : base + 2 * PAIR] = jnp.where(first, side[:, PAIR:], mine)

    for c in range(parts):
        @pl.when(step == owned + c)
        def _(c=c):
            cols = slice(c * width, (c + 1) * width)
            ship(c, mm(hid_s[:, cols], cot_ref[...], TN))
            ship(parts + c, mm(normed_s[...], dpre_s[:, cols], TN))
            if c == parts - 1:
                ship(2 * parts, mm(low_s[...], branch_s[...], TN))
                for n in range(2 * parts + 1):
                    shipment(n).wait()


def backward_kernel(
    layout, numbers, q_ref, k_ref, v_ref, dx_ref, kept_ref,
    dq_ref, dk_ref, dv_ref, later_ref,
    acc_q, acc_k, acc_v, pen, dpen, later,
):
    tile = layout.tile
    step = pl.program_id(0)
    i, j = layout.get(numbers, "bwd_i", step), layout.get(numbers, "bwd_j", step)
    flag = layout.get(numbers, "bwd_f", step)
    halves = half_masks(tile)

    @pl.when(step == 0)
    def _():
        acc_q[...] = jnp.zeros_like(acc_q)
        later_ref[...] = jnp.zeros_like(later_ref)

    @pl.when((flag & 2) != 0)
    def _():
        acc_k[...] = jnp.zeros_like(acc_k)
        acc_v[...] = jnp.zeros_like(acc_v)
        later[...] = jnp.zeros_like(later)

    @pl.when((flag & 1) != 0)
    def _():
        slot = layout.get(numbers, "slot", i)
        scores0 = head0_scores(q_ref[0, :, :PAIR], k_ref[0, :, :PAIR], tile)

        def products(pair):
            at = slice(pair * PAIR, (pair + 1) * PAIR)
            k_pair, q_pair, v_pair = k_ref[0, :, at], q_ref[0, :, at], v_ref[0, :, at]
            made = []
            for half in range(2):
                head = 2 * pair + half
                scores = scores0 if head == 0 else mm(jnp.where(halves[half], q_pair, 0), k_pair, NT) * HEAD_DIM**-0.5
                dx = dx_ref[0, :, head * PAIR : (head + 1) * PAIR]
                made.append((scores, mm(dx, jnp.where(halves[half], v_pair, 1), NT)))
            return made

        made = {PAIRS - 1: products(PAIRS - 1)}
        ready = {}
        strict, allowed, rate = tile_marks(layout, numbers, i, j)
        chosen = jnp.where(strict, jnp.maximum(scores0, 0.0), 0.0)
        above, _ = before_sum(chosen, tile)
        pen[...] = jnp.where(allowed, (rate * LOG2E) * (kept_ref[i, j] + above), FAR)

        def pointwise(pair, made):
            grads, weights = [], []
            for scores, d_probs in made:
                numer = jnp.exp2(scores * LOG2E - pen[...])
                weights.append(numer.astype(BF16))
                grads.append(numer * d_probs)
            both = grads[0] + grads[1]
            if pair == PAIRS - 1:
                dpen[...] = both
            elif pair > 0:
                dpen[...] += both
            else:
                below, total = after_sum(dpen[...] + both, tile)
                picked = strict & (scores0 > 0.0)
                grads[0] = grads[0] + jnp.where(picked, -rate * (later[...] + below), 0.0)
                later[...] = later[...] + total
                later_ref[slot, j] = total
            return weights, [g.astype(BF16) for g in grads]

        def collect(pair, weights, lows):
            at = slice(pair * PAIR, (pair + 1) * PAIR)
            k_pair, q_pair = k_ref[0, :, at], q_ref[0, :, at]
            d_q = None
            for half in range(2):
                head = 2 * pair + half
                part = slice(half * HEAD_DIM, (half + 1) * HEAD_DIM)
                head_at = slice(head * HEAD_DIM, (head + 1) * HEAD_DIM)
                dx = dx_ref[0, :, head * PAIR : (head + 1) * PAIR]
                acc_v[head_at, :] += mm(dx, weights[half], TN)[part]
                acc_k[head_at, :] += mm(q_pair, lows[half], TN)[part]
                more = mm(lows[half], jnp.where(halves[half], k_pair, 0), NN)
                d_q = more if d_q is None else d_q + more
            acc_q[slot, :, at] += d_q

        for pair in range(PAIRS - 1, -2, -1):
            if pair > 0:
                made[pair - 1] = products(pair - 1)
            if pair >= 0:
                ready[pair] = pointwise(pair, made.pop(pair))
            if pair + 1 in ready:
                collect(pair + 1, *ready.pop(pair + 1))

    @pl.when((flag & 4) != 0)
    def _():
        dk_ref[0] = jnp.transpose((acc_k[...] * HEAD_DIM**-0.5).astype(BF16))
        dv_ref[0] = jnp.transpose(acc_v[...].astype(BF16))

    @pl.when(step == pl.num_programs(0) - 1)
    def _():
        for slot in range(acc_q.shape[0]):
            dq_ref[slot] = (acc_q[slot] * HEAD_DIM**-0.5).astype(BF16)


def late_kernel(
    layout, numbers, q_ref, k_ref, far_totals_ref, dq_in_ref, dk_in_ref,
    dq_ref, dk_ref,
    acc_q, acc_k,
):
    tile = layout.tile
    first, _ = half_masks(tile)
    acc_q[...] = jnp.zeros_like(acc_q)
    acc_k[...] = jnp.zeros_like(acc_k)
    count = layout.get(numbers, "late_n", 0)

    def group_step(group, carry):
        adds = []
        for n in range(UNROLL):
            at = group * UNROLL + n
            valid = at < count
            at = jnp.minimum(at, layout.size("late_i") - 1)
            i, j = layout.get(numbers, "late_i", at), layout.get(numbers, "late_j", at)
            slot, at_i, at_j = (layout.get(numbers, name, t) for name, t in (("slot", i), ("loc", i), ("loc", j)))
            slot = jnp.maximum(slot, 0)
            later = jnp.zeros((1, tile), F32)
            for f in range(layout.size("far")):
                later += jnp.where(valid & (layout.get(numbers, "far", f) > i), far_totals_ref[f, j], 0.0)
            strict, _, rate = tile_marks(layout, numbers, i, j)
            scores = head0_scores(q_ref[at_i], k_ref[at_j], tile)
            factor = (-(HEAD_DIM**-0.5) * rate) * later
            d_low = jnp.where(strict & (scores > 0.0), factor, 0.0).astype(BF16)
            adds.append((slot, at_j, mm(q_ref[at_i], d_low, TN), mm(d_low, k_ref[at_j], NN)))
        for slot, at_j, for_k, for_q in adds:
            acc_k[at_j] += for_k
            acc_q[slot] += for_q
        return carry

    lax.fori_loop(0, lax.div(count + (UNROLL - 1), jnp.int32(UNROLL)), group_step, 0)
    for slot in range(acc_q.shape[0]):
        dq_ref[slot] = (dq_in_ref[slot].astype(F32) + jnp.where(first, acc_q[slot], 0.0)).astype(BF16)

    def finish(t, carry):
        dk_ref[t] = (dk_in_ref[t].astype(F32) + jnp.where(first, jnp.transpose(acc_k[t]), 0.0)).astype(BF16)
        return carry

    lax.fori_loop(0, acc_k.shape[0], finish, 0)


def unproject_kernel(layout, base, numbers, dq_ref, dk_ref, dv_ref, normed_ref, w_ref, gain_ref, out_ref, gain_grad_ref):
    step = pl.program_id(0)
    width = normed_ref.shape[2]
    slot = layout.get(numbers, "slot_loc", base + step)

    @pl.when(step == 0)
    def _():
        gain_grad_ref[...] = jnp.zeros_like(gain_grad_ref)

    d_query = jnp.where(slot >= 0, dq_ref[0], jnp.zeros_like(dq_ref[0]))
    d_normed = (
        mm(dv_ref[0], w_ref[:, 2 * width :], NT)
        + mm(dk_ref[0], w_ref[:, width : 2 * width], NT)
        + mm(d_query, w_ref[:, :width], NT)
    )
    out_ref[0] = d_normed.astype(out_ref.dtype)
    gain_grad_ref[...] += jnp.sum(d_normed * normed_ref[0].astype(F32), axis=0, keepdims=True) / gain_ref[...]


def flat(ref, cols):
    block = ref[:, :, cols]
    return block.reshape(block.shape[0] * block.shape[1], block.shape[2])


def value_weight_kernel(normed_ref, dk_ref, dv_ref, out_ref):
    width = normed_ref.shape[2]
    half = width // 2
    normed = flat(normed_ref, slice(None))
    out_ref[:, :half] = mm(normed, flat(dk_ref, slice(half, width)), TN).astype(BF16)
    out_ref[:, half:] = mm(normed, flat(dv_ref, slice(None)), TN).astype(BF16)


def query_weight_kernel(layout, numbers, normed_ref, dq_ref, dk_ref, out_ref):
    width = normed_ref.shape[2]
    half = width // 2
    total = jnp.zeros((width, width), F32)
    for slot in range(layout.owned):
        total += mm(normed_ref[layout.get(numbers, "own_at", slot)], dq_ref[slot], TN)
    out_ref[:, :width] = total.astype(BF16)
    out_ref[:, width:] = mm(flat(normed_ref, slice(None)), flat(dk_ref, slice(0, half)), TN).astype(BF16)


def input_kernel(part_ref, back_ref, x_ref, branch_ref, gain_ref, out_ref):
    values = x_ref[0].astype(F32)
    shifted = values - jnp.mean(values, axis=1, keepdims=True)
    scale = lax.rsqrt(jnp.mean(shifted * shifted, axis=1, keepdims=True) + LN_EPS)
    xhat = shifted * scale
    grown = (part_ref[0] + back_ref[0].astype(F32)) * gain_ref[...]
    mean_grown = jnp.mean(grown, axis=1, keepdims=True)
    mean_both = jnp.mean(grown * xhat, axis=1, keepdims=True)
    dx = scale * (grown - mean_grown - xhat * mean_both)
    out_ref[0] = (branch_ref[0].astype(F32) + dx).astype(BF16)


SMEM = pl.BlockSpec(memory_space=pltpu.SMEM)
VMEM = pl.BlockSpec(memory_space=pltpu.VMEM)


def estimate(flops):
    flops = int(flops)
    return pl.CostEstimate(flops=flops, bytes_accessed=flops // 600, transcendentals=0)


def held(shape):
    return pl.BlockSpec(shape, lambda *_: (0,) * len(shape), pipeline_mode=pl.Buffered(1))


def fixed(shape):
    return pl.BlockSpec(shape, lambda *_: (0,) * len(shape))


def sds(shape, dtype):
    return jax.ShapeDtypeStruct(shape, dtype)


def project(x, weight, gain, tiles, first, into):
    owned, tile, width = x.shape
    outs = (sds((tiles, tile, width), BF16),) * 4
    row = pl.BlockSpec((1, tile, width), lambda s: (s, 0, 0))
    placed = pl.BlockSpec((1, tile, width), lambda s: (s + first, 0, 0))
    extra = [pl.BlockSpec(memory_space=pl.ANY)] * len(into)
    return pl.pallas_call(
        project_kernel,
        grid=(owned,),
        out_shape=outs,
        in_specs=[row, held(weight.shape), held(gain.shape)] + extra,
        out_specs=(placed,) * 4,
        input_output_aliases={3 + n: n for n in range(len(into))},
        compiler_params=pltpu.CompilerParams(vmem_limit_bytes=20 * 2**20),
        cost_estimate=estimate(2 * owned * tile * width * weight.shape[1]),
    )(x, weight, gain, *into)


def middle(attended, inverse, x, cot, wo, wu, wd, gain, dp_count):
    owned, tile, width = x.shape
    hid = wu.shape[1]
    parts = hid // width
    rows = owned * tile
    row = pl.BlockSpec((1, tile, width), lambda s: (jnp.minimum(s, owned - 1), 0, 0))
    wide = pl.BlockSpec((1, tile, 2 * width), lambda s: (jnp.minimum(s, owned - 1), 0, 0))

    share = width // dp_count
    joined = share % 16 == 0 and dp_count % parts == 0
    if joined:
        stage_down = (parts, dp_count // parts, share * parts, width)
        stage_rest = (parts + 1, dp_count, share, width)
        grads = (dp_count, share * (2 * parts + 1), width)
    else:
        stage_down, stage_rest, grads = ((n, width, width) for n in (parts, parts + 1, 2 * parts + 1))
    return pl.pallas_call(
        functools.partial(middle_kernel, tile, owned, width),
        grid=(owned + parts,),
        out_shape=(
            sds((owned, tile, width), BF16),
            sds((owned, tile, width), BF16),
            sds((owned, tile, 2 * width), BF16),
            sds((1, width), F32),
            sds(grads, BF16),
        ),
        in_specs=[
            row, row, row, held((rows, width)), held(wo.shape), held(wu.shape), held(wd.shape), held(gain.shape),
        ],
        out_specs=(
            row, row, wide,
            pl.BlockSpec((1, width), lambda s: (0, 0)),
            pl.BlockSpec(memory_space=pl.ANY),
        ),
        scratch_shapes=[
            pltpu.VMEM((rows, hid), BF16),
            pltpu.VMEM((rows, hid), BF16),
            pltpu.VMEM((rows, width), BF16),
            pltpu.VMEM((rows, width), BF16),
            pltpu.VMEM((rows, width), BF16),
            pltpu.VMEM(stage_down, BF16),
            pltpu.VMEM(stage_rest, BF16),
            pltpu.SemaphoreType.DMA((2 * parts + 1,)),
        ],
        compiler_params=pltpu.CompilerParams(vmem_limit_bytes=VMEM_LIMIT),
        cost_estimate=estimate(2 * rows * width * (3 * width + 6 * hid)),
    )(attended, inverse, x, cot, wo, wu, wd, gain)


def kernel_call(kernel, room, grid, numbers, operands, in_specs, outs, out_specs, scratch, flops, aliases=None):
    return pl.pallas_call(
        kernel,
        grid_spec=pltpu.PrefetchScalarGridSpec(
            num_scalar_prefetch=1, grid=grid, in_specs=in_specs, out_specs=out_specs, scratch_shapes=scratch
        ),
        out_shape=outs,
        input_output_aliases=aliases or {},
        compiler_params=pltpu.CompilerParams(vmem_limit_bytes=room * 2**20),
        cost_estimate=estimate(flops),
    )(numbers, *operands)


def run_sums(layout, numbers, q, k):
    tiles, tile, _ = q.shape
    every = pl.BlockSpec((tiles, tile, PAIR), lambda n, x: (0, 0, 0))
    kept, sums = (tiles, tiles, 1, tile), (tiles, 1, tile)
    groups = -(-layout.size("all_i") // UNROLL) * UNROLL
    return kernel_call(
        functools.partial(sums_kernel, layout), 12, (1,), numbers, (q, k), [every, every],
        (sds(kept, F32), sds(sums, F32)), (fixed(kept), fixed(sums)),
        [pltpu.VMEM((groups, 1, tile), F32)], tiles * tiles * tile * tile * PAIR,
    )


def run_forward(layout, numbers, q, k, v, kept):
    tiles, tile, width = q.shape
    get, owned = layout.get, layout.owned
    rows = pl.BlockSpec((1, tile, width), lambda n, x: (get(x, "loc", get(x, "fwd_i", n)), 0, 0))
    keys = pl.BlockSpec((1, tile, width), lambda n, x: (get(x, "loc", get(x, "fwd_j", n)), 0, 0))
    slots = pl.BlockSpec((1, tile, width), lambda n, x: (get(x, "slot", get(x, "fwd_i", n)), 0, 0))
    return kernel_call(
        functools.partial(forward_kernel, layout), 20, (layout.size("fwd_i"),), numbers,
        (q, k, v, kept), [rows, keys, keys, fixed(kept.shape)],
        (sds((owned, tile, width), F32),) * 2, (slots, slots),
        [pltpu.VMEM((HEADS, tile, PAIR), F32), pltpu.VMEM((tile, tile), F32)],
        4 * layout.size("fwd_i") * tile * tile * width,
    )


def run_backward(layout, numbers, q, k, v, dx, kept):
    tiles, tile, width = q.shape
    get, owned = layout.get, layout.owned
    rows = pl.BlockSpec((1, tile, width), lambda n, x: (get(x, "loc", get(x, "bwd_i", n)), 0, 0))
    keys = pl.BlockSpec((1, tile, width), lambda n, x: (get(x, "loc", get(x, "bwd_j", n)), 0, 0))
    slots = pl.BlockSpec(
        (1, tile, 2 * width), lambda n, x: (jnp.maximum(get(x, "slot", get(x, "bwd_i", n)), 0), 0, 0)
    )
    totals = (owned, tiles, 1, tile)
    return kernel_call(
        functools.partial(backward_kernel, layout), 28, (layout.size("bwd_i"),), numbers,
        (q, k, v, dx, kept), [rows, keys, keys, slots, fixed(kept.shape)],
        (
            sds((owned, tile, width), BF16),
            sds((tiles, tile, width), BF16),
            sds((tiles, tile, width), BF16),
            sds(totals, F32),
        ),
        (fixed((owned, tile, width)), keys, keys, fixed(totals)),
        [
            pltpu.VMEM((owned, tile, width), F32),
            pltpu.VMEM((width, tile), F32),
            pltpu.VMEM((width, tile), F32),
            pltpu.VMEM((tile, tile), F32),
            pltpu.VMEM((tile, tile), F32),
            pltpu.VMEM((1, tile), F32),
        ],
        10 * layout.size("bwd_i") * tile * tile * width,
    )


def run_late(layout, numbers, q, k, far_totals, dq, dk):
    tiles, tile, _ = q.shape
    owned = dq.shape[0]
    some = pl.BlockSpec((owned, tile, PAIR), lambda n, x: (0, 0, 0))
    every = pl.BlockSpec((tiles, tile, PAIR), lambda n, x: (0, 0, 0))
    return kernel_call(
        functools.partial(late_kernel, layout), 16, (1,), numbers,
        (q, k, far_totals, dq, dk), [every, every, fixed(far_totals.shape), some, every],
        (sds(dq.shape, BF16), sds(dk.shape, BF16)), (some, every),
        [pltpu.VMEM((owned, tile, PAIR), F32), pltpu.VMEM((tiles, PAIR, tile), F32)],
        6 * layout.size("late_i") * tile * tile * PAIR,
        {4: 0, 5: 1},
    )


def unproject(layout, numbers, base, count, dq, dk, dv, normed, weight, gain, dtype):
    tile, width = layout.tile, dq.shape[2]
    row = pl.BlockSpec((1, tile, width), lambda s, x: (s, 0, 0))
    placed = pl.BlockSpec((1, tile, width), lambda s, x: (base + s, 0, 0))
    picked = pl.BlockSpec((1, tile, width), lambda s, x: (jnp.maximum(layout.get(x, "slot_loc", base + s), 0), 0, 0))
    return kernel_call(
        functools.partial(unproject_kernel, layout, base), 20, (count,), numbers,
        (dq, dk, dv, normed, weight, gain),
        [picked, placed, placed, placed, held(weight.shape), held(gain.shape)],
        (sds((count, tile, width), dtype), sds((1, width), F32)), (row, fixed((1, width))),
        [], 2 * count * tile * width * weight.shape[1],
    )


def value_weight_grad(normed, dk, dv):
    width = normed.shape[2]
    return pl.pallas_call(
        value_weight_kernel,
        out_shape=sds((width, 3 * width // 2), BF16),
        in_specs=[VMEM] * 3,
        out_specs=VMEM,
        compiler_params=pltpu.CompilerParams(vmem_limit_bytes=30 * 2**20),
        cost_estimate=estimate(3 * normed.shape[0] * normed.shape[1] * width * width),
    )(normed, dk, dv)


def query_weight_grad(layout, numbers, normed, dq, dk):
    width = normed.shape[2]
    return pl.pallas_call(
        functools.partial(query_weight_kernel, layout),
        out_shape=sds((width, 3 * width // 2), BF16),
        in_specs=[SMEM, VMEM, VMEM, VMEM],
        out_specs=VMEM,
        compiler_params=pltpu.CompilerParams(vmem_limit_bytes=28 * 2**20),
        cost_estimate=estimate(2 * normed.shape[0] * normed.shape[1] * width * width),
    )(numbers, normed, dq, dk)


def finish_input(part, back, x, branch, gain):
    owned, tile, width = x.shape
    row = pl.BlockSpec((1, tile, width), lambda s: (s, 0, 0))
    return pl.pallas_call(
        input_kernel,
        grid=(owned,),
        out_shape=sds(x.shape, BF16),
        in_specs=[row, row, row, row, held(gain.shape)],
        out_specs=row,
        compiler_params=pltpu.CompilerParams(vmem_limit_bytes=16 * 2**20),
        cost_estimate=estimate(2 * owned * tile * width * 600),
    )(part, back, x, branch, gain)


def swap_seq(array):
    return lax.ppermute(array, "seq", [(0, 1), (1, 0)])


def powers(size):
    return [1 << n for n in range(size.bit_length() - 1)]


def is_power(size):
    return size & (size - 1) == 0


def sum_everywhere(values):
    for axis in ("seq", "dp"):
        size = lax.axis_size(axis)
        if not is_power(size):
            values = lax.psum(values, axis)
            continue
        for bit in powers(size):
            values = values + lax.ppermute(values, axis, [(i, i ^ bit) for i in range(size)])
    return values


def scatter_halving(grad, order):
    count = lax.axis_size("dp")
    index = lax.axis_index("dp")
    bits = len(powers(count))
    held_bits = list(range(bits))[::-1]
    parts = grad.reshape((2,) * bits + grad.shape[1:])
    for n in order:
        axis = held_bits.index(n)
        held_bits.remove(n)
        mine = (index >> n) & 1
        keep = lax.dynamic_index_in_dim(parts, mine, axis, keepdims=False)
        send = lax.dynamic_index_in_dim(parts, 1 - mine, axis, keepdims=False)
        got = lax.ppermute(send, "dp", [(i, i ^ (1 << n)) for i in range(count)])
        parts = (keep.astype(F32) + got.astype(F32)).astype(BF16)
    return parts


def on_device(
    tokens, cotangent, lengths, threshold, attn_gain, qkv_weight, out_weight, mlp_gain, up_weight, down_weight
):
    _, block_len, width = tokens.shape
    blocks = lax.axis_size("seq")
    dp_count = lax.axis_size("dp")
    me = lax.axis_index("seq")
    tile = pick_tile(block_len)
    owned = block_len // tile
    tiles = owned * blocks
    rows = blocks * block_len
    hid = up_weight.shape[1]
    token_own = tokens[0]
    cot_own = cotangent[0]
    attn_gain = attn_gain.reshape(1, width)
    mlp_gain = mlp_gain.reshape(1, width)
    by_tile = (owned, tile, width)

    layout = Layout(rows, lengths.shape[1], tile, owned, blocks)
    count = layout.count
    numbers = layout.chosen(lengths[0], me)
    given, taken = layout.part(numbers, "given"), layout.part(numbers, "taken")

    def put(array, pieces):
        for n in range(count):
            array = lax.dynamic_update_slice_in_dim(array, pieces[n][None], given[n], 0)
        return array

    def swap_tiles(array):
        if count == 0:
            return array
        sent = jnp.stack([lax.dynamic_index_in_dim(array, given[n], 0, False) for n in range(count)])
        return put(array, swap_seq(sent))

    x_own = token_own.reshape(by_tile)
    if blocks == 2:
        x_others = swap_seq(token_own).reshape(by_tile)
    else:
        gathered = lax.all_gather(token_own, "seq", axis=0, tiled=False)
        x_others = jnp.roll(gathered, -me, axis=0)[1:].reshape(tiles - owned, tile, width)
    cot_tiles, x_others = lax.optimization_barrier((cot_own.reshape(by_tile), x_others))
    cot = swap_tiles(cot_tiles).reshape(block_len, width)
    parts = project(x_own, qkv_weight, attn_gain, tiles, 0, ())
    q_all, k_all, v_all, normed_all = project(x_others, qkv_weight, attn_gain, tiles, owned, parts)
    x = x_own
    if count:
        x = put(x_own, [lax.dynamic_index_in_dim(x_others, taken[n], 0, False) for n in range(count)])

    kept, sums = run_sums(layout, numbers, q_all, k_all)
    attended, inverse = run_forward(layout, numbers, q_all, k_all, v_all, kept)
    limit = threshold[0].astype(F32) / 1024.0
    ends = jnp.cumsum(lengths[0])
    positions = jnp.arange(rows, dtype=jnp.int32)
    passed = positions[:, None] >= ends[None, :]
    start = jnp.max(jnp.where(passed, ends[None, :], 0), axis=1)
    end = jnp.min(jnp.where(passed, rows, ends[None, :]), axis=1)
    over = jnp.maximum(4.0 / (end - start).astype(F32) * sums.reshape(rows) - limit, 0.0)
    excess_part = jnp.sum(jnp.where(positions // block_len == me, over, 0.0))

    out_c, branch_c, dx, mlp_gain_grad, early_grads = middle(
        attended, inverse, x, cot, out_weight, up_weight, down_weight, mlp_gain, dp_count
    )
    output = swap_tiles(out_c)
    branch = swap_tiles(branch_c)
    parts_hid = hid // width
    if early_grads.shape[0] != dp_count or early_grads.ndim != 3 or early_grads.shape[1] == width:
        down_grad = early_grads[:parts_hid].reshape(dp_count, -1, width)
        rest = early_grads[parts_hid:].reshape(parts_hid + 1, dp_count, -1, width).transpose(1, 0, 2, 3)
        early_grads = jnp.concatenate([down_grad, rest.reshape(dp_count, -1, width)], axis=1)
    early = lax.psum_scatter(early_grads, "dp", scatter_dimension=0, tiled=False)

    dq, dk, dv, totals = run_backward(layout, numbers, q_all, k_all, v_all, dx, kept)
    dk, dv, output, branch = lax.optimization_barrier((dk, dv, output, branch))
    if blocks == 2:
        far_totals = swap_seq(totals)
    else:
        far_totals = lax.all_gather(totals, "seq", axis=0, tiled=True)
    value_grad = value_weight_grad(normed_all, dk, dv)
    dq, dk = run_late(layout, numbers, q_all, k_all, far_totals, dq, dk)

    def back_through(base, number, dtype):
        return unproject(layout, numbers, base, number, dq, dk, dv, normed_all, qkv_weight, attn_gain, dtype)

    away, gain_away = back_through(owned, tiles - owned, BF16)
    if blocks == 2:
        back = swap_seq(away)
    else:
        by_block = jnp.concatenate([jnp.zeros((owned, tile, width), BF16), away]).reshape(blocks, block_len, width)
        back = lax.psum_scatter(jnp.roll(by_block, me, axis=0), "seq", scatter_dimension=0, tiled=False)
        back = back.reshape(by_tile)
    away, dq, dk = lax.optimization_barrier((away, dq, dk))
    query_grad = query_weight_grad(layout, numbers, normed_all, dq, dk)
    d_part, gain_home = back_through(0, owned, F32)
    gains = sum_everywhere(
        jnp.concatenate([gain_away + gain_home, mlp_gain_grad, jnp.full((1, 128), excess_part)], axis=1)
    )

    def over_seq(piece):
        if blocks == 2:
            return piece.astype(F32) + swap_seq(piece).astype(F32)
        return lax.psum(piece, "seq").astype(F32)

    halves = [grad.reshape(dp_count, -1, 3 * width // 2) for grad in (query_grad, value_grad)]
    if is_power(dp_count) and dp_count > 1:
        bits = list(range(len(powers(dp_count))))
        halves = [scatter_halving(halves[0], bits), scatter_halving(halves[1], bits[:1] + bits[2:] + bits[1:2])]
    else:
        halves = [lax.psum_scatter(grad, "dp", scatter_dimension=0, tiled=False) for grad in halves]
    late = jnp.concatenate(halves, axis=1)
    back, late, early = lax.optimization_barrier((back, late, early))
    qkv_piece = over_seq(late)
    early = over_seq(early)
    input_grad = finish_input(d_part, back, x_own, branch, attn_gain)

    part = width // dp_count
    n_down = hid // dp_count
    down_piece = early[:n_down]
    up_piece = early[n_down : 2 * n_down].reshape(hid // width, part, width).transpose(1, 0, 2).reshape(part, hid)
    out_piece = early[2 * n_down :]
    at = lax.axis_index("dp") * part
    attn_piece = lax.dynamic_slice_in_dim(gains[0], at, part)
    mlp_piece = lax.dynamic_slice_in_dim(gains[0], width + at, part)
    excess = (gains[0, 2 * width : 2 * width + 1] / (dp_count * rows)).reshape(1)
    return (
        output.reshape(1, block_len, width),
        input_grad.reshape(1, block_len, width),
        attn_piece,
        qkv_piece,
        out_piece,
        mlp_piece,
        up_piece,
        down_piece,
        excess,
    )


def solution(mesh):
    return jax.shard_map(
        on_device,
        mesh=mesh,
        in_specs=(
            P("dp", "seq", None),
            P("dp", "seq", None),
            P("dp", None),
            P(),
            P(),
            P(),
            P(),
            P(),
            P(),
            P(),
        ),
        out_specs=(
            P("dp", "seq", None),
            P("dp", "seq", None),
            P("dp"),
            P("dp", None),
            P("dp", None),
            P("dp"),
            P("dp", None),
            P("dp", None),
            P(),
        ),
        check_vma=False,
    )
```

```python
import functools
import itertools

import jax
import jax.numpy as jnp
import numpy as np
from jax import lax
from jax.experimental import pallas as pl
from jax.experimental.pallas import tpu as pltpu
from jax.sharding import PartitionSpec as P

HEADS = 12
HEAD_DIM = 64
PAIRS = HEADS // 2
PAIR = 2 * HEAD_DIM

LONG = 2048
SHORT = 512

LN_EPS = 1e-05
GELU_C = 0.7978845608028654
LOG2E = 1.4426950408889634
FAR = 1e30
VMEM_LIMIT = 60 * 2**20

BF16 = jnp.bfloat16
F32 = jnp.float32
NN = (((1,), (0,)), ((), ()))
NT = (((1,), (1,)), ((), ()))
TN = (((0,), (0,)), ((), ()))


def mm(left, right, dims):
    return lax.dot_general(left, right, dims, preferred_element_type=F32)


def pick_tile(block_len):
    return 256 if block_len % 256 == 0 else block_len


def layer_norm(values, gain):
    centre = jnp.mean(values, axis=-1, keepdims=True)
    shifted = values - centre
    spread = jnp.mean(shifted * shifted, axis=-1, keepdims=True)
    return shifted * lax.rsqrt(spread + LN_EPS) * gain


def gelu_tanh(values):
    return 0.5 * values * (1.0 + jnp.tanh(GELU_C * (values + 0.044715 * values * values * values)))


def split2(values):
    high = values.astype(BF16)
    return high, (values - high.astype(F32)).astype(BF16)


def half_masks(rows):
    lane = lax.broadcasted_iota(jnp.int32, (rows, PAIR), 1)
    return (lane < HEAD_DIM, lane >= HEAD_DIM)


class Layout:
    def __init__(self, rows, slots, tile, owned, blocks):
        self.tile, self.owned, self.blocks, self.tiles = tile, owned, blocks, owned * blocks
        self.aligned = SHORT % tile == 0
        self.count = 2 if blocks == 2 and owned >= 4 else 0
        ways = [[LONG, SHORT], [SHORT, LONG], [SHORT] * (rows // SHORT)]
        made = [self.plan(way + [0] * (slots - len(way)), me) for way in ways for me in range(blocks)]
        self.at, at, columns = {}, 0, []
        for name in made[0]:
            size = max(len(m[name]) for m in made)
            self.at[name] = (at, size)
            at += size
            columns.append([m[name] + m[name][-1:] * (size - len(m[name])) for m in made])
        self.table = np.array([sum((c[n] for c in columns), []) for n in range(len(made))], np.int32)

    def plan(self, lengths, me):
        tile, owned, blocks, tiles = self.tile, self.owned, self.blocks, self.tiles
        ends = [int(e) for e in np.cumsum(lengths)]
        low = [max([e for e in ends if e <= t * tile], default=0) // tile for t in range(tiles)]
        last = [min(e for e in ends if e > t * tile) for t in range(tiles)]
        length = [e - max([f for f in ends if f < e], default=0) for e in last]
        cost = [t - low[t] + 1 for t in range(tiles)]
        homes = [[b * owned + t for t in range(owned)] for b in range(blocks)]
        works = [list(h) for h in homes]
        given = [[0], [0]]
        if self.count:
            options = list(itertools.combinations(range(owned), self.count))

            def apart(choice):
                a, b = choice
                gain = sum(cost[owned + t] for t in b) - sum(cost[t] for t in a)
                return abs(sum(cost[:owned]) - sum(cost[owned:]) + 2 * gain), -sum(a), sum(b)

            given = list(min(itertools.product(options, options), key=apart))
            for side in range(2):
                for t, u in zip(given[side], given[1 - side]):
                    works[side][t] = (1 - side) * owned + u
        own = works[me]
        slot = [own.index(t) if t in own else -1 for t in range(tiles)]
        loc = [((t // owned - me) % blocks) * owned + t % owned for t in range(tiles)]
        far = works[1 - me] if blocks == 2 else [t if t not in own else -1 for t in range(tiles)]
        pairs = [(i, j) for i in range(tiles) for j in range(low[i], i + 1)]
        forward = [(i, j) for i, j in pairs if slot[i] >= 0]
        backward, flags = [], []
        for j in range(tiles):
            mine = [(i, j) for i in reversed(range(j, tiles)) if slot[i] >= 0 and low[i] <= j]
            marks = [1] * len(mine)
            if not mine:
                mine, marks = [(j, j)], [0]
            marks[0] += 2
            marks[-1] += 4
            backward += mine
            flags += marks
        late = [(i, j) for i, j in forward if any(f > i and low[f] <= j for f in far)]
        return {
            "ends": ends,
            "length": length,
            "loc": loc,
            "slot": slot,
            "own": own,
            "own_at": [loc[t] for t in own],
            "slot_loc": [slot[loc.index(t)] for t in range(tiles)],
            "far": far,
            "given": list(given[me]) if self.count else [0],
            "taken": list(given[1 - me]) if self.count else [0],
            "all_n": [len(pairs)],
            "all_i": [i for i, _ in pairs],
            "all_j": [j for _, j in pairs],
            "fwd_i": [i for i, _ in forward],
            "fwd_j": [j for _, j in forward],
            "fwd_f": [1 + 2 * (j == low[i]) for i, j in forward] + [0],
            "bwd_i": [i for i, _ in backward],
            "bwd_j": [j for _, j in backward],
            "bwd_f": flags + [0],
            "late_n": [len(late)],
            "late_i": [i for i, _ in late] + [0],
            "late_j": [j for _, j in late] + [0],
        }

    def chosen(self, lengths, me):
        way = jnp.where(lengths[0] == LONG, 0, jnp.where(lengths[1] == LONG, 1, 2))
        return lax.dynamic_index_in_dim(jnp.array(self.table), way * self.blocks + me, 0, keepdims=False)

    def get(self, numbers, name, index):
        return numbers[self.at[name][0] + index]

    def part(self, numbers, name):
        at, size = self.at[name]
        return numbers[at : at + size]

    def size(self, name):
        return self.at[name][1]


def tile_marks(layout, numbers, i, j):
    tile = layout.tile
    row = lax.broadcasted_iota(jnp.int32, (tile, tile), 0)
    key = lax.broadcasted_iota(jnp.int32, (tile, tile), 1)
    if layout.aligned:
        apart = key - row
        ahead = jnp.where(i == j, 0, tile)
        length = jnp.full((1, 1), layout.get(numbers, "length", i), jnp.int32)
        return apart < ahead, apart <= ahead, 4.0 / length.astype(F32)
    places = i * tile + lax.broadcasted_iota(jnp.int32, (tile, 1), 0)
    start = jnp.zeros((tile, 1), jnp.int32)
    end = jnp.full((tile, 1), 2**30, jnp.int32)
    for n in range(layout.size("ends")):
        edge = layout.get(numbers, "ends", n)
        start = jnp.maximum(start, jnp.where(places >= edge, edge, 0))
        end = jnp.minimum(end, jnp.where(places < edge, edge, 2**30))
    inside = j * tile + key >= start
    apart = (j - i) * tile + key - row
    return inside & (apart < 0), inside & (apart <= 0), 4.0 / (end - start).astype(F32)


def head0_scores(q_pair, k_pair, tile):
    first, _ = half_masks(tile)
    return mm(jnp.where(first, q_pair, 0), k_pair, NT) * HEAD_DIM**-0.5


def before_sum(chosen, tile):
    rows = lax.broadcasted_iota(jnp.int32, (tile, tile), 0)
    cols = lax.broadcasted_iota(jnp.int32, (tile, tile), 1)
    lower = (cols < rows).astype(F32).astype(BF16)
    high, low = split2(chosen)
    above = mm(lower, high, NN) + mm(lower, low, NN)
    return above, above[tile - 1 :, :] + chosen[tile - 1 :, :]


def after_sum(values, tile):
    rows = lax.broadcasted_iota(jnp.int32, (tile, tile), 0)
    cols = lax.broadcasted_iota(jnp.int32, (tile, tile), 1)
    upper = (cols > rows).astype(F32).astype(BF16)
    high, low = split2(values)
    below = mm(upper, high, NN) + mm(upper, low, NN)
    return below, below[:1, :] + values[:1, :]


def project_kernel(x_ref, w_ref, gain_ref, *refs):
    q_ref, k_ref, v_ref, normed_ref, x_out_ref = refs[-5:]
    x_out_ref[0] = x_ref[0]
    width = x_ref.shape[2]
    normed = layer_norm(x_ref[0].astype(F32), gain_ref[...]).astype(BF16)
    normed_ref[0] = normed
    for part, ref in enumerate((q_ref, k_ref, v_ref)):
        ref[0] = mm(normed, w_ref[:, part * width : (part + 1) * width], NN).astype(BF16)


UNROLL = 4


def sums_kernel(layout, numbers, q_ref, k_ref, kept_ref, sums_ref, column):
    tile = layout.tile
    last = layout.size("all_i") - 1

    def group_step(group, carry):
        for n in range(UNROLL):
            at = jnp.minimum(group * UNROLL + n, last)
            i, j = layout.get(numbers, "all_i", at), layout.get(numbers, "all_j", at)
            at_i, at_j = layout.get(numbers, "loc", i), layout.get(numbers, "loc", j)
            strict, _, _ = tile_marks(layout, numbers, i, j)
            scores = head0_scores(q_ref[at_i], k_ref[at_j], tile)
            chosen = jnp.where(strict, jnp.maximum(scores, 0.0), 0.0)
            column[group * UNROLL + n] = jnp.sum(chosen, axis=0, keepdims=True)
        return carry

    count = layout.get(numbers, "all_n", 0)
    lax.fori_loop(0, lax.div(count + (UNROLL - 1), jnp.int32(UNROLL)), group_step, 0)
    sums_ref[...] = jnp.zeros_like(sums_ref)

    def add_step(n, carry):
        i, j = layout.get(numbers, "all_i", n), layout.get(numbers, "all_j", n)
        kept_ref[i, j] = sums_ref[j]
        sums_ref[j] += column[n]
        return carry

    lax.fori_loop(0, count, add_step, 0)


def forward_kernel(layout, numbers, q_ref, k_ref, v_ref, kept_ref, att_ref, inv_ref, acc, pen):
    tile = layout.tile
    step = pl.program_id(0)
    i, j = layout.get(numbers, "fwd_i", step), layout.get(numbers, "fwd_j", step)
    flag = layout.get(numbers, "fwd_f", step)
    halves = half_masks(tile)

    @pl.when((flag & 2) != 0)
    def _():
        acc[...] = jnp.zeros_like(acc)

    @pl.when((flag & 1) != 0)
    def _():
        def logits_of(head):
            pair, half = divmod(head, 2)
            at = slice(pair * PAIR, (pair + 1) * PAIR)
            return mm(jnp.where(halves[half], q_ref[0, :, at], 0), k_ref[0, :, at], NT)

        def gather(head, numer):
            pair, half = divmod(head, 2)
            at = slice(pair * PAIR, (pair + 1) * PAIR)
            acc[head] += mm(numer, jnp.where(halves[half], v_ref[0, :, at], 1), NN)

        raw = {head: logits_of(head) for head in range(3)}
        strict, allowed, rate = tile_marks(layout, numbers, i, j)
        chosen = jnp.where(strict, jnp.maximum(raw[0] * HEAD_DIM**-0.5, 0.0), 0.0)
        above, _ = before_sum(chosen, tile)
        pen[...] = jnp.where(allowed, (rate * LOG2E) * (kept_ref[i, j] + above), FAR)
        waiting = {}
        for head in range(HEADS + 2):
            if 3 <= head + 3 < HEADS:
                raw[head + 3] = logits_of(head + 3)
            if head < HEADS:
                waiting[head] = jnp.exp2(raw.pop(head) * (HEAD_DIM**-0.5 * LOG2E) - pen[...]).astype(BF16)
            if head >= 2:
                gather(head - 2, waiting.pop(head - 2))

        @pl.when(i == j)
        def _():
            for pair in range(PAIRS):
                at = slice(pair * PAIR, (pair + 1) * PAIR)
                low, high = acc[2 * pair], acc[2 * pair + 1]
                numer = jnp.where(halves[0], low, high)
                inverse = 1.0 / pltpu.roll(jnp.where(halves[0], high, low), HEAD_DIM, 1)
                att_ref[0, :, at] = numer * inverse
                inv_ref[0, :, at] = inverse


def middle_kernel(
    tile, owned, chunk,
    numbers, att_ref, inv_ref, x_ref, cot_ref, wo_ref, wu_ref, wd_ref, gain_ref,
    out_ref, branch_ref, dx_ref, grads_ref,
    hid_s, dpre_s, low_s, normed_s, branch_s, stage_down, stage_rest, sems,
):
    step = pl.program_id(0)
    width = x_ref.shape[2]
    hid = wu_ref.shape[1]
    parts = hid // width
    joined = len(stage_rest.shape) == 4

    def shipment(n):
        source = stage_down.at[n] if n < parts else stage_rest.at[n - parts]
        if not joined:
            target = grads_ref.at[n]
        elif n < parts:
            some, long = stage_down.shape[1:3]
            target = grads_ref.at[pl.ds(n * some, some), pl.ds(0, long), :]
        else:
            share = stage_rest.shape[2]
            target = grads_ref.at[:, pl.ds(share * n, share), :]
        return pltpu.make_async_copy(source, target, sems.at[n])

    def ship(n, block):
        stage, at = (stage_down, n) if n < parts else (stage_rest, n - parts)
        stage[at] = block.astype(BF16).reshape(stage.shape[1:])
        shipment(n).start()

    @pl.when(step < owned)
    def _():
        at = pl.ds(pl.multiple_of(step * tile, tile), tile)
        attended = att_ref[0]
        cot = cot_ref[at, :]
        gain = gain_ref[...]
        low = attended.astype(BF16)
        low_s[at, :] = low
        residual = x_ref[0].astype(F32) + mm(low, wo_ref[...], NN)
        centre = jnp.mean(residual, axis=1, keepdims=True)
        shifted = residual - centre
        scale = lax.rsqrt(jnp.mean(shifted * shifted, axis=1, keepdims=True) + LN_EPS)
        xhat = shifted * scale
        normed = (xhat * gain).astype(BF16)
        normed_s[at, :] = normed
        result = residual
        d_normed = jnp.zeros((tile, width), F32)
        for c in range(hid // chunk):
            cols = slice(c * chunk, (c + 1) * chunk)
            pre = mm(normed, wu_ref[:, cols], NN)
            square = pre * pre
            wave = jnp.tanh(pre * (GELU_C + (GELU_C * 0.044715) * square))
            rising = 0.5 + 0.5 * wave
            hidden = (pre * rising).astype(BF16)
            bend = pre * ((0.5 * GELU_C) + (1.5 * GELU_C * 0.044715) * square)
            d_pre = (mm(cot, wd_ref[cols, :], NT) * (rising + bend * (1.0 - wave * wave))).astype(BF16)
            hid_s[at, cols] = hidden
            dpre_s[at, cols] = d_pre
            result = result + mm(hidden, wd_ref[cols, :], NN)
            d_normed = d_normed + mm(d_pre, wu_ref[:, cols], NT)
        out_ref[0] = result.astype(BF16)
        grown = d_normed * gain
        mean_grown = jnp.mean(grown, axis=1, keepdims=True)
        mean_both = jnp.mean(grown * xhat, axis=1, keepdims=True)
        branch = (cot.astype(F32) + scale * (grown - mean_grown - xhat * mean_both)).astype(BF16)
        branch_ref[0] = branch
        branch_s[at, :] = branch
        d_attended = mm(branch, wo_ref[...], NT).astype(BF16).astype(F32)
        scaled = (d_attended * inv_ref[0]).astype(BF16)
        product = scaled.astype(F32) * attended
        rows = lax.broadcasted_iota(jnp.int32, (PAIR, 2 * PAIR), 0)
        cols = lax.broadcasted_iota(jnp.int32, (PAIR, 2 * PAIR), 1)
        block = cols // HEAD_DIM
        spread = jnp.where(block == jnp.where(rows < HEAD_DIM, 1, 2), -1.0, 0.0).astype(BF16)
        lane = lax.broadcasted_iota(jnp.int32, (tile, 2 * PAIR), 1) % HEAD_DIM
        first, _ = half_masks(tile)
        for pair in range(PAIRS):
            here = slice(pair * PAIR, (pair + 1) * PAIR)
            high, rest = split2(product[:, here])
            minus_dot = mm(high, spread, NN) + mm(rest, spread, NN)
            dot_high, dot_low = split2(minus_dot)
            side = jnp.where(lane == 0, dot_high, jnp.where(lane == 1, dot_low, 0))
            mine = scaled[:, here]
            base = 2 * pair * PAIR
            dx_ref[0, :, base : base + PAIR] = jnp.where(first, mine, side[:, :PAIR])
            dx_ref[0, :, base + PAIR : base + 2 * PAIR] = jnp.where(first, side[:, PAIR:], mine)

    for c in range(parts):
        @pl.when(step == owned + c)
        def _(c=c):
            cols = slice(c * width, (c + 1) * width)
            ship(c, mm(hid_s[:, cols], cot_ref[...], TN))
            ship(parts + c, mm(normed_s[...], dpre_s[:, cols], TN))
            if c == parts - 1:
                ship(2 * parts, mm(low_s[...], branch_s[...], TN))
                for n in range(2 * parts + 1):
                    shipment(n).wait()


def backward_kernel(
    layout, numbers, q_ref, k_ref, v_ref, dx_ref, kept_ref,
    dq_ref, dk_ref, dv_ref, later_ref,
    acc_q, acc_k, acc_v, pen, dpen, later,
):
    tile = layout.tile
    step = pl.program_id(0)
    i, j = layout.get(numbers, "bwd_i", step), layout.get(numbers, "bwd_j", step)
    flag = layout.get(numbers, "bwd_f", step)
    halves = half_masks(tile)

    @pl.when(step == 0)
    def _():
        acc_q[...] = jnp.zeros_like(acc_q)
        later_ref[...] = jnp.zeros_like(later_ref)

    @pl.when((flag & 2) != 0)
    def _():
        acc_k[...] = jnp.zeros_like(acc_k)
        acc_v[...] = jnp.zeros_like(acc_v)
        later[...] = jnp.zeros_like(later)

    @pl.when((flag & 1) != 0)
    def _():
        slot = layout.get(numbers, "slot", i)
        scores0 = head0_scores(q_ref[0, :, :PAIR], k_ref[0, :, :PAIR], tile)

        def products(pair):
            at = slice(pair * PAIR, (pair + 1) * PAIR)
            k_pair, q_pair, v_pair = k_ref[0, :, at], q_ref[0, :, at], v_ref[0, :, at]
            made = []
            for half in range(2):
                head = 2 * pair + half
                scores = scores0 if head == 0 else mm(jnp.where(halves[half], q_pair, 0), k_pair, NT) * HEAD_DIM**-0.5
                dx = dx_ref[0, :, head * PAIR : (head + 1) * PAIR]
                made.append((scores, mm(dx, jnp.where(halves[half], v_pair, 1), NT)))
            return made

        made = {PAIRS - 1: products(PAIRS - 1)}
        ready = {}
        strict, allowed, rate = tile_marks(layout, numbers, i, j)
        chosen = jnp.where(strict, jnp.maximum(scores0, 0.0), 0.0)
        above, _ = before_sum(chosen, tile)
        pen[...] = jnp.where(allowed, (rate * LOG2E) * (kept_ref[i, j] + above), FAR)

        def pointwise(pair, made):
            grads, weights = [], []
            for scores, d_probs in made:
                numer = jnp.exp2(scores * LOG2E - pen[...])
                weights.append(numer.astype(BF16))
                grads.append(numer * d_probs)
            both = grads[0] + grads[1]
            if pair == PAIRS - 1:
                dpen[...] = both
            elif pair > 0:
                dpen[...] += both
            else:
                below, total = after_sum(dpen[...] + both, tile)
                picked = strict & (scores0 > 0.0)
                grads[0] = grads[0] + jnp.where(picked, -rate * (later[...] + below), 0.0)
                later[...] = later[...] + total
                later_ref[slot, j] = total
            return weights, [g.astype(BF16) for g in grads]

        def collect(pair, weights, lows):
            at = slice(pair * PAIR, (pair + 1) * PAIR)
            k_pair, q_pair = k_ref[0, :, at], q_ref[0, :, at]
            d_q = None
            for half in range(2):
                head = 2 * pair + half
                part = slice(half * HEAD_DIM, (half + 1) * HEAD_DIM)
                head_at = slice(head * HEAD_DIM, (head + 1) * HEAD_DIM)
                dx = dx_ref[0, :, head * PAIR : (head + 1) * PAIR]
                acc_v[head_at, :] += mm(dx, weights[half], TN)[part]
                acc_k[head_at, :] += mm(q_pair, lows[half], TN)[part]
                more = mm(lows[half], jnp.where(halves[half], k_pair, 0), NN)
                d_q = more if d_q is None else d_q + more
            acc_q[slot, :, at] += d_q

        for pair in range(PAIRS - 1, -2, -1):
            if pair > 0:
                made[pair - 1] = products(pair - 1)
            if pair >= 0:
                ready[pair] = pointwise(pair, made.pop(pair))
            if pair + 1 in ready:
                collect(pair + 1, *ready.pop(pair + 1))

    @pl.when((flag & 4) != 0)
    def _():
        dk_ref[0] = jnp.transpose((acc_k[...] * HEAD_DIM**-0.5).astype(BF16))
        dv_ref[0] = jnp.transpose(acc_v[...].astype(BF16))

    @pl.when(step == pl.num_programs(0) - 1)
    def _():
        for slot in range(acc_q.shape[0]):
            dq_ref[slot] = (acc_q[slot] * HEAD_DIM**-0.5).astype(BF16)


def late_kernel(
    layout, numbers, q_ref, k_ref, far_totals_ref, dq_in_ref, dk_in_ref,
    dq_ref, dk_ref,
    acc_q, acc_k,
):
    tile = layout.tile
    first, _ = half_masks(tile)
    acc_q[...] = jnp.zeros_like(acc_q)
    acc_k[...] = jnp.zeros_like(acc_k)
    count = layout.get(numbers, "late_n", 0)

    def group_step(group, carry):
        adds = []
        for n in range(UNROLL):
            at = group * UNROLL + n
            valid = at < count
            at = jnp.minimum(at, layout.size("late_i") - 1)
            i, j = layout.get(numbers, "late_i", at), layout.get(numbers, "late_j", at)
            slot, at_i, at_j = (layout.get(numbers, name, t) for name, t in (("slot", i), ("loc", i), ("loc", j)))
            slot = jnp.maximum(slot, 0)
            later = jnp.zeros((1, tile), F32)
            for f in range(layout.size("far")):
                later += jnp.where(valid & (layout.get(numbers, "far", f) > i), far_totals_ref[f, j], 0.0)
            strict, _, rate = tile_marks(layout, numbers, i, j)
            scores = head0_scores(q_ref[at_i], k_ref[at_j], tile)
            factor = (-(HEAD_DIM**-0.5) * rate) * later
            d_low = jnp.where(strict & (scores > 0.0), factor, 0.0).astype(BF16)
            adds.append((slot, at_j, mm(q_ref[at_i], d_low, TN), mm(d_low, k_ref[at_j], NN)))
        for slot, at_j, for_k, for_q in adds:
            acc_k[at_j] += for_k
            acc_q[slot] += for_q
        return carry

    lax.fori_loop(0, lax.div(count + (UNROLL - 1), jnp.int32(UNROLL)), group_step, 0)
    for slot in range(acc_q.shape[0]):
        dq_ref[slot] = (dq_in_ref[slot].astype(F32) + jnp.where(first, acc_q[slot], 0.0)).astype(BF16)

    def finish(t, carry):
        dk_ref[t] = (dk_in_ref[t].astype(F32) + jnp.where(first, jnp.transpose(acc_k[t]), 0.0)).astype(BF16)
        return carry

    lax.fori_loop(0, acc_k.shape[0], finish, 0)


def through_weight(layout, base, numbers, dq_ref, dk_ref, dv_ref, w_ref):
    width = dq_ref.shape[2]
    slot = layout.get(numbers, "slot_loc", base + pl.program_id(0))
    d_query = jnp.where(slot >= 0, dq_ref[0], jnp.zeros_like(dq_ref[0]))
    return (
        mm(dv_ref[0], w_ref[:, 2 * width :], NT)
        + mm(dk_ref[0], w_ref[:, width : 2 * width], NT)
        + mm(d_query, w_ref[:, :width], NT)
    )


def away_kernel(layout, base, numbers, dq_ref, dk_ref, dv_ref, w_ref, out_ref):
    out_ref[0] = through_weight(layout, base, numbers, dq_ref, dk_ref, dv_ref, w_ref).astype(BF16)


def home_kernel(layout, numbers, dq_ref, dk_ref, dv_ref, w_ref, back_ref, x_ref, branch_ref, gain_ref, out_ref):
    values = x_ref[0].astype(F32)
    shifted = values - jnp.mean(values, axis=1, keepdims=True)
    scale = lax.rsqrt(jnp.mean(shifted * shifted, axis=1, keepdims=True) + LN_EPS)
    xhat = shifted * scale
    d_normed = through_weight(layout, 0, numbers, dq_ref, dk_ref, dv_ref, w_ref)
    grown = (d_normed + back_ref[0].astype(F32)) * gain_ref[...]
    mean_grown = jnp.mean(grown, axis=1, keepdims=True)
    mean_both = jnp.mean(grown * xhat, axis=1, keepdims=True)
    dx = scale * (grown - mean_grown - xhat * mean_both)
    out_ref[0] = (branch_ref[0].astype(F32) + dx).astype(BF16)


def flat(ref, cols):
    block = ref[:, :, cols]
    return block.reshape(block.shape[0] * block.shape[1], block.shape[2])


def value_weight_kernel(normed_ref, dk_ref, dv_ref, out_ref):
    width = normed_ref.shape[2]
    half = width // 2
    normed = flat(normed_ref, slice(None))
    out_ref[:, :half] = mm(normed, flat(dk_ref, slice(half, width)), TN).astype(BF16)
    out_ref[:, half:] = mm(normed, flat(dv_ref, slice(None)), TN).astype(BF16)


def query_weight_kernel(layout, numbers, normed_ref, dq_ref, dk_ref, out_ref):
    width = normed_ref.shape[2]
    half = width // 2
    total = jnp.zeros((width, width), F32)
    for slot in range(layout.owned):
        total += mm(normed_ref[layout.get(numbers, "own_at", slot)], dq_ref[slot], TN)
    out_ref[:, :width] = total.astype(BF16)
    out_ref[:, width:] = mm(flat(normed_ref, slice(None)), flat(dk_ref, slice(0, half)), TN).astype(BF16)


SMEM = pl.BlockSpec(memory_space=pltpu.SMEM)
VMEM = pl.BlockSpec(memory_space=pltpu.VMEM)


def estimate(flops):
    flops = int(flops)
    return pl.CostEstimate(flops=flops, bytes_accessed=flops // 600, transcendentals=0)


def held(shape):
    return pl.BlockSpec(shape, lambda *_: (0,) * len(shape), pipeline_mode=pl.Buffered(1))


def fixed(shape):
    return pl.BlockSpec(shape, lambda *_: (0,) * len(shape))


def sds(shape, dtype):
    return jax.ShapeDtypeStruct(shape, dtype)


def project(x, weight, gain, tiles, first, into):
    owned, tile, width = x.shape
    outs = (sds((tiles, tile, width), BF16),) * 5
    row = pl.BlockSpec((1, tile, width), lambda s: (s, 0, 0))
    placed = pl.BlockSpec((1, tile, width), lambda s: (s + first, 0, 0))
    extra = [pl.BlockSpec(memory_space=pl.ANY)] * len(into)
    return pl.pallas_call(
        project_kernel,
        grid=(owned,),
        out_shape=outs,
        in_specs=[row, held(weight.shape), held(gain.shape)] + extra,
        out_specs=(placed,) * 5,
        input_output_aliases={3 + n: n for n in range(len(into))},
        compiler_params=pltpu.CompilerParams(vmem_limit_bytes=20 * 2**20),
        cost_estimate=estimate(2 * owned * tile * width * weight.shape[1]),
    )(x, weight, gain, *into)


def middle(layout, numbers, attended, inverse, x, cot, wo, wu, wd, gain, dp_count):
    owned, tile, width = attended.shape
    hid = wu.shape[1]
    parts = hid // width
    rows = owned * tile
    row = pl.BlockSpec((1, tile, width), lambda s, n: (jnp.minimum(s, owned - 1), 0, 0))
    wide = pl.BlockSpec((1, tile, 2 * width), lambda s, n: (jnp.minimum(s, owned - 1), 0, 0))

    def token_place(s, n):
        return layout.get(n, "own_at", jnp.minimum(s, owned - 1)), 0, 0

    share = width // dp_count
    joined = share % 16 == 0 and dp_count % parts == 0
    if joined:
        stage_down = (parts, dp_count // parts, share * parts, width)
        stage_rest = (parts + 1, dp_count, share, width)
        grads = (dp_count, share * (2 * parts + 1), width)
    else:
        stage_down, stage_rest, grads = ((n, width, width) for n in (parts, parts + 1, 2 * parts + 1))
    return kernel_call(
        functools.partial(middle_kernel, tile, owned, width), VMEM_LIMIT // 2**20, (owned + parts,), numbers,
        (attended, inverse, x, cot, wo, wu, wd, gain),
        [
            row, row, pl.BlockSpec((1, tile, width), token_place), held((rows, width)),
            held(wo.shape), held(wu.shape), held(wd.shape), held(gain.shape),
        ],
        (
            sds((owned, tile, width), BF16),
            sds((owned, tile, width), BF16),
            sds((owned, tile, 2 * width), BF16),
            sds(grads, BF16),
        ),
        (row, row, wide, pl.BlockSpec(memory_space=pl.ANY)),
        [
            pltpu.VMEM((rows, hid), BF16),
            pltpu.VMEM((rows, hid), BF16),
            pltpu.VMEM((rows, width), BF16),
            pltpu.VMEM((rows, width), BF16),
            pltpu.VMEM((rows, width), BF16),
            pltpu.VMEM(stage_down, BF16),
            pltpu.VMEM(stage_rest, BF16),
            pltpu.SemaphoreType.DMA((2 * parts + 1,)),
        ],
        2 * rows * width * (3 * width + 6 * hid),
    )


def kernel_call(kernel, room, grid, numbers, operands, in_specs, outs, out_specs, scratch, flops, aliases=None):
    return pl.pallas_call(
        kernel,
        grid_spec=pltpu.PrefetchScalarGridSpec(
            num_scalar_prefetch=1, grid=grid, in_specs=in_specs, out_specs=out_specs, scratch_shapes=scratch
        ),
        out_shape=outs,
        input_output_aliases=aliases or {},
        compiler_params=pltpu.CompilerParams(vmem_limit_bytes=room * 2**20),
        cost_estimate=estimate(flops),
    )(numbers, *operands)


def run_sums(layout, numbers, q, k):
    tiles, tile, _ = q.shape
    every = pl.BlockSpec((tiles, tile, PAIR), lambda n, x: (0, 0, 0))
    kept, sums = (tiles, tiles, 1, tile), (tiles, 1, tile)
    groups = -(-layout.size("all_i") // UNROLL) * UNROLL
    return kernel_call(
        functools.partial(sums_kernel, layout), 20, (1,), numbers, (q, k), [every, every],
        (sds(kept, F32), sds(sums, F32)), (fixed(kept), fixed(sums)),
        [pltpu.VMEM((groups, 1, tile), F32)], tiles * tiles * tile * tile * PAIR,
    )


def run_forward(layout, numbers, q, k, v, kept):
    tiles, tile, width = q.shape
    get, owned = layout.get, layout.owned
    rows = pl.BlockSpec((1, tile, width), lambda n, x: (get(x, "loc", get(x, "fwd_i", n)), 0, 0))
    keys = pl.BlockSpec((1, tile, width), lambda n, x: (get(x, "loc", get(x, "fwd_j", n)), 0, 0))
    slots = pl.BlockSpec((1, tile, width), lambda n, x: (get(x, "slot", get(x, "fwd_i", n)), 0, 0))
    return kernel_call(
        functools.partial(forward_kernel, layout), 20, (layout.size("fwd_i"),), numbers,
        (q, k, v, kept), [rows, keys, keys, fixed(kept.shape)],
        (sds((owned, tile, width), F32),) * 2, (slots, slots),
        [pltpu.VMEM((HEADS, tile, PAIR), F32), pltpu.VMEM((tile, tile), F32)],
        4 * layout.size("fwd_i") * tile * tile * width,
    )


def run_backward(layout, numbers, q, k, v, dx, kept):
    tiles, tile, width = q.shape
    get, owned = layout.get, layout.owned
    rows = pl.BlockSpec((1, tile, width), lambda n, x: (get(x, "loc", get(x, "bwd_i", n)), 0, 0))
    keys = pl.BlockSpec((1, tile, width), lambda n, x: (get(x, "loc", get(x, "bwd_j", n)), 0, 0))
    slots = pl.BlockSpec(
        (1, tile, 2 * width), lambda n, x: (jnp.maximum(get(x, "slot", get(x, "bwd_i", n)), 0), 0, 0)
    )
    totals = (owned, tiles, 1, tile)
    return kernel_call(
        functools.partial(backward_kernel, layout), 28, (layout.size("bwd_i"),), numbers,
        (q, k, v, dx, kept), [rows, keys, keys, slots, fixed(kept.shape)],
        (
            sds((owned, tile, width), BF16),
            sds((tiles, tile, width), BF16),
            sds((tiles, tile, width), BF16),
            sds(totals, F32),
        ),
        (fixed((owned, tile, width)), keys, keys, fixed(totals)),
        [
            pltpu.VMEM((owned, tile, width), F32),
            pltpu.VMEM((width, tile), F32),
            pltpu.VMEM((width, tile), F32),
            pltpu.VMEM((tile, tile), F32),
            pltpu.VMEM((tile, tile), F32),
            pltpu.VMEM((1, tile), F32),
        ],
        10 * layout.size("bwd_i") * tile * tile * width,
    )


def run_late(layout, numbers, q, k, far_totals, dq, dk):
    tiles, tile, _ = q.shape
    owned = dq.shape[0]
    some = pl.BlockSpec((owned, tile, PAIR), lambda n, x: (0, 0, 0))
    every = pl.BlockSpec((tiles, tile, PAIR), lambda n, x: (0, 0, 0))
    return kernel_call(
        functools.partial(late_kernel, layout), 16, (1,), numbers,
        (q, k, far_totals, dq, dk), [every, every, fixed(far_totals.shape), some, every],
        (sds(dq.shape, BF16), sds(dk.shape, BF16)), (some, every),
        [pltpu.VMEM((owned, tile, PAIR), F32), pltpu.VMEM((tiles, PAIR, tile), F32)],
        6 * layout.size("late_i") * tile * tile * PAIR,
        {4: 0, 5: 1},
    )


def tile_specs(layout, base, width):
    tile = layout.tile
    row = pl.BlockSpec((1, tile, width), lambda s, x: (s, 0, 0))
    placed = pl.BlockSpec((1, tile, width), lambda s, x: (base + s, 0, 0))
    picked = pl.BlockSpec((1, tile, width), lambda s, x: (jnp.maximum(layout.get(x, "slot_loc", base + s), 0), 0, 0))
    return row, placed, picked


def run_away(layout, numbers, dq, dk, dv, weight):
    width, count, base = dq.shape[2], layout.tiles - layout.owned, layout.owned
    row, placed, picked = tile_specs(layout, base, width)
    return kernel_call(
        functools.partial(away_kernel, layout, base), 20, (count,), numbers, (dq, dk, dv, weight),
        [picked, placed, placed, held(weight.shape)], sds((count, layout.tile, width), BF16), row,
        [], 2 * count * layout.tile * width * weight.shape[1],
    )


def run_home(layout, numbers, dq, dk, dv, weight, back, x, branch, gain):
    width = dq.shape[2]
    row, placed, picked = tile_specs(layout, 0, width)
    return kernel_call(
        functools.partial(home_kernel, layout), 56, (layout.owned,), numbers,
        (dq, dk, dv, weight, back, x, branch, gain),
        [picked, placed, placed, held(weight.shape), row, row, row, held(gain.shape)],
        sds(x.shape, BF16), row, [], 2 * x.shape[0] * layout.tile * width * weight.shape[1],
    )


def value_weight_grad(normed, dk, dv):
    width = normed.shape[2]
    return pl.pallas_call(
        value_weight_kernel,
        out_shape=sds((width, 3 * width // 2), BF16),
        in_specs=[VMEM] * 3,
        out_specs=VMEM,
        compiler_params=pltpu.CompilerParams(vmem_limit_bytes=30 * 2**20),
        cost_estimate=estimate(3 * normed.shape[0] * normed.shape[1] * width * width),
    )(normed, dk, dv)


def query_weight_grad(layout, numbers, normed, dq, dk):
    width = normed.shape[2]
    return pl.pallas_call(
        functools.partial(query_weight_kernel, layout),
        out_shape=sds((width, 3 * width // 2), BF16),
        in_specs=[SMEM, VMEM, VMEM, VMEM],
        out_specs=VMEM,
        compiler_params=pltpu.CompilerParams(vmem_limit_bytes=28 * 2**20),
        cost_estimate=estimate(2 * normed.shape[0] * normed.shape[1] * width * width),
    )(numbers, normed, dq, dk)


def swap_seq(array):
    return lax.ppermute(array, "seq", [(0, 1), (1, 0)])


def powers(size):
    return [1 << n for n in range(size.bit_length() - 1)]


def is_power(size):
    return size & (size - 1) == 0


def scatter_halving(grad, order):
    count = lax.axis_size("dp")
    index = lax.axis_index("dp")
    bits = len(powers(count))
    held_bits = list(range(bits))[::-1]
    parts = grad.reshape((2,) * bits + grad.shape[1:])
    for n in order:
        axis = held_bits.index(n)
        held_bits.remove(n)
        mine = (index >> n) & 1
        keep = lax.dynamic_index_in_dim(parts, mine, axis, keepdims=False)
        send = lax.dynamic_index_in_dim(parts, 1 - mine, axis, keepdims=False)
        got = lax.ppermute(send, "dp", [(i, i ^ (1 << n)) for i in range(count)])
        parts = (keep.astype(F32) + got.astype(F32)).astype(BF16)
    return parts


def on_device(
    tokens, cotangent, lengths, threshold, attn_gain, qkv_weight, out_weight, mlp_gain, up_weight, down_weight
):
    _, block_len, width = tokens.shape
    blocks = lax.axis_size("seq")
    dp_count = lax.axis_size("dp")
    me = lax.axis_index("seq")
    tile = pick_tile(block_len)
    owned = block_len // tile
    tiles = owned * blocks
    rows = blocks * block_len
    hid = up_weight.shape[1]
    token_own = tokens[0]
    cot_own = cotangent[0]
    attn_gain = attn_gain.reshape(1, width)
    mlp_gain = mlp_gain.reshape(1, width)
    by_tile = (owned, tile, width)

    layout = Layout(rows, lengths.shape[1], tile, owned, blocks)
    count = layout.count
    numbers = layout.chosen(lengths[0], me)
    given = layout.part(numbers, "given")

    def put(array, pieces):
        for n in range(count):
            array = lax.dynamic_update_slice_in_dim(array, pieces[n][None], given[n], 0)
        return array

    def swap_tiles(array):
        if count == 0:
            return array
        sent = jnp.stack([lax.dynamic_index_in_dim(array, given[n], 0, False) for n in range(count)])
        return put(array, swap_seq(sent))

    x_own = token_own.reshape(by_tile)
    if blocks == 2:
        x_others = swap_seq(token_own).reshape(by_tile)
    else:
        gathered = lax.all_gather(token_own, "seq", axis=0, tiled=False)
        x_others = jnp.roll(gathered, -me, axis=0)[1:].reshape(tiles - owned, tile, width)
    cot_tiles, x_others = lax.optimization_barrier((cot_own.reshape(by_tile), x_others))
    cot = swap_tiles(cot_tiles).reshape(block_len, width)
    parts = project(x_own, qkv_weight, attn_gain, tiles, 0, ())
    q_all, k_all, v_all, normed_all, x_all = project(x_others, qkv_weight, attn_gain, tiles, owned, parts)

    kept, sums = run_sums(layout, numbers, q_all, k_all)
    attended, inverse = run_forward(layout, numbers, q_all, k_all, v_all, kept)
    limit = threshold[0].astype(F32) / 1024.0
    ends = jnp.cumsum(lengths[0])
    positions = jnp.arange(rows, dtype=jnp.int32)
    passed = positions[:, None] >= ends[None, :]
    start = jnp.max(jnp.where(passed, ends[None, :], 0), axis=1)
    end = jnp.min(jnp.where(passed, rows, ends[None, :]), axis=1)
    over = jnp.maximum(4.0 / (end - start).astype(F32) * sums.reshape(rows) - limit, 0.0)
    excess = jnp.full((1, 128), jnp.sum(jnp.where(positions // block_len == me, over, 0.0)))
    hops = [("dp", bit) for bit in powers(dp_count)] + [("seq", bit) for bit in powers(blocks)]
    if not (is_power(dp_count) and is_power(blocks)):
        excess, hops = lax.psum(excess, ("seq", "dp")), []

    def hop_beside(excess, result):
        if hops:
            axis, bit = hops.pop(0)
            excess += lax.ppermute(excess, axis, [(i, i ^ bit) for i in range(lax.axis_size(axis))])
        return lax.optimization_barrier((excess, result))

    excess, attended = hop_beside(excess, attended)

    out_c, branch_c, dx, early_grads = middle(
        layout, numbers, attended, inverse, x_all, cot, out_weight, up_weight, down_weight, mlp_gain, dp_count
    )
    excess, dx = hop_beside(excess, dx)
    output = swap_tiles(out_c)
    branch = swap_tiles(branch_c)
    parts_hid = hid // width
    if early_grads.shape[0] != dp_count or early_grads.ndim != 3 or early_grads.shape[1] == width:
        down_grad = early_grads[:parts_hid].reshape(dp_count, -1, width)
        rest = early_grads[parts_hid:].reshape(parts_hid + 1, dp_count, -1, width).transpose(1, 0, 2, 3)
        early_grads = jnp.concatenate([down_grad, rest.reshape(dp_count, -1, width)], axis=1)
    early = lax.psum_scatter(early_grads, "dp", scatter_dimension=0, tiled=False)

    dq, dk, dv, totals = run_backward(layout, numbers, q_all, k_all, v_all, dx, kept)
    excess, (dk, dv, output, branch) = hop_beside(excess, (dk, dv, output, branch))
    if blocks == 2:
        far_totals = swap_seq(totals)
    else:
        far_totals = lax.all_gather(totals, "seq", axis=0, tiled=True)
    value_grad = value_weight_grad(normed_all, dk, dv)
    excess, far_totals = hop_beside(excess, far_totals)
    dq, dk = run_late(layout, numbers, q_all, k_all, far_totals, dq, dk)

    away = run_away(layout, numbers, dq, dk, dv, qkv_weight)
    if blocks == 2:
        back = swap_seq(away)
    else:
        by_block = jnp.concatenate([jnp.zeros((owned, tile, width), BF16), away]).reshape(blocks, block_len, width)
        back = lax.psum_scatter(jnp.roll(by_block, me, axis=0), "seq", scatter_dimension=0, tiled=False)
        back = back.reshape(by_tile)
    away, dq, dk = lax.optimization_barrier((away, dq, dk))
    excess, dq = hop_beside(excess, dq)
    query_grad = query_weight_grad(layout, numbers, normed_all, dq, dk)
    def over_seq(piece):
        if blocks == 2:
            return piece.astype(F32) + swap_seq(piece).astype(F32)
        return lax.psum(piece, "seq").astype(F32)

    halves = [grad.reshape(dp_count, -1, 3 * width // 2) for grad in (query_grad, value_grad)]
    if is_power(dp_count) and dp_count > 1:
        bits = list(range(len(powers(dp_count))))
        halves = [scatter_halving(halves[0], bits), scatter_halving(halves[1], bits[:1] + bits[2:] + bits[1:2])]
    else:
        halves = [lax.psum_scatter(grad, "dp", scatter_dimension=0, tiled=False) for grad in halves]
    late = jnp.concatenate(halves, axis=1)
    back, late, early = lax.optimization_barrier((back, late, early))
    qkv_piece = over_seq(late)
    early = over_seq(early)
    input_grad = run_home(layout, numbers, dq, dk, dv, qkv_weight, back, x_own, branch, attn_gain)

    part = width // dp_count
    n_down = hid // dp_count
    down_piece = early[:n_down]
    up_piece = early[n_down : 2 * n_down].reshape(hid // width, part, width).transpose(1, 0, 2).reshape(part, hid)
    out_piece = early[2 * n_down :]
    at = lax.axis_index("dp") * part

    def gain_grad(weight, weight_grad, gain):
        mine = lax.dynamic_slice_in_dim(weight, at, part).astype(F32)
        return jnp.sum(mine * weight_grad, axis=1) / lax.dynamic_slice_in_dim(gain[0], at, part)

    attn_piece = gain_grad(qkv_weight, qkv_piece, attn_gain)
    mlp_piece = gain_grad(up_weight, up_piece, mlp_gain)
    while hops:
        excess, _ = hop_beside(excess, excess)
    excess = excess[0, :1] / (dp_count * rows)
    return (
        output.reshape(1, block_len, width),
        input_grad.reshape(1, block_len, width),
        attn_piece,
        qkv_piece,
        out_piece,
        mlp_piece,
        up_piece,
        down_piece,
        excess,
    )


def solution(mesh):
    return jax.shard_map(
        on_device,
        mesh=mesh,
        in_specs=(
            P("dp", "seq", None),
            P("dp", "seq", None),
            P("dp", None),
            P(),
            P(),
            P(),
            P(),
            P(),
            P(),
            P(),
        ),
        out_specs=(
            P("dp", "seq", None),
            P("dp", "seq", None),
            P("dp"),
            P("dp", None),
            P("dp", None),
            P("dp"),
            P("dp", None),
            P("dp", None),
            P(),
        ),
        check_vma=False,
    )
```

```python
import functools
import itertools

import jax
import jax.numpy as jnp
import numpy as np
from jax import lax
from jax.experimental import pallas as pl
from jax.experimental.pallas import tpu as pltpu
from jax.sharding import PartitionSpec as P

HEADS = 12
HEAD_DIM = 64
PAIRS = HEADS // 2
PAIR = 2 * HEAD_DIM

LONG = 2048
SHORT = 512

LN_EPS = 1e-05
GELU_C = 0.7978845608028654
LOG2E = 1.4426950408889634
FAR = 1e30
VMEM_LIMIT = 60 * 2**20

BF16 = jnp.bfloat16
F32 = jnp.float32
NN = (((1,), (0,)), ((), ()))
NT = (((1,), (1,)), ((), ()))
TN = (((0,), (0,)), ((), ()))


def mm(left, right, dims):
    return lax.dot_general(left, right, dims, preferred_element_type=F32)


def pick_tile(block_len):
    return 256 if block_len % 256 == 0 else block_len


def layer_norm(values, gain):
    centre = jnp.mean(values, axis=-1, keepdims=True)
    shifted = values - centre
    spread = jnp.mean(shifted * shifted, axis=-1, keepdims=True)
    return shifted * lax.rsqrt(spread + LN_EPS) * gain


def gelu_tanh(values):
    return 0.5 * values * (1.0 + jnp.tanh(GELU_C * (values + 0.044715 * values * values * values)))


def split2(values):
    high = values.astype(BF16)
    return high, (values - high.astype(F32)).astype(BF16)


def half_masks(rows):
    lane = lax.broadcasted_iota(jnp.int32, (rows, PAIR), 1)
    return (lane < HEAD_DIM, lane >= HEAD_DIM)


class Layout:
    def __init__(self, rows, slots, tile, owned, blocks):
        self.tile, self.owned, self.blocks, self.tiles = tile, owned, blocks, owned * blocks
        self.aligned = SHORT % tile == 0
        self.count = 2 if blocks == 2 and owned >= 4 else 0
        ways = [[LONG, SHORT], [SHORT, LONG], [SHORT] * (rows // SHORT)]
        made = [self.plan(way + [0] * (slots - len(way)), me) for way in ways for me in range(blocks)]
        self.at, at, columns = {}, 0, []
        for name in made[0]:
            size = max(len(m[name]) for m in made)
            self.at[name] = (at, size)
            at += size
            columns.append([m[name] + m[name][-1:] * (size - len(m[name])) for m in made])
        self.table = np.array([sum((c[n] for c in columns), []) for n in range(len(made))], np.int32)

    def plan(self, lengths, me):
        tile, owned, blocks, tiles = self.tile, self.owned, self.blocks, self.tiles
        ends = [int(e) for e in np.cumsum(lengths)]
        low = [max([e for e in ends if e <= t * tile], default=0) // tile for t in range(tiles)]
        last = [min(e for e in ends if e > t * tile) for t in range(tiles)]
        length = [e - max([f for f in ends if f < e], default=0) for e in last]
        cost = [t - low[t] + 1 for t in range(tiles)]
        homes = [[b * owned + t for t in range(owned)] for b in range(blocks)]
        works = [list(h) for h in homes]
        given = [[0], [0]]
        if self.count:
            options = list(itertools.combinations(range(owned), self.count))

            def apart(choice):
                a, b = choice
                gain = sum(cost[owned + t] for t in b) - sum(cost[t] for t in a)
                return abs(sum(cost[:owned]) - sum(cost[owned:]) + 2 * gain), -sum(a), sum(b)

            given = list(min(itertools.product(options, options), key=apart))
            for side in range(2):
                for t, u in zip(given[side], given[1 - side]):
                    works[side][t] = (1 - side) * owned + u
        own = works[me]
        slot = [own.index(t) if t in own else -1 for t in range(tiles)]
        loc = [((t // owned - me) % blocks) * owned + t % owned for t in range(tiles)]
        far = works[1 - me] if blocks == 2 else [t if t not in own else -1 for t in range(tiles)]
        pairs = [(i, j) for i in range(tiles) for j in range(low[i], i + 1)]
        forward = [(i, j) for i, j in pairs if slot[i] >= 0]
        backward, flags = [], []
        for j in range(tiles):
            mine = [(i, j) for i in reversed(range(j, tiles)) if slot[i] >= 0 and low[i] <= j]
            marks = [1] * len(mine)
            if not mine:
                mine, marks = [(j, j)], [0]
            marks[0] += 2
            marks[-1] += 4
            backward += mine
            flags += marks
        late = [(i, j) for i, j in forward if any(f > i and low[f] <= j for f in far)]
        return {
            "ends": ends,
            "length": length,
            "loc": loc,
            "slot": slot,
            "own": own,
            "own_at": [loc[t] for t in own],
            "slot_loc": [slot[loc.index(t)] for t in range(tiles)],
            "far": far,
            "given": list(given[me]) if self.count else [0],
            "taken": list(given[1 - me]) if self.count else [0],
            "all_n": [len(pairs)],
            "all_i": [i for i, _ in pairs],
            "all_j": [j for _, j in pairs],
            "fwd_i": [i for i, _ in forward],
            "fwd_j": [j for _, j in forward],
            "fwd_f": [1 + 2 * (j == low[i]) for i, j in forward] + [0],
            "bwd_i": [i for i, _ in backward],
            "bwd_j": [j for _, j in backward],
            "bwd_f": flags + [0],
            "late_n": [len(late)],
            "late_i": [i for i, _ in late] + [0],
            "late_j": [j for _, j in late] + [0],
        }

    def chosen(self, lengths, me):
        way = jnp.where(lengths[0] == LONG, 0, jnp.where(lengths[1] == LONG, 1, 2))
        return lax.dynamic_index_in_dim(jnp.array(self.table), way * self.blocks + me, 0, keepdims=False)

    def get(self, numbers, name, index):
        return numbers[self.at[name][0] + index]

    def part(self, numbers, name):
        at, size = self.at[name]
        return numbers[at : at + size]

    def size(self, name):
        return self.at[name][1]


def tile_marks(layout, numbers, i, j):
    tile = layout.tile
    row = lax.broadcasted_iota(jnp.int32, (tile, tile), 0)
    key = lax.broadcasted_iota(jnp.int32, (tile, tile), 1)
    if layout.aligned:
        apart = key - row
        ahead = jnp.where(i == j, 0, tile)
        length = jnp.full((1, 1), layout.get(numbers, "length", i), jnp.int32)
        return apart < ahead, apart <= ahead, 4.0 / length.astype(F32)
    places = i * tile + lax.broadcasted_iota(jnp.int32, (tile, 1), 0)
    start = jnp.zeros((tile, 1), jnp.int32)
    end = jnp.full((tile, 1), 2**30, jnp.int32)
    for n in range(layout.size("ends")):
        edge = layout.get(numbers, "ends", n)
        start = jnp.maximum(start, jnp.where(places >= edge, edge, 0))
        end = jnp.minimum(end, jnp.where(places < edge, edge, 2**30))
    inside = j * tile + key >= start
    apart = (j - i) * tile + key - row
    return inside & (apart < 0), inside & (apart <= 0), 4.0 / (end - start).astype(F32)


def head0_scores(q_pair, k_pair, tile):
    first, _ = half_masks(tile)
    return mm(jnp.where(first, q_pair, 0), k_pair, NT) * HEAD_DIM**-0.5


def before_sum(chosen, tile):
    rows = lax.broadcasted_iota(jnp.int32, (tile, tile), 0)
    cols = lax.broadcasted_iota(jnp.int32, (tile, tile), 1)
    lower = (cols < rows).astype(F32).astype(BF16)
    high, low = split2(chosen)
    above = mm(lower, high, NN) + mm(lower, low, NN)
    return above, above[tile - 1 :, :] + chosen[tile - 1 :, :]


def after_sum(values, tile):
    rows = lax.broadcasted_iota(jnp.int32, (tile, tile), 0)
    cols = lax.broadcasted_iota(jnp.int32, (tile, tile), 1)
    upper = (cols > rows).astype(F32).astype(BF16)
    high, low = split2(values)
    below = mm(upper, high, NN) + mm(upper, low, NN)
    return below, below[:1, :] + values[:1, :]


def project_kernel(x_ref, w_ref, gain_ref, *refs):
    q_ref, k_ref, v_ref, normed_ref, x_out_ref = refs[-5:]
    x_out_ref[0] = x_ref[0]
    width = x_ref.shape[2]
    normed = layer_norm(x_ref[0].astype(F32), gain_ref[...]).astype(BF16)
    normed_ref[0] = normed
    for part, ref in enumerate((q_ref, k_ref, v_ref)):
        ref[0] = mm(normed, w_ref[:, part * width : (part + 1) * width], NN).astype(BF16)


UNROLL = 4


def sums_kernel(layout, numbers, q_ref, k_ref, kept_ref, sums_ref, column):
    tile = layout.tile
    last = layout.size("all_i") - 1

    def group_step(group, carry):
        for n in range(UNROLL):
            at = jnp.minimum(group * UNROLL + n, last)
            i, j = layout.get(numbers, "all_i", at), layout.get(numbers, "all_j", at)
            at_i, at_j = layout.get(numbers, "loc", i), layout.get(numbers, "loc", j)
            strict, _, _ = tile_marks(layout, numbers, i, j)
            scores = head0_scores(q_ref[at_i], k_ref[at_j], tile)
            chosen = jnp.where(strict, jnp.maximum(scores, 0.0), 0.0)
            column[group * UNROLL + n] = jnp.sum(chosen, axis=0, keepdims=True)
        return carry

    count = layout.get(numbers, "all_n", 0)
    lax.fori_loop(0, lax.div(count + (UNROLL - 1), jnp.int32(UNROLL)), group_step, 0)
    sums_ref[...] = jnp.zeros_like(sums_ref)

    def add_step(n, carry):
        i, j = layout.get(numbers, "all_i", n), layout.get(numbers, "all_j", n)
        kept_ref[i, j] = sums_ref[j]
        sums_ref[j] += column[n]
        return carry

    lax.fori_loop(0, count, add_step, 0)


def forward_kernel(layout, numbers, q_ref, k_ref, v_ref, kept_ref, att_ref, inv_ref, acc, pen):
    tile = layout.tile
    step = pl.program_id(0)
    i, j = layout.get(numbers, "fwd_i", step), layout.get(numbers, "fwd_j", step)
    flag = layout.get(numbers, "fwd_f", step)
    halves = half_masks(tile)

    @pl.when((flag & 2) != 0)
    def _():
        acc[...] = jnp.zeros_like(acc)

    @pl.when((flag & 1) != 0)
    def _():
        def logits_of(head):
            pair, half = divmod(head, 2)
            at = slice(pair * PAIR, (pair + 1) * PAIR)
            return mm(jnp.where(halves[half], q_ref[0, :, at], 0), k_ref[0, :, at], NT)

        def gather(head, numer):
            pair, half = divmod(head, 2)
            at = slice(pair * PAIR, (pair + 1) * PAIR)
            acc[head] += mm(numer, jnp.where(halves[half], v_ref[0, :, at], 1), NN)

        raw = {head: logits_of(head) for head in range(3)}
        strict, allowed, rate = tile_marks(layout, numbers, i, j)
        chosen = jnp.where(strict, jnp.maximum(raw[0] * HEAD_DIM**-0.5, 0.0), 0.0)
        above, _ = before_sum(chosen, tile)
        pen[...] = jnp.where(allowed, (rate * LOG2E) * (kept_ref[i, j] + above), FAR)
        waiting = {}
        for head in range(HEADS + 2):
            if 3 <= head + 3 < HEADS:
                raw[head + 3] = logits_of(head + 3)
            if head < HEADS:
                waiting[head] = jnp.exp2(raw.pop(head) * (HEAD_DIM**-0.5 * LOG2E) - pen[...]).astype(BF16)
            if head >= 2:
                gather(head - 2, waiting.pop(head - 2))

        @pl.when(i == j)
        def _():
            for pair in range(PAIRS):
                at = slice(pair * PAIR, (pair + 1) * PAIR)
                low, high = acc[2 * pair], acc[2 * pair + 1]
                numer = jnp.where(halves[0], low, high)
                inverse = 1.0 / pltpu.roll(jnp.where(halves[0], high, low), HEAD_DIM, 1)
                att_ref[0, :, at] = numer * inverse
                inv_ref[0, :, at] = inverse


def middle_kernel(
    tile, owned, chunk,
    numbers, att_ref, inv_ref, x_ref, cot_ref, wo_ref, wu_ref, wd_ref, gain_ref,
    out_ref, branch_ref, dx_ref, grads_ref,
    hid_s, dpre_s, low_s, normed_s, branch_s, stage_down, stage_rest, sems,
):
    step = pl.program_id(0)
    width = x_ref.shape[2]
    hid = wu_ref.shape[1]
    parts = hid // width
    joined = len(stage_rest.shape) == 4

    def shipment(n):
        source = stage_down.at[n] if n < parts else stage_rest.at[n - parts]
        if not joined:
            target = grads_ref.at[n]
        elif n < parts:
            some, long = stage_down.shape[1:3]
            target = grads_ref.at[pl.ds(n * some, some), pl.ds(0, long), :]
        else:
            share = stage_rest.shape[2]
            target = grads_ref.at[:, pl.ds(share * n, share), :]
        return pltpu.make_async_copy(source, target, sems.at[n])

    def ship(n, block):
        stage, at = (stage_down, n) if n < parts else (stage_rest, n - parts)
        stage[at] = block.astype(BF16).reshape(stage.shape[1:])
        shipment(n).start()

    @pl.when(step < owned)
    def _():
        at = pl.ds(pl.multiple_of(step * tile, tile), tile)
        attended = att_ref[0]
        cot = cot_ref[at, :]
        gain = gain_ref[...]
        low = attended.astype(BF16)
        low_s[at, :] = low
        residual = x_ref[0].astype(F32) + mm(low, wo_ref[...], NN)
        centre = jnp.mean(residual, axis=1, keepdims=True)
        shifted = residual - centre
        scale = lax.rsqrt(jnp.mean(shifted * shifted, axis=1, keepdims=True) + LN_EPS)
        xhat = shifted * scale
        normed = (xhat * gain).astype(BF16)
        normed_s[at, :] = normed
        result = residual
        d_normed = jnp.zeros((tile, width), F32)
        for c in range(hid // chunk):
            cols = slice(c * chunk, (c + 1) * chunk)
            pre = mm(normed, wu_ref[:, cols], NN)
            square = pre * pre
            wave = jnp.tanh(pre * (GELU_C + (GELU_C * 0.044715) * square))
            rising = 0.5 + 0.5 * wave
            hidden = (pre * rising).astype(BF16)
            bend = pre * ((0.5 * GELU_C) + (1.5 * GELU_C * 0.044715) * square)
            d_pre = (mm(cot, wd_ref[cols, :], NT) * (rising + bend * (1.0 - wave * wave))).astype(BF16)
            hid_s[at, cols] = hidden
            dpre_s[at, cols] = d_pre
            result = result + mm(hidden, wd_ref[cols, :], NN)
            d_normed = d_normed + mm(d_pre, wu_ref[:, cols], NT)
        out_ref[0] = result.astype(BF16)
        grown = d_normed * gain
        mean_grown = jnp.mean(grown, axis=1, keepdims=True)
        mean_both = jnp.mean(grown * xhat, axis=1, keepdims=True)
        branch = (cot.astype(F32) + scale * (grown - mean_grown - xhat * mean_both)).astype(BF16)
        branch_ref[0] = branch
        branch_s[at, :] = branch
        d_attended = mm(branch, wo_ref[...], NT).astype(BF16).astype(F32)
        scaled = (d_attended * inv_ref[0]).astype(BF16)
        product = scaled.astype(F32) * attended
        rows = lax.broadcasted_iota(jnp.int32, (PAIR, 2 * PAIR), 0)
        cols = lax.broadcasted_iota(jnp.int32, (PAIR, 2 * PAIR), 1)
        block = cols // HEAD_DIM
        spread = jnp.where(block == jnp.where(rows < HEAD_DIM, 1, 2), -1.0, 0.0).astype(BF16)
        lane = lax.broadcasted_iota(jnp.int32, (tile, 2 * PAIR), 1) % HEAD_DIM
        first, _ = half_masks(tile)
        for pair in range(PAIRS):
            here = slice(pair * PAIR, (pair + 1) * PAIR)
            high, rest = split2(product[:, here])
            minus_dot = mm(high, spread, NN) + mm(rest, spread, NN)
            dot_high, dot_low = split2(minus_dot)
            side = jnp.where(lane == 0, dot_high, jnp.where(lane == 1, dot_low, 0))
            mine = scaled[:, here]
            base = 2 * pair * PAIR
            dx_ref[0, :, base : base + PAIR] = jnp.where(first, mine, side[:, :PAIR])
            dx_ref[0, :, base + PAIR : base + 2 * PAIR] = jnp.where(first, side[:, PAIR:], mine)

    for c in range(parts):
        @pl.when(step == owned + c)
        def _(c=c):
            cols = slice(c * width, (c + 1) * width)
            ship(c, mm(hid_s[:, cols], cot_ref[...], TN))
            ship(parts + c, mm(normed_s[...], dpre_s[:, cols], TN))
            if c == parts - 1:
                ship(2 * parts, mm(low_s[...], branch_s[...], TN))
                for n in range(2 * parts + 1):
                    shipment(n).wait()


def backward_kernel(
    layout, numbers, q_ref, k_ref, v_ref, dx_ref, kept_ref,
    dq_ref, dk_ref, dv_ref, later_ref,
    acc_q, acc_k, acc_v, pen, dpen, later,
):
    tile = layout.tile
    step = pl.program_id(0)
    i, j = layout.get(numbers, "bwd_i", step), layout.get(numbers, "bwd_j", step)
    flag = layout.get(numbers, "bwd_f", step)
    halves = half_masks(tile)

    @pl.when(step == 0)
    def _():
        acc_q[...] = jnp.zeros_like(acc_q)
        later_ref[...] = jnp.zeros_like(later_ref)

    @pl.when((flag & 2) != 0)
    def _():
        acc_k[...] = jnp.zeros_like(acc_k)
        acc_v[...] = jnp.zeros_like(acc_v)
        later[...] = jnp.zeros_like(later)

    @pl.when((flag & 1) != 0)
    def _():
        slot = layout.get(numbers, "slot", i)
        scores0 = head0_scores(q_ref[0, :, :PAIR], k_ref[0, :, :PAIR], tile)

        def products(pair):
            at = slice(pair * PAIR, (pair + 1) * PAIR)
            k_pair, q_pair, v_pair = k_ref[0, :, at], q_ref[0, :, at], v_ref[0, :, at]
            made = []
            for half in range(2):
                head = 2 * pair + half
                scores = scores0 if head == 0 else mm(jnp.where(halves[half], q_pair, 0), k_pair, NT) * HEAD_DIM**-0.5
                dx = dx_ref[0, :, head * PAIR : (head + 1) * PAIR]
                made.append((scores, mm(dx, jnp.where(halves[half], v_pair, 1), NT)))
            return made

        made = {PAIRS - 1: products(PAIRS - 1)}
        ready = {}
        strict, allowed, rate = tile_marks(layout, numbers, i, j)
        chosen = jnp.where(strict, jnp.maximum(scores0, 0.0), 0.0)
        above, _ = before_sum(chosen, tile)
        pen[...] = jnp.where(allowed, (rate * LOG2E) * (kept_ref[i, j] + above), FAR)

        def pointwise(pair, made):
            grads, weights = [], []
            for scores, d_probs in made:
                numer = jnp.exp2(scores * LOG2E - pen[...])
                weights.append(numer.astype(BF16))
                grads.append(numer * d_probs)
            both = grads[0] + grads[1]
            if pair == PAIRS - 1:
                dpen[...] = both
            elif pair > 0:
                dpen[...] += both
            else:
                below, total = after_sum(dpen[...] + both, tile)
                picked = strict & (scores0 > 0.0)
                grads[0] = grads[0] + jnp.where(picked, -rate * (later[...] + below), 0.0)
                later[...] = later[...] + total
                later_ref[slot, j] = total
            return weights, [g.astype(BF16) for g in grads]

        def collect(pair, weights, lows):
            at = slice(pair * PAIR, (pair + 1) * PAIR)
            k_pair, q_pair = k_ref[0, :, at], q_ref[0, :, at]
            d_q = None
            for half in range(2):
                head = 2 * pair + half
                part = slice(half * HEAD_DIM, (half + 1) * HEAD_DIM)
                head_at = slice(head * HEAD_DIM, (head + 1) * HEAD_DIM)
                dx = dx_ref[0, :, head * PAIR : (head + 1) * PAIR]
                acc_v[head_at, :] += mm(dx, weights[half], TN)[part]
                acc_k[head_at, :] += mm(q_pair, lows[half], TN)[part]
                more = mm(lows[half], jnp.where(halves[half], k_pair, 0), NN)
                d_q = more if d_q is None else d_q + more
            acc_q[slot, :, at] += d_q

        for pair in range(PAIRS - 1, -2, -1):
            if pair > 0:
                made[pair - 1] = products(pair - 1)
            if pair >= 0:
                ready[pair] = pointwise(pair, made.pop(pair))
            if pair + 1 in ready:
                collect(pair + 1, *ready.pop(pair + 1))

    @pl.when((flag & 4) != 0)
    def _():
        dk_ref[0] = jnp.transpose((acc_k[...] * HEAD_DIM**-0.5).astype(BF16))
        dv_ref[0] = jnp.transpose(acc_v[...].astype(BF16))

    @pl.when(step == pl.num_programs(0) - 1)
    def _():
        for slot in range(acc_q.shape[0]):
            dq_ref[slot] = (acc_q[slot] * HEAD_DIM**-0.5).astype(BF16)


def late_kernel(
    layout, numbers, q_ref, k_ref, far_totals_ref, dq_in_ref, dk_in_ref,
    dq_ref, dk_ref,
    acc_q, acc_k,
):
    tile = layout.tile
    first, _ = half_masks(tile)
    acc_q[...] = jnp.zeros_like(acc_q)
    acc_k[...] = jnp.zeros_like(acc_k)
    count = layout.get(numbers, "late_n", 0)

    def group_step(group, carry):
        adds = []
        for n in range(UNROLL):
            at = group * UNROLL + n
            valid = at < count
            at = jnp.minimum(at, layout.size("late_i") - 1)
            i, j = layout.get(numbers, "late_i", at), layout.get(numbers, "late_j", at)
            slot, at_i, at_j = (layout.get(numbers, name, t) for name, t in (("slot", i), ("loc", i), ("loc", j)))
            slot = jnp.maximum(slot, 0)
            later = jnp.zeros((1, tile), F32)
            for f in range(layout.size("far")):
                later += jnp.where(valid & (layout.get(numbers, "far", f) > i), far_totals_ref[f, j], 0.0)
            strict, _, rate = tile_marks(layout, numbers, i, j)
            scores = head0_scores(q_ref[at_i], k_ref[at_j], tile)
            factor = (-(HEAD_DIM**-0.5) * rate) * later
            d_low = jnp.where(strict & (scores > 0.0), factor, 0.0).astype(BF16)
            adds.append((slot, at_j, mm(q_ref[at_i], d_low, TN), mm(d_low, k_ref[at_j], NN)))
        for slot, at_j, for_k, for_q in adds:
            acc_k[at_j] += for_k
            acc_q[slot] += for_q
        return carry

    lax.fori_loop(0, lax.div(count + (UNROLL - 1), jnp.int32(UNROLL)), group_step, 0)
    for slot in range(acc_q.shape[0]):
        dq_ref[slot] = (dq_in_ref[slot].astype(F32) + jnp.where(first, acc_q[slot], 0.0)).astype(BF16)

    def finish(t, carry):
        dk_ref[t] = (dk_in_ref[t].astype(F32) + jnp.where(first, jnp.transpose(acc_k[t]), 0.0)).astype(BF16)
        return carry

    lax.fori_loop(0, acc_k.shape[0], finish, 0)


def through_weight(layout, base, numbers, dq_ref, dk_ref, dv_ref, w_ref):
    width = dq_ref.shape[2]
    slot = layout.get(numbers, "slot_loc", base + pl.program_id(0))
    d_query = jnp.where(slot >= 0, dq_ref[0], jnp.zeros_like(dq_ref[0]))
    return (
        mm(dv_ref[0], w_ref[:, 2 * width :], NT)
        + mm(dk_ref[0], w_ref[:, width : 2 * width], NT)
        + mm(d_query, w_ref[:, :width], NT)
    )


def away_kernel(layout, base, numbers, dq_ref, dk_ref, dv_ref, w_ref, out_ref):
    out_ref[0] = through_weight(layout, base, numbers, dq_ref, dk_ref, dv_ref, w_ref).astype(BF16)


def home_kernel(layout, numbers, dq_ref, dk_ref, dv_ref, w_ref, back_ref, x_ref, branch_ref, gain_ref, out_ref):
    values = x_ref[0].astype(F32)
    shifted = values - jnp.mean(values, axis=1, keepdims=True)
    scale = lax.rsqrt(jnp.mean(shifted * shifted, axis=1, keepdims=True) + LN_EPS)
    xhat = shifted * scale
    d_normed = through_weight(layout, 0, numbers, dq_ref, dk_ref, dv_ref, w_ref)
    grown = (d_normed + back_ref[0].astype(F32)) * gain_ref[...]
    mean_grown = jnp.mean(grown, axis=1, keepdims=True)
    mean_both = jnp.mean(grown * xhat, axis=1, keepdims=True)
    dx = scale * (grown - mean_grown - xhat * mean_both)
    out_ref[0] = (branch_ref[0].astype(F32) + dx).astype(BF16)


def flat(ref, cols):
    block = ref[:, :, cols]
    return block.reshape(block.shape[0] * block.shape[1], block.shape[2])


def value_weight_kernel(normed_ref, dk_ref, dv_ref, out_ref):
    width = normed_ref.shape[2]
    half = width // 2
    normed = flat(normed_ref, slice(None))
    out_ref[:, :half] = mm(normed, flat(dk_ref, slice(half, width)), TN).astype(BF16)
    out_ref[:, half:] = mm(normed, flat(dv_ref, slice(None)), TN).astype(BF16)


def query_weight_kernel(layout, numbers, normed_ref, dq_ref, dk_ref, out_ref):
    width = normed_ref.shape[2]
    half = width // 2
    total = jnp.zeros((width, width), F32)
    for slot in range(layout.owned):
        total += mm(normed_ref[layout.get(numbers, "own_at", slot)], dq_ref[slot], TN)
    out_ref[:, :width] = total.astype(BF16)
    out_ref[:, width:] = mm(flat(normed_ref, slice(None)), flat(dk_ref, slice(0, half)), TN).astype(BF16)


SMEM = pl.BlockSpec(memory_space=pltpu.SMEM)
VMEM = pl.BlockSpec(memory_space=pltpu.VMEM)


def estimate(flops):
    flops = int(flops)
    return pl.CostEstimate(flops=flops, bytes_accessed=flops // 600, transcendentals=0)


def held(shape):
    return pl.BlockSpec(shape, lambda *_: (0,) * len(shape), pipeline_mode=pl.Buffered(1))


def fixed(shape):
    return pl.BlockSpec(shape, lambda *_: (0,) * len(shape))


def in_hbm(shape, dtype):
    return pltpu.HBM(shape, dtype)


def stay(*arrays):
    return tuple(pltpu.with_memory_space_constraint(a, pltpu.HBM) for a in arrays)


def sds(shape, dtype):
    return jax.ShapeDtypeStruct(shape, dtype)


def project(x, weight, gain, tiles, first, into):
    owned, tile, width = x.shape
    outs = (sds((tiles, tile, width), BF16),) * 2 + (in_hbm((tiles, tile, width), BF16),) * 3
    row = pl.BlockSpec((1, tile, width), lambda s: (s, 0, 0))
    placed = pl.BlockSpec((1, tile, width), lambda s: (s + first, 0, 0))
    extra = [pl.BlockSpec(memory_space=pl.ANY)] * len(into)
    return pl.pallas_call(
        project_kernel,
        grid=(owned,),
        out_shape=outs,
        in_specs=[row, held(weight.shape), held(gain.shape)] + extra,
        out_specs=(placed,) * 5,
        input_output_aliases={3 + n: n for n in range(len(into))},
        compiler_params=pltpu.CompilerParams(vmem_limit_bytes=20 * 2**20),
        cost_estimate=estimate(2 * owned * tile * width * weight.shape[1]),
    )(x, weight, gain, *into)


def middle(layout, numbers, attended, inverse, x, cot, wo, wu, wd, gain, dp_count):
    owned, tile, width = attended.shape
    hid = wu.shape[1]
    parts = hid // width
    rows = owned * tile
    row = pl.BlockSpec((1, tile, width), lambda s, n: (jnp.minimum(s, owned - 1), 0, 0))
    wide = pl.BlockSpec((1, tile, 2 * width), lambda s, n: (jnp.minimum(s, owned - 1), 0, 0))

    def token_place(s, n):
        return layout.get(n, "own_at", jnp.minimum(s, owned - 1)), 0, 0

    share = width // dp_count
    joined = share % 16 == 0 and dp_count % parts == 0
    if joined:
        stage_down = (parts, dp_count // parts, share * parts, width)
        stage_rest = (parts + 1, dp_count, share, width)
        grads = (dp_count, share * (2 * parts + 1), width)
    else:
        stage_down, stage_rest, grads = ((n, width, width) for n in (parts, parts + 1, 2 * parts + 1))
    return kernel_call(
        functools.partial(middle_kernel, tile, owned, width), VMEM_LIMIT // 2**20, (owned + parts,), numbers,
        (attended, inverse, x, cot, wo, wu, wd, gain),
        [
            row, row, pl.BlockSpec((1, tile, width), token_place), held((rows, width)),
            held(wo.shape), held(wu.shape), held(wd.shape), held(gain.shape),
        ],
        (
            sds((owned, tile, width), BF16),
            sds((owned, tile, width), BF16),
            sds((owned, tile, 2 * width), BF16),
            sds(grads, BF16),
        ),
        (row, row, wide, pl.BlockSpec(memory_space=pl.ANY)),
        [
            pltpu.VMEM((rows, hid), BF16),
            pltpu.VMEM((rows, hid), BF16),
            pltpu.VMEM((rows, width), BF16),
            pltpu.VMEM((rows, width), BF16),
            pltpu.VMEM((rows, width), BF16),
            pltpu.VMEM(stage_down, BF16),
            pltpu.VMEM(stage_rest, BF16),
            pltpu.SemaphoreType.DMA((2 * parts + 1,)),
        ],
        2 * rows * width * (3 * width + 6 * hid),
    )


def kernel_call(kernel, room, grid, numbers, operands, in_specs, outs, out_specs, scratch, flops, aliases=None):
    return pl.pallas_call(
        kernel,
        grid_spec=pltpu.PrefetchScalarGridSpec(
            num_scalar_prefetch=1, grid=grid, in_specs=in_specs, out_specs=out_specs, scratch_shapes=scratch
        ),
        out_shape=outs,
        input_output_aliases=aliases or {},
        compiler_params=pltpu.CompilerParams(vmem_limit_bytes=room * 2**20),
        cost_estimate=estimate(flops),
    )(numbers, *operands)


def run_sums(layout, numbers, q, k):
    tiles, tile, _ = q.shape
    every = pl.BlockSpec((tiles, tile, PAIR), lambda n, x: (0, 0, 0))
    kept, sums = (tiles, tiles, 1, tile), (tiles, 1, tile)
    groups = -(-layout.size("all_i") // UNROLL) * UNROLL
    return kernel_call(
        functools.partial(sums_kernel, layout), 20, (1,), numbers, (q, k), [every, every],
        (sds(kept, F32), sds(sums, F32)), (fixed(kept), fixed(sums)),
        [pltpu.VMEM((groups, 1, tile), F32)], tiles * tiles * tile * tile * PAIR,
    )


def run_forward(layout, numbers, q, k, v, kept):
    tiles, tile, width = q.shape
    get, owned = layout.get, layout.owned
    rows = pl.BlockSpec((1, tile, width), lambda n, x: (get(x, "loc", get(x, "fwd_i", n)), 0, 0))
    keys = pl.BlockSpec((1, tile, width), lambda n, x: (get(x, "loc", get(x, "fwd_j", n)), 0, 0))
    slots = pl.BlockSpec((1, tile, width), lambda n, x: (get(x, "slot", get(x, "fwd_i", n)), 0, 0))
    return kernel_call(
        functools.partial(forward_kernel, layout), 20, (layout.size("fwd_i"),), numbers,
        (q, k, v, kept), [rows, keys, keys, fixed(kept.shape)],
        (in_hbm((owned, tile, width), F32),) * 2, (slots, slots),
        [pltpu.VMEM((HEADS, tile, PAIR), F32), pltpu.VMEM((tile, tile), F32)],
        4 * layout.size("fwd_i") * tile * tile * width,
    )


def run_backward(layout, numbers, q, k, v, dx, kept):
    tiles, tile, width = q.shape
    get, owned = layout.get, layout.owned
    rows = pl.BlockSpec((1, tile, width), lambda n, x: (get(x, "loc", get(x, "bwd_i", n)), 0, 0))
    keys = pl.BlockSpec((1, tile, width), lambda n, x: (get(x, "loc", get(x, "bwd_j", n)), 0, 0))
    slots = pl.BlockSpec(
        (1, tile, 2 * width), lambda n, x: (jnp.maximum(get(x, "slot", get(x, "bwd_i", n)), 0), 0, 0)
    )
    totals = (owned, tiles, 1, tile)
    return kernel_call(
        functools.partial(backward_kernel, layout), 28, (layout.size("bwd_i"),), numbers,
        (*stay(q, k, v), dx, kept), [rows, keys, keys, slots, fixed(kept.shape)],
        (
            sds((owned, tile, width), BF16),
            sds((tiles, tile, width), BF16),
            sds((tiles, tile, width), BF16),
            sds(totals, F32),
        ),
        (fixed((owned, tile, width)), keys, keys, fixed(totals)),
        [
            pltpu.VMEM((owned, tile, width), F32),
            pltpu.VMEM((width, tile), F32),
            pltpu.VMEM((width, tile), F32),
            pltpu.VMEM((tile, tile), F32),
            pltpu.VMEM((tile, tile), F32),
            pltpu.VMEM((1, tile), F32),
        ],
        10 * layout.size("bwd_i") * tile * tile * width,
    )


def run_late(layout, numbers, q, k, far_totals, dq, dk):
    tiles, tile, _ = q.shape
    owned = dq.shape[0]
    some = pl.BlockSpec((owned, tile, PAIR), lambda n, x: (0, 0, 0))
    every = pl.BlockSpec((tiles, tile, PAIR), lambda n, x: (0, 0, 0))
    return kernel_call(
        functools.partial(late_kernel, layout), 16, (1,), numbers,
        (q, k, far_totals, dq, dk), [every, every, fixed(far_totals.shape), some, every],
        (sds(dq.shape, BF16), sds(dk.shape, BF16)), (some, every),
        [pltpu.VMEM((owned, tile, PAIR), F32), pltpu.VMEM((tiles, PAIR, tile), F32)],
        6 * layout.size("late_i") * tile * tile * PAIR,
        {4: 0, 5: 1},
    )


def tile_specs(layout, base, width):
    tile = layout.tile
    row = pl.BlockSpec((1, tile, width), lambda s, x: (s, 0, 0))
    placed = pl.BlockSpec((1, tile, width), lambda s, x: (base + s, 0, 0))
    picked = pl.BlockSpec((1, tile, width), lambda s, x: (jnp.maximum(layout.get(x, "slot_loc", base + s), 0), 0, 0))
    return row, placed, picked


def run_away(layout, numbers, dq, dk, dv, weight):
    width, count, base = dq.shape[2], layout.tiles - layout.owned, layout.owned
    row, placed, picked = tile_specs(layout, base, width)
    return kernel_call(
        functools.partial(away_kernel, layout, base), 20, (count,), numbers, (dq, dk, dv, weight),
        [picked, placed, placed, held(weight.shape)], sds((count, layout.tile, width), BF16), row,
        [], 2 * count * layout.tile * width * weight.shape[1],
    )


def run_home(layout, numbers, dq, dk, dv, weight, back, x, branch, gain):
    width = dq.shape[2]
    row, placed, picked = tile_specs(layout, 0, width)
    return kernel_call(
        functools.partial(home_kernel, layout), 56, (layout.owned,), numbers,
        (dq, dk, dv, weight, back, x, branch, gain),
        [picked, placed, placed, held(weight.shape), row, row, row, held(gain.shape)],
        sds(x.shape, BF16), row, [], 2 * x.shape[0] * layout.tile * width * weight.shape[1],
    )


def value_weight_grad(normed, dk, dv):
    width = normed.shape[2]
    return pl.pallas_call(
        value_weight_kernel,
        out_shape=sds((width, 3 * width // 2), BF16),
        in_specs=[VMEM] * 3,
        out_specs=VMEM,
        compiler_params=pltpu.CompilerParams(vmem_limit_bytes=30 * 2**20),
        cost_estimate=estimate(3 * normed.shape[0] * normed.shape[1] * width * width),
    )(normed, dk, dv)


def query_weight_grad(layout, numbers, normed, dq, dk):
    width = normed.shape[2]
    return pl.pallas_call(
        functools.partial(query_weight_kernel, layout),
        out_shape=sds((width, 3 * width // 2), BF16),
        in_specs=[SMEM, VMEM, VMEM, VMEM],
        out_specs=VMEM,
        compiler_params=pltpu.CompilerParams(vmem_limit_bytes=28 * 2**20),
        cost_estimate=estimate(2 * normed.shape[0] * normed.shape[1] * width * width),
    )(numbers, normed, dq, dk)


def swap_seq(array):
    return lax.ppermute(array, "seq", [(0, 1), (1, 0)])


def powers(size):
    return [1 << n for n in range(size.bit_length() - 1)]


def is_power(size):
    return size & (size - 1) == 0


def scatter_halving(grad, order):
    count = lax.axis_size("dp")
    index = lax.axis_index("dp")
    bits = len(powers(count))
    held_bits = list(range(bits))[::-1]
    parts = grad.reshape((2,) * bits + grad.shape[1:])
    for n in order:
        axis = held_bits.index(n)
        held_bits.remove(n)
        mine = (index >> n) & 1
        keep = lax.dynamic_index_in_dim(parts, mine, axis, keepdims=False)
        send = lax.dynamic_index_in_dim(parts, 1 - mine, axis, keepdims=False)
        got = lax.ppermute(send, "dp", [(i, i ^ (1 << n)) for i in range(count)])
        parts = (keep.astype(F32) + got.astype(F32)).astype(BF16)
    return parts


def on_device(
    tokens, cotangent, lengths, threshold, attn_gain, qkv_weight, out_weight, mlp_gain, up_weight, down_weight
):
    _, block_len, width = tokens.shape
    blocks = lax.axis_size("seq")
    dp_count = lax.axis_size("dp")
    me = lax.axis_index("seq")
    tile = pick_tile(block_len)
    owned = block_len // tile
    tiles = owned * blocks
    rows = blocks * block_len
    hid = up_weight.shape[1]
    token_own = tokens[0]
    cot_own = cotangent[0]
    attn_gain = attn_gain.reshape(1, width)
    mlp_gain = mlp_gain.reshape(1, width)
    by_tile = (owned, tile, width)

    layout = Layout(rows, lengths.shape[1], tile, owned, blocks)
    count = layout.count
    numbers = layout.chosen(lengths[0], me)
    given = layout.part(numbers, "given")

    def put(array, pieces):
        for n in range(count):
            array = lax.dynamic_update_slice_in_dim(array, pieces[n][None], given[n], 0)
        return array

    def swap_tiles(array):
        if count == 0:
            return array
        sent = jnp.stack([lax.dynamic_index_in_dim(array, given[n], 0, False) for n in range(count)])
        return put(array, swap_seq(sent))

    x_own = token_own.reshape(by_tile)
    if blocks == 2:
        x_others = swap_seq(token_own).reshape(by_tile)
    else:
        gathered = lax.all_gather(token_own, "seq", axis=0, tiled=False)
        x_others = jnp.roll(gathered, -me, axis=0)[1:].reshape(tiles - owned, tile, width)
    cot_tiles, x_others = lax.optimization_barrier((cot_own.reshape(by_tile), x_others))
    cot = swap_tiles(cot_tiles).reshape(block_len, width)
    parts = project(x_own, qkv_weight, attn_gain, tiles, 0, ())
    q_all, k_all, v_all, normed_all, x_all = project(x_others, qkv_weight, attn_gain, tiles, owned, parts)

    kept, sums = run_sums(layout, numbers, q_all, k_all)
    attended, inverse = run_forward(layout, numbers, q_all, k_all, v_all, kept)
    limit = threshold[0].astype(F32) / 1024.0
    ends = jnp.cumsum(lengths[0])
    positions = jnp.arange(rows, dtype=jnp.int32)
    passed = positions[:, None] >= ends[None, :]
    start = jnp.max(jnp.where(passed, ends[None, :], 0), axis=1)
    end = jnp.min(jnp.where(passed, rows, ends[None, :]), axis=1)
    over = jnp.maximum(4.0 / (end - start).astype(F32) * sums.reshape(rows) - limit, 0.0)
    excess = jnp.full((1, 128), jnp.sum(jnp.where(positions // block_len == me, over, 0.0)))
    hops = [("dp", bit) for bit in powers(dp_count)] + [("seq", bit) for bit in powers(blocks)]
    if not (is_power(dp_count) and is_power(blocks)):
        excess, hops = lax.psum(excess, ("seq", "dp")), []

    def hop_beside(excess, result):
        if hops:
            axis, bit = hops.pop(0)
            excess += lax.ppermute(excess, axis, [(i, i ^ bit) for i in range(lax.axis_size(axis))])
        return lax.optimization_barrier((excess, result))

    excess, attended = hop_beside(excess, attended)

    out_c, branch_c, dx, early_grads = middle(
        layout, numbers, attended, inverse, x_all, cot, out_weight, up_weight, down_weight, mlp_gain, dp_count
    )
    excess, dx = hop_beside(excess, dx)
    output = swap_tiles(out_c)
    branch = swap_tiles(branch_c)
    parts_hid = hid // width
    if early_grads.shape[0] != dp_count or early_grads.ndim != 3 or early_grads.shape[1] == width:
        down_grad = early_grads[:parts_hid].reshape(dp_count, -1, width)
        rest = early_grads[parts_hid:].reshape(parts_hid + 1, dp_count, -1, width).transpose(1, 0, 2, 3)
        early_grads = jnp.concatenate([down_grad, rest.reshape(dp_count, -1, width)], axis=1)
    early = lax.psum_scatter(early_grads, "dp", scatter_dimension=0, tiled=False)

    dq, dk, dv, totals = run_backward(layout, numbers, q_all, k_all, v_all, dx, kept)
    excess, (dk, dv, output, branch) = hop_beside(excess, (dk, dv, output, branch))
    if blocks == 2:
        far_totals = swap_seq(totals)
    else:
        far_totals = lax.all_gather(totals, "seq", axis=0, tiled=True)
    value_grad = value_weight_grad(normed_all, dk, dv)
    excess, far_totals = hop_beside(excess, far_totals)
    dq, dk = run_late(layout, numbers, q_all, k_all, far_totals, dq, dk)

    away = run_away(layout, numbers, dq, dk, dv, qkv_weight)
    if blocks == 2:
        back = swap_seq(away)
    else:
        by_block = jnp.concatenate([jnp.zeros((owned, tile, width), BF16), away]).reshape(blocks, block_len, width)
        back = lax.psum_scatter(jnp.roll(by_block, me, axis=0), "seq", scatter_dimension=0, tiled=False)
        back = back.reshape(by_tile)
    away, dq, dk = lax.optimization_barrier((away, dq, dk))
    excess, dq = hop_beside(excess, dq)
    query_grad = query_weight_grad(layout, numbers, normed_all, dq, dk)
    def over_seq(piece):
        if blocks == 2:
            return piece.astype(F32) + swap_seq(piece).astype(F32)
        return lax.psum(piece, "seq").astype(F32)

    halves = [grad.reshape(dp_count, -1, 3 * width // 2) for grad in (query_grad, value_grad)]
    if is_power(dp_count) and dp_count > 1:
        bits = list(range(len(powers(dp_count))))
        halves = [scatter_halving(halves[0], bits), scatter_halving(halves[1], bits[:1] + bits[2:] + bits[1:2])]
    else:
        halves = [lax.psum_scatter(grad, "dp", scatter_dimension=0, tiled=False) for grad in halves]
    late = jnp.concatenate(halves, axis=1)
    _, late, early = lax.optimization_barrier((back, late, early))
    qkv_piece = over_seq(late)
    early = over_seq(early)
    input_grad = run_home(layout, numbers, dq, dk, dv, qkv_weight, back, x_own, branch, attn_gain)

    part = width // dp_count
    n_down = hid // dp_count
    down_piece = early[:n_down]
    up_piece = early[n_down : 2 * n_down].reshape(hid // width, part, width).transpose(1, 0, 2).reshape(part, hid)
    out_piece = early[2 * n_down :]
    at = lax.axis_index("dp") * part

    def gain_grad(weight, weight_grad, gain):
        mine = lax.dynamic_slice_in_dim(weight, at, part).astype(F32)
        return jnp.sum(mine * weight_grad, axis=1) / lax.dynamic_slice_in_dim(gain[0], at, part)

    attn_piece = gain_grad(qkv_weight, qkv_piece, attn_gain)
    mlp_piece = gain_grad(up_weight, up_piece, mlp_gain)
    while hops:
        excess, _ = hop_beside(excess, excess)
    excess = excess[0, :1] / (dp_count * rows)
    return (
        output.reshape(1, block_len, width),
        input_grad.reshape(1, block_len, width),
        attn_piece,
        qkv_piece,
        out_piece,
        mlp_piece,
        up_piece,
        down_piece,
        excess,
    )


def solution(mesh):
    return jax.shard_map(
        on_device,
        mesh=mesh,
        in_specs=(
            P("dp", "seq", None),
            P("dp", "seq", None),
            P("dp", None),
            P(),
            P(),
            P(),
            P(),
            P(),
            P(),
            P(),
        ),
        out_specs=(
            P("dp", "seq", None),
            P("dp", "seq", None),
            P("dp"),
            P("dp", None),
            P("dp", None),
            P("dp"),
            P("dp", None),
            P("dp", None),
            P(),
        ),
        check_vma=False,
    )
```

```python
import functools
import itertools

import jax
import jax.numpy as jnp
import numpy as np
from jax import lax
from jax.experimental import pallas as pl
from jax.experimental.pallas import tpu as pltpu
from jax.sharding import PartitionSpec as P

HEADS = 12
HEAD_DIM = 64
PAIRS = HEADS // 2
PAIR = 2 * HEAD_DIM

LONG = 2048
SHORT = 512

LN_EPS = 1e-05
GELU_C = 0.7978845608028654
LOG2E = 1.4426950408889634
FAR = 1e30
VMEM_LIMIT = 60 * 2**20

BF16 = jnp.bfloat16
F32 = jnp.float32
NN = (((1,), (0,)), ((), ()))
NT = (((1,), (1,)), ((), ()))
TN = (((0,), (0,)), ((), ()))


def mm(left, right, dims):
    return lax.dot_general(left, right, dims, preferred_element_type=F32)


def pick_tile(block_len):
    return 256 if block_len % 256 == 0 else block_len


def layer_norm(values, gain):
    centre = jnp.mean(values, axis=-1, keepdims=True)
    shifted = values - centre
    spread = jnp.mean(shifted * shifted, axis=-1, keepdims=True)
    return shifted * lax.rsqrt(spread + LN_EPS) * gain


def gelu_tanh(values):
    return 0.5 * values * (1.0 + jnp.tanh(GELU_C * (values + 0.044715 * values * values * values)))


def split2(values):
    high = values.astype(BF16)
    return high, (values - high.astype(F32)).astype(BF16)


def half_masks(rows):
    lane = lax.broadcasted_iota(jnp.int32, (rows, PAIR), 1)
    return (lane < HEAD_DIM, lane >= HEAD_DIM)


class Layout:
    def __init__(self, rows, slots, tile, owned, blocks):
        self.tile, self.owned, self.blocks, self.tiles = tile, owned, blocks, owned * blocks
        self.aligned = SHORT % tile == 0
        self.count = 2 if blocks == 2 and owned >= 4 else 0
        ways = [[LONG, SHORT], [SHORT, LONG], [SHORT] * (rows // SHORT)]
        made = [self.plan(way + [0] * (slots - len(way)), me) for way in ways for me in range(blocks)]
        self.at, at, columns = {}, 0, []
        for name in made[0]:
            size = max(len(m[name]) for m in made)
            self.at[name] = (at, size)
            at += size
            columns.append([m[name] + m[name][-1:] * (size - len(m[name])) for m in made])
        self.table = np.array([sum((c[n] for c in columns), []) for n in range(len(made))], np.int32)

    def plan(self, lengths, me):
        tile, owned, blocks, tiles = self.tile, self.owned, self.blocks, self.tiles
        ends = [int(e) for e in np.cumsum(lengths)]
        low = [max([e for e in ends if e <= t * tile], default=0) // tile for t in range(tiles)]
        last = [min(e for e in ends if e > t * tile) for t in range(tiles)]
        length = [e - max([f for f in ends if f < e], default=0) for e in last]
        cost = [t - low[t] + 1 for t in range(tiles)]
        homes = [[b * owned + t for t in range(owned)] for b in range(blocks)]
        works = [list(h) for h in homes]
        given = [[0], [0]]
        if self.count:
            options = list(itertools.combinations(range(owned), self.count))

            def apart(choice):
                a, b = choice
                gain = sum(cost[owned + t] for t in b) - sum(cost[t] for t in a)
                return abs(sum(cost[:owned]) - sum(cost[owned:]) + 2 * gain), -sum(a), sum(b)

            given = list(min(itertools.product(options, options), key=apart))
            for side in range(2):
                for t, u in zip(given[side], given[1 - side]):
                    works[side][t] = (1 - side) * owned + u
        own = works[me]
        slot = [own.index(t) if t in own else -1 for t in range(tiles)]
        loc = [((t // owned - me) % blocks) * owned + t % owned for t in range(tiles)]
        far = works[1 - me] if blocks == 2 else [t if t not in own else -1 for t in range(tiles)]
        pairs = [(i, j) for i in range(tiles) for j in range(low[i], i + 1)]
        forward = [(i, j) for i, j in pairs if slot[i] >= 0]
        backward, flags = [], []
        for j in range(tiles):
            mine = [(i, j) for i in reversed(range(j, tiles)) if slot[i] >= 0 and low[i] <= j]
            marks = [1] * len(mine)
            if not mine:
                mine, marks = [(j, j)], [0]
            marks[0] += 2
            marks[-1] += 4
            backward += mine
            flags += marks
        late = [(i, j) for i, j in forward if any(f > i and low[f] <= j for f in far)]
        return {
            "ends": ends,
            "length": length,
            "loc": loc,
            "slot": slot,
            "own": own,
            "own_at": [loc[t] for t in own],
            "slot_loc": [slot[loc.index(t)] for t in range(tiles)],
            "far": far,
            "given": list(given[me]) if self.count else [0],
            "taken": list(given[1 - me]) if self.count else [0],
            "all_n": [len(pairs)],
            "all_i": [i for i, _ in pairs],
            "all_j": [j for _, j in pairs],
            "fwd_i": [i for i, _ in forward],
            "fwd_j": [j for _, j in forward],
            "fwd_f": [1 + 2 * (j == low[i]) for i, j in forward] + [0],
            "bwd_i": [i for i, _ in backward],
            "bwd_j": [j for _, j in backward],
            "bwd_f": flags + [0],
            "late_n": [len(late)],
            "late_i": [i for i, _ in late] + [0],
            "late_j": [j for _, j in late] + [0],
        }

    def chosen(self, lengths, me):
        way = jnp.where(lengths[0] == LONG, 0, jnp.where(lengths[1] == LONG, 1, 2))
        return lax.dynamic_index_in_dim(jnp.array(self.table), way * self.blocks + me, 0, keepdims=False)

    def get(self, numbers, name, index):
        return numbers[self.at[name][0] + index]

    def part(self, numbers, name):
        at, size = self.at[name]
        return numbers[at : at + size]

    def size(self, name):
        return self.at[name][1]


def tile_marks(layout, numbers, i, j):
    tile = layout.tile
    row = lax.broadcasted_iota(jnp.int32, (tile, tile), 0)
    key = lax.broadcasted_iota(jnp.int32, (tile, tile), 1)
    if layout.aligned:
        apart = key - row
        ahead = jnp.where(i == j, 0, tile)
        length = jnp.full((1, 1), layout.get(numbers, "length", i), jnp.int32)
        return apart < ahead, apart <= ahead, 4.0 / length.astype(F32)
    places = i * tile + lax.broadcasted_iota(jnp.int32, (tile, 1), 0)
    start = jnp.zeros((tile, 1), jnp.int32)
    end = jnp.full((tile, 1), 2**30, jnp.int32)
    for n in range(layout.size("ends")):
        edge = layout.get(numbers, "ends", n)
        start = jnp.maximum(start, jnp.where(places >= edge, edge, 0))
        end = jnp.minimum(end, jnp.where(places < edge, edge, 2**30))
    inside = j * tile + key >= start
    apart = (j - i) * tile + key - row
    return inside & (apart < 0), inside & (apart <= 0), 4.0 / (end - start).astype(F32)


def head0_scores(q_pair, k_pair, tile):
    first, _ = half_masks(tile)
    return mm(jnp.where(first, q_pair, 0), k_pair, NT) * HEAD_DIM**-0.5


def before_sum(chosen, tile):
    rows = lax.broadcasted_iota(jnp.int32, (tile, tile), 0)
    cols = lax.broadcasted_iota(jnp.int32, (tile, tile), 1)
    lower = (cols < rows).astype(F32).astype(BF16)
    high, low = split2(chosen)
    above = mm(lower, high, NN) + mm(lower, low, NN)
    return above, above[tile - 1 :, :] + chosen[tile - 1 :, :]


def after_sum(values, tile):
    rows = lax.broadcasted_iota(jnp.int32, (tile, tile), 0)
    cols = lax.broadcasted_iota(jnp.int32, (tile, tile), 1)
    upper = (cols > rows).astype(F32).astype(BF16)
    high, low = split2(values)
    below = mm(upper, high, NN) + mm(upper, low, NN)
    return below, below[:1, :] + values[:1, :]


def project_kernel(x_ref, w_ref, gain_ref, *refs):
    q_ref, k_ref, v_ref, normed_ref, x_out_ref = refs[-5:]
    x_out_ref[0] = x_ref[0]
    width = x_ref.shape[2]
    normed = layer_norm(x_ref[0].astype(F32), gain_ref[...]).astype(BF16)
    normed_ref[0] = normed
    for part, ref in enumerate((q_ref, k_ref, v_ref)):
        ref[0] = mm(normed, w_ref[:, part * width : (part + 1) * width], NN).astype(BF16)


UNROLL = 4


def sums_kernel(layout, numbers, q_ref, k_ref, kept_ref, sums_ref, column):
    tile = layout.tile
    last = layout.size("all_i") - 1

    def group_step(group, carry):
        for n in range(UNROLL):
            at = jnp.minimum(group * UNROLL + n, last)
            i, j = layout.get(numbers, "all_i", at), layout.get(numbers, "all_j", at)
            at_i, at_j = layout.get(numbers, "loc", i), layout.get(numbers, "loc", j)
            strict, _, _ = tile_marks(layout, numbers, i, j)
            scores = head0_scores(q_ref[at_i], k_ref[at_j], tile)
            chosen = jnp.where(strict, jnp.maximum(scores, 0.0), 0.0)
            column[group * UNROLL + n] = jnp.sum(chosen, axis=0, keepdims=True)
        return carry

    count = layout.get(numbers, "all_n", 0)
    lax.fori_loop(0, lax.div(count + (UNROLL - 1), jnp.int32(UNROLL)), group_step, 0)
    sums_ref[...] = jnp.zeros_like(sums_ref)

    def add_step(n, carry):
        i, j = layout.get(numbers, "all_i", n), layout.get(numbers, "all_j", n)
        kept_ref[i, j] = sums_ref[j]
        sums_ref[j] += column[n]
        return carry

    lax.fori_loop(0, count, add_step, 0)


def forward_kernel(layout, numbers, q_ref, k_ref, v_ref, kept_ref, att_ref, inv_ref, acc, pen):
    tile = layout.tile
    step = pl.program_id(0)
    i, j = layout.get(numbers, "fwd_i", step), layout.get(numbers, "fwd_j", step)
    flag = layout.get(numbers, "fwd_f", step)
    halves = half_masks(tile)

    @pl.when((flag & 2) != 0)
    def _():
        acc[...] = jnp.zeros_like(acc)

    @pl.when((flag & 1) != 0)
    def _():
        def logits_of(head):
            pair, half = divmod(head, 2)
            at = slice(pair * PAIR, (pair + 1) * PAIR)
            return mm(jnp.where(halves[half], q_ref[0, :, at], 0), k_ref[0, :, at], NT)

        def gather(head, numer):
            pair, half = divmod(head, 2)
            at = slice(pair * PAIR, (pair + 1) * PAIR)
            acc[head] += mm(numer, jnp.where(halves[half], v_ref[0, :, at], 1), NN)

        raw = {head: logits_of(head) for head in range(3)}
        strict, allowed, rate = tile_marks(layout, numbers, i, j)
        chosen = jnp.where(strict, jnp.maximum(raw[0] * HEAD_DIM**-0.5, 0.0), 0.0)
        above, _ = before_sum(chosen, tile)
        pen[...] = jnp.where(allowed, (rate * LOG2E) * (kept_ref[i, j] + above), FAR)
        waiting = {}
        for head in range(HEADS + 2):
            if 3 <= head + 3 < HEADS:
                raw[head + 3] = logits_of(head + 3)
            if head < HEADS:
                waiting[head] = jnp.exp2(raw.pop(head) * (HEAD_DIM**-0.5 * LOG2E) - pen[...]).astype(BF16)
            if head >= 2:
                gather(head - 2, waiting.pop(head - 2))

        @pl.when(i == j)
        def _():
            for pair in range(PAIRS):
                at = slice(pair * PAIR, (pair + 1) * PAIR)
                low, high = acc[2 * pair], acc[2 * pair + 1]
                numer = jnp.where(halves[0], low, high)
                inverse = 1.0 / pltpu.roll(jnp.where(halves[0], high, low), HEAD_DIM, 1)
                att_ref[0, :, at] = numer * inverse
                inv_ref[0, :, at] = inverse


def middle_kernel(
    tile, owned, chunk,
    numbers, att_ref, inv_ref, x_ref, cot_ref, wo_ref, wu_ref, wd_ref, gain_ref,
    out_ref, branch_ref, dx_ref, grads_ref,
    hid_s, dpre_s, low_s, normed_s, branch_s, stage_down, stage_rest, sems,
):
    step = pl.program_id(0)
    width = x_ref.shape[2]
    hid = wu_ref.shape[1]
    parts = hid // width
    joined = len(stage_rest.shape) == 4

    def shipment(n):
        source = stage_down.at[n] if n < parts else stage_rest.at[n - parts]
        if not joined:
            target = grads_ref.at[n]
        elif n < parts:
            some, long = stage_down.shape[1:3]
            target = grads_ref.at[pl.ds(n * some, some), pl.ds(0, long), :]
        else:
            share = stage_rest.shape[2]
            target = grads_ref.at[:, pl.ds(share * n, share), :]
        return pltpu.make_async_copy(source, target, sems.at[n])

    def ship(n, block):
        stage, at = (stage_down, n) if n < parts else (stage_rest, n - parts)
        stage[at] = block.astype(BF16).reshape(stage.shape[1:])
        shipment(n).start()

    @pl.when(step < owned)
    def _():
        at = pl.ds(pl.multiple_of(step * tile, tile), tile)
        attended = att_ref[0]
        cot = cot_ref[at, :]
        gain = gain_ref[...]
        low = attended.astype(BF16)
        low_s[at, :] = low
        residual = x_ref[0].astype(F32) + mm(low, wo_ref[...], NN)
        centre = jnp.mean(residual, axis=1, keepdims=True)
        shifted = residual - centre
        scale = lax.rsqrt(jnp.mean(shifted * shifted, axis=1, keepdims=True) + LN_EPS)
        xhat = shifted * scale
        normed = (xhat * gain).astype(BF16)
        normed_s[at, :] = normed
        result = residual
        d_normed = jnp.zeros((tile, width), F32)
        for c in range(hid // chunk):
            cols = slice(c * chunk, (c + 1) * chunk)
            pre = mm(normed, wu_ref[:, cols], NN)
            square = pre * pre
            wave = jnp.tanh(pre * (GELU_C + (GELU_C * 0.044715) * square))
            rising = 0.5 + 0.5 * wave
            hidden = (pre * rising).astype(BF16)
            bend = pre * ((0.5 * GELU_C) + (1.5 * GELU_C * 0.044715) * square)
            d_pre = (mm(cot, wd_ref[cols, :], NT) * (rising + bend * (1.0 - wave * wave))).astype(BF16)
            hid_s[at, cols] = hidden
            dpre_s[at, cols] = d_pre
            result = result + mm(hidden, wd_ref[cols, :], NN)
            d_normed = d_normed + mm(d_pre, wu_ref[:, cols], NT)
        out_ref[0] = result.astype(BF16)
        grown = d_normed * gain
        mean_grown = jnp.mean(grown, axis=1, keepdims=True)
        mean_both = jnp.mean(grown * xhat, axis=1, keepdims=True)
        branch = (cot.astype(F32) + scale * (grown - mean_grown - xhat * mean_both)).astype(BF16)
        branch_ref[0] = branch
        branch_s[at, :] = branch
        d_attended = mm(branch, wo_ref[...], NT).astype(BF16).astype(F32)
        scaled = (d_attended * inv_ref[0]).astype(BF16)
        product = scaled.astype(F32) * attended
        rows = lax.broadcasted_iota(jnp.int32, (PAIR, 2 * PAIR), 0)
        cols = lax.broadcasted_iota(jnp.int32, (PAIR, 2 * PAIR), 1)
        block = cols // HEAD_DIM
        spread = jnp.where(block == jnp.where(rows < HEAD_DIM, 1, 2), -1.0, 0.0).astype(BF16)
        lane = lax.broadcasted_iota(jnp.int32, (tile, 2 * PAIR), 1) % HEAD_DIM
        first, _ = half_masks(tile)
        for pair in range(PAIRS):
            here = slice(pair * PAIR, (pair + 1) * PAIR)
            high, rest = split2(product[:, here])
            minus_dot = mm(high, spread, NN) + mm(rest, spread, NN)
            dot_high, dot_low = split2(minus_dot)
            side = jnp.where(lane == 0, dot_high, jnp.where(lane == 1, dot_low, 0))
            mine = scaled[:, here]
            base = 2 * pair * PAIR
            dx_ref[0, :, base : base + PAIR] = jnp.where(first, mine, side[:, :PAIR])
            dx_ref[0, :, base + PAIR : base + 2 * PAIR] = jnp.where(first, side[:, PAIR:], mine)

    for c in range(parts):
        @pl.when(step == owned + c)
        def _(c=c):
            cols = slice(c * width, (c + 1) * width)
            ship(c, mm(hid_s[:, cols], cot_ref[...], TN))
            ship(parts + c, mm(normed_s[...], dpre_s[:, cols], TN))
            if c == parts - 1:
                ship(2 * parts, mm(low_s[...], branch_s[...], TN))
                for n in range(2 * parts + 1):
                    shipment(n).wait()


def backward_kernel(
    layout, numbers, q_ref, k_ref, v_ref, dx_ref, kept_ref,
    dq_ref, dk_ref, dv_ref, later_ref,
    acc_q, acc_k, acc_v, pen, dpen, later,
):
    tile = layout.tile
    step = pl.program_id(0)
    i, j = layout.get(numbers, "bwd_i", step), layout.get(numbers, "bwd_j", step)
    flag = layout.get(numbers, "bwd_f", step)
    halves = half_masks(tile)

    @pl.when(step == 0)
    def _():
        acc_q[...] = jnp.zeros_like(acc_q)
        later_ref[...] = jnp.zeros_like(later_ref)

    @pl.when((flag & 2) != 0)
    def _():
        acc_k[...] = jnp.zeros_like(acc_k)
        acc_v[...] = jnp.zeros_like(acc_v)
        later[...] = jnp.zeros_like(later)

    @pl.when((flag & 1) != 0)
    def _():
        slot = layout.get(numbers, "slot", i)
        scores0 = head0_scores(q_ref[0, :, :PAIR], k_ref[0, :, :PAIR], tile)

        def products(pair):
            at = slice(pair * PAIR, (pair + 1) * PAIR)
            k_pair, q_pair, v_pair = k_ref[0, :, at], q_ref[0, :, at], v_ref[0, :, at]
            made = []
            for half in range(2):
                head = 2 * pair + half
                scores = scores0 if head == 0 else mm(jnp.where(halves[half], q_pair, 0), k_pair, NT) * HEAD_DIM**-0.5
                dx = dx_ref[0, :, head * PAIR : (head + 1) * PAIR]
                made.append((scores, mm(dx, jnp.where(halves[half], v_pair, 1), NT)))
            return made

        made = {PAIRS - 1: products(PAIRS - 1)}
        ready = {}
        strict, allowed, rate = tile_marks(layout, numbers, i, j)
        chosen = jnp.where(strict, jnp.maximum(scores0, 0.0), 0.0)
        above, _ = before_sum(chosen, tile)
        pen[...] = jnp.where(allowed, (rate * LOG2E) * (kept_ref[i, j] + above), FAR)

        def pointwise(pair, made):
            grads, weights = [], []
            for scores, d_probs in made:
                numer = jnp.exp2(scores * LOG2E - pen[...])
                weights.append(numer.astype(BF16))
                grads.append(numer * d_probs)
            both = grads[0] + grads[1]
            if pair == PAIRS - 1:
                dpen[...] = both
            elif pair > 0:
                dpen[...] += both
            else:
                below, total = after_sum(dpen[...] + both, tile)
                picked = strict & (scores0 > 0.0)
                grads[0] = grads[0] + jnp.where(picked, -rate * (later[...] + below), 0.0)
                later[...] = later[...] + total
                later_ref[slot, j] = total
            return weights, [g.astype(BF16) for g in grads]

        def collect(pair, weights, lows):
            at = slice(pair * PAIR, (pair + 1) * PAIR)
            k_pair, q_pair = k_ref[0, :, at], q_ref[0, :, at]
            d_q = None
            for half in range(2):
                head = 2 * pair + half
                part = slice(half * HEAD_DIM, (half + 1) * HEAD_DIM)
                head_at = slice(head * HEAD_DIM, (head + 1) * HEAD_DIM)
                dx = dx_ref[0, :, head * PAIR : (head + 1) * PAIR]
                acc_v[head_at, :] += mm(dx, weights[half], TN)[part]
                acc_k[head_at, :] += mm(q_pair, lows[half], TN)[part]
                more = mm(lows[half], jnp.where(halves[half], k_pair, 0), NN)
                d_q = more if d_q is None else d_q + more
            acc_q[slot, :, at] += d_q

        for pair in range(PAIRS - 1, -2, -1):
            if pair > 0:
                made[pair - 1] = products(pair - 1)
            if pair >= 0:
                ready[pair] = pointwise(pair, made.pop(pair))
            if pair + 1 in ready:
                collect(pair + 1, *ready.pop(pair + 1))

    @pl.when((flag & 4) != 0)
    def _():
        dk_ref[0] = jnp.transpose((acc_k[...] * HEAD_DIM**-0.5).astype(BF16))
        dv_ref[0] = jnp.transpose(acc_v[...].astype(BF16))

    @pl.when(step == pl.num_programs(0) - 1)
    def _():
        for slot in range(acc_q.shape[0]):
            dq_ref[slot] = (acc_q[slot] * HEAD_DIM**-0.5).astype(BF16)


def late_kernel(
    layout, numbers, q_ref, k_ref, far_totals_ref, dq_in_ref, dk_in_ref,
    dq_ref, dk_ref,
    acc_q, acc_k,
):
    tile = layout.tile
    first, _ = half_masks(tile)
    acc_q[...] = jnp.zeros_like(acc_q)
    acc_k[...] = jnp.zeros_like(acc_k)
    count = layout.get(numbers, "late_n", 0)

    def group_step(group, carry):
        adds = []
        for n in range(UNROLL):
            at = group * UNROLL + n
            valid = at < count
            at = jnp.minimum(at, layout.size("late_i") - 1)
            i, j = layout.get(numbers, "late_i", at), layout.get(numbers, "late_j", at)
            slot, at_i, at_j = (layout.get(numbers, name, t) for name, t in (("slot", i), ("loc", i), ("loc", j)))
            slot = jnp.maximum(slot, 0)
            later = jnp.zeros((1, tile), F32)
            for f in range(layout.size("far")):
                later += jnp.where(valid & (layout.get(numbers, "far", f) > i), far_totals_ref[f, j], 0.0)
            strict, _, rate = tile_marks(layout, numbers, i, j)
            scores = head0_scores(q_ref[at_i], k_ref[at_j], tile)
            factor = (-(HEAD_DIM**-0.5) * rate) * later
            d_low = jnp.where(strict & (scores > 0.0), factor, 0.0).astype(BF16)
            adds.append((slot, at_j, mm(q_ref[at_i], d_low, TN), mm(d_low, k_ref[at_j], NN)))
        for slot, at_j, for_k, for_q in adds:
            acc_k[at_j] += for_k
            acc_q[slot] += for_q
        return carry

    lax.fori_loop(0, lax.div(count + (UNROLL - 1), jnp.int32(UNROLL)), group_step, 0)
    for slot in range(acc_q.shape[0]):
        dq_ref[slot] = (dq_in_ref[slot].astype(F32) + jnp.where(first, acc_q[slot], 0.0)).astype(BF16)

    def finish(t, carry):
        dk_ref[t] = (dk_in_ref[t].astype(F32) + jnp.where(first, jnp.transpose(acc_k[t]), 0.0)).astype(BF16)
        return carry

    lax.fori_loop(0, acc_k.shape[0], finish, 0)


def through_weight(layout, base, numbers, dq_ref, dk_ref, dv_ref, w_ref):
    width = dq_ref.shape[2]
    slot = layout.get(numbers, "slot_loc", base + pl.program_id(0))
    d_query = jnp.where(slot >= 0, dq_ref[0], jnp.zeros_like(dq_ref[0]))
    return (
        mm(dv_ref[0], w_ref[:, 2 * width :], NT)
        + mm(dk_ref[0], w_ref[:, width : 2 * width], NT)
        + mm(d_query, w_ref[:, :width], NT)
    )


def away_kernel(layout, base, numbers, dq_ref, dk_ref, dv_ref, w_ref, out_ref):
    out_ref[0] = through_weight(layout, base, numbers, dq_ref, dk_ref, dv_ref, w_ref).astype(BF16)


def home_kernel(layout, numbers, dq_ref, dk_ref, dv_ref, w_ref, back_ref, x_ref, branch_ref, gain_ref, out_ref):
    values = x_ref[0].astype(F32)
    shifted = values - jnp.mean(values, axis=1, keepdims=True)
    scale = lax.rsqrt(jnp.mean(shifted * shifted, axis=1, keepdims=True) + LN_EPS)
    xhat = shifted * scale
    d_normed = through_weight(layout, 0, numbers, dq_ref, dk_ref, dv_ref, w_ref)
    grown = (d_normed + back_ref[0].astype(F32)) * gain_ref[...]
    mean_grown = jnp.mean(grown, axis=1, keepdims=True)
    mean_both = jnp.mean(grown * xhat, axis=1, keepdims=True)
    dx = scale * (grown - mean_grown - xhat * mean_both)
    out_ref[0] = (branch_ref[0].astype(F32) + dx).astype(BF16)


def flat(ref, cols):
    block = ref[:, :, cols]
    return block.reshape(block.shape[0] * block.shape[1], block.shape[2])


def value_weight_kernel(normed_ref, dk_ref, dv_ref, out_ref):
    width = normed_ref.shape[2]
    half = width // 2
    normed = flat(normed_ref, slice(None))
    out_ref[:, :half] = mm(normed, flat(dk_ref, slice(half, width)), TN).astype(BF16)
    out_ref[:, half:] = mm(normed, flat(dv_ref, slice(None)), TN).astype(BF16)


def query_weight_kernel(layout, numbers, normed_ref, dq_ref, dk_ref, out_ref):
    width = normed_ref.shape[2]
    half = width // 2
    total = jnp.zeros((width, width), F32)
    for slot in range(layout.owned):
        total += mm(normed_ref[layout.get(numbers, "own_at", slot)], dq_ref[slot], TN)
    out_ref[:, :width] = total.astype(BF16)
    out_ref[:, width:] = mm(flat(normed_ref, slice(None)), flat(dk_ref, slice(0, half)), TN).astype(BF16)


SMEM = pl.BlockSpec(memory_space=pltpu.SMEM)
VMEM = pl.BlockSpec(memory_space=pltpu.VMEM)


def estimate(flops):
    flops = int(flops)
    return pl.CostEstimate(flops=flops, bytes_accessed=flops // 600, transcendentals=0)


def held(shape):
    return pl.BlockSpec(shape, lambda *_: (0,) * len(shape), pipeline_mode=pl.Buffered(1))


def fixed(shape):
    return pl.BlockSpec(shape, lambda *_: (0,) * len(shape))


def in_hbm(shape, dtype):
    return pltpu.HBM(shape, dtype)


def stay(*arrays):
    return tuple(pltpu.with_memory_space_constraint(a, pltpu.HBM) for a in arrays)


def sds(shape, dtype):
    return jax.ShapeDtypeStruct(shape, dtype)


def project(x, weight, gain, tiles, first, into):
    owned, tile, width = x.shape
    outs = (sds((tiles, tile, width), BF16),) * 2 + (in_hbm((tiles, tile, width), BF16),) * 3
    row = pl.BlockSpec((1, tile, width), lambda s: (s, 0, 0))
    placed = pl.BlockSpec((1, tile, width), lambda s: (s + first, 0, 0))
    extra = [pl.BlockSpec(memory_space=pl.ANY)] * len(into)
    return pl.pallas_call(
        project_kernel,
        grid=(owned,),
        out_shape=outs,
        in_specs=[row, held(weight.shape), held(gain.shape)] + extra,
        out_specs=(placed,) * 5,
        input_output_aliases={3 + n: n for n in range(len(into))},
        compiler_params=pltpu.CompilerParams(vmem_limit_bytes=20 * 2**20),
        cost_estimate=estimate(2 * owned * tile * width * weight.shape[1]),
    )(x, weight, gain, *into)


def middle(layout, numbers, attended, inverse, x, cot, wo, wu, wd, gain, dp_count):
    owned, tile, width = attended.shape
    hid = wu.shape[1]
    parts = hid // width
    rows = owned * tile
    row = pl.BlockSpec((1, tile, width), lambda s, n: (jnp.minimum(s, owned - 1), 0, 0))
    wide = pl.BlockSpec((1, tile, 2 * width), lambda s, n: (jnp.minimum(s, owned - 1), 0, 0))

    def token_place(s, n):
        return layout.get(n, "own_at", jnp.minimum(s, owned - 1)), 0, 0

    share = width // dp_count
    joined = share % 16 == 0 and dp_count % parts == 0
    if joined:
        stage_down = (parts, dp_count // parts, share * parts, width)
        stage_rest = (parts + 1, dp_count, share, width)
        grads = (dp_count, share * (2 * parts + 1), width)
    else:
        stage_down, stage_rest, grads = ((n, width, width) for n in (parts, parts + 1, 2 * parts + 1))
    return kernel_call(
        functools.partial(middle_kernel, tile, owned, width), VMEM_LIMIT // 2**20, (owned + parts,), numbers,
        (attended, inverse, x, cot, wo, wu, wd, gain),
        [
            row, row, pl.BlockSpec((1, tile, width), token_place), held((rows, width)),
            held(wo.shape), held(wu.shape), held(wd.shape), held(gain.shape),
        ],
        (
            sds((owned, tile, width), BF16),
            sds((owned, tile, width), BF16),
            sds((owned, tile, 2 * width), BF16),
            sds(grads, BF16),
        ),
        (row, row, wide, pl.BlockSpec(memory_space=pl.ANY)),
        [
            pltpu.VMEM((rows, hid), BF16),
            pltpu.VMEM((rows, hid), BF16),
            pltpu.VMEM((rows, width), BF16),
            pltpu.VMEM((rows, width), BF16),
            pltpu.VMEM((rows, width), BF16),
            pltpu.VMEM(stage_down, BF16),
            pltpu.VMEM(stage_rest, BF16),
            pltpu.SemaphoreType.DMA((2 * parts + 1,)),
        ],
        2 * rows * width * (3 * width + 6 * hid),
    )


def kernel_call(kernel, room, grid, numbers, operands, in_specs, outs, out_specs, scratch, flops, aliases=None):
    return pl.pallas_call(
        kernel,
        grid_spec=pltpu.PrefetchScalarGridSpec(
            num_scalar_prefetch=1, grid=grid, in_specs=in_specs, out_specs=out_specs, scratch_shapes=scratch
        ),
        out_shape=outs,
        input_output_aliases=aliases or {},
        compiler_params=pltpu.CompilerParams(vmem_limit_bytes=room * 2**20),
        cost_estimate=estimate(flops),
    )(numbers, *operands)


def run_sums(layout, numbers, q, k):
    tiles, tile, _ = q.shape
    every = pl.BlockSpec((tiles, tile, PAIR), lambda n, x: (0, 0, 0))
    kept, sums = (tiles, tiles, 1, tile), (tiles, 1, tile)
    groups = -(-layout.size("all_i") // UNROLL) * UNROLL
    return kernel_call(
        functools.partial(sums_kernel, layout), 20, (1,), numbers, (q, k), [every, every],
        (sds(kept, F32), sds(sums, F32)), (fixed(kept), fixed(sums)),
        [pltpu.VMEM((groups, 1, tile), F32)], tiles * tiles * tile * tile * PAIR,
    )


def run_forward(layout, numbers, q, k, v, kept):
    tiles, tile, width = q.shape
    get, owned = layout.get, layout.owned
    rows = pl.BlockSpec((1, tile, width), lambda n, x: (get(x, "loc", get(x, "fwd_i", n)), 0, 0))
    keys = pl.BlockSpec((1, tile, width), lambda n, x: (get(x, "loc", get(x, "fwd_j", n)), 0, 0))
    slots = pl.BlockSpec((1, tile, width), lambda n, x: (get(x, "slot", get(x, "fwd_i", n)), 0, 0))
    return kernel_call(
        functools.partial(forward_kernel, layout), 20, (layout.size("fwd_i"),), numbers,
        (q, k, v, kept), [rows, keys, keys, fixed(kept.shape)],
        (in_hbm((owned, tile, width), F32),) * 2, (slots, slots),
        [pltpu.VMEM((HEADS, tile, PAIR), F32), pltpu.VMEM((tile, tile), F32)],
        4 * layout.size("fwd_i") * tile * tile * width,
    )


def run_backward(layout, numbers, q, k, v, dx, kept):
    tiles, tile, width = q.shape
    get, owned = layout.get, layout.owned
    rows = pl.BlockSpec((1, tile, width), lambda n, x: (get(x, "loc", get(x, "bwd_i", n)), 0, 0))
    keys = pl.BlockSpec((1, tile, width), lambda n, x: (get(x, "loc", get(x, "bwd_j", n)), 0, 0))
    slots = pl.BlockSpec(
        (1, tile, 2 * width), lambda n, x: (jnp.maximum(get(x, "slot", get(x, "bwd_i", n)), 0), 0, 0)
    )
    totals = (owned, tiles, 1, tile)
    return kernel_call(
        functools.partial(backward_kernel, layout), 28, (layout.size("bwd_i"),), numbers,
        (*stay(q, k, v), dx, kept), [rows, keys, keys, slots, fixed(kept.shape)],
        (
            sds((owned, tile, width), BF16),
            sds((tiles, tile, width), BF16),
            sds((tiles, tile, width), BF16),
            sds(totals, F32),
        ),
        (fixed((owned, tile, width)), keys, keys, fixed(totals)),
        [
            pltpu.VMEM((owned, tile, width), F32),
            pltpu.VMEM((width, tile), F32),
            pltpu.VMEM((width, tile), F32),
            pltpu.VMEM((tile, tile), F32),
            pltpu.VMEM((tile, tile), F32),
            pltpu.VMEM((1, tile), F32),
        ],
        10 * layout.size("bwd_i") * tile * tile * width,
    )


def run_late(layout, numbers, q, k, far_totals, dq, dk):
    tiles, tile, _ = q.shape
    owned = dq.shape[0]
    some = pl.BlockSpec((owned, tile, PAIR), lambda n, x: (0, 0, 0))
    every = pl.BlockSpec((tiles, tile, PAIR), lambda n, x: (0, 0, 0))
    return kernel_call(
        functools.partial(late_kernel, layout), 16, (1,), numbers,
        (q, k, far_totals, dq, dk), [every, every, fixed(far_totals.shape), some, every],
        (sds(dq.shape, BF16), sds(dk.shape, BF16)), (some, every),
        [pltpu.VMEM((owned, tile, PAIR), F32), pltpu.VMEM((tiles, PAIR, tile), F32)],
        6 * layout.size("late_i") * tile * tile * PAIR,
        {4: 0, 5: 1},
    )


def tile_specs(layout, base, width):
    tile = layout.tile
    row = pl.BlockSpec((1, tile, width), lambda s, x: (s, 0, 0))
    placed = pl.BlockSpec((1, tile, width), lambda s, x: (base + s, 0, 0))
    picked = pl.BlockSpec((1, tile, width), lambda s, x: (jnp.maximum(layout.get(x, "slot_loc", base + s), 0), 0, 0))
    return row, placed, picked


def run_away(layout, numbers, dq, dk, dv, weight):
    width, count, base = dq.shape[2], layout.tiles - layout.owned, layout.owned
    row, placed, picked = tile_specs(layout, base, width)
    return kernel_call(
        functools.partial(away_kernel, layout, base), 20, (count,), numbers, (dq, dk, dv, weight),
        [picked, placed, placed, held(weight.shape)], sds((count, layout.tile, width), BF16), row,
        [], 2 * count * layout.tile * width * weight.shape[1],
    )


def run_home(layout, numbers, dq, dk, dv, weight, back, x, branch, gain):
    width = dq.shape[2]
    row, placed, picked = tile_specs(layout, 0, width)
    return kernel_call(
        functools.partial(home_kernel, layout), 56, (layout.owned,), numbers,
        (dq, dk, dv, weight, back, x, branch, gain),
        [picked, placed, placed, held(weight.shape), row, row, row, held(gain.shape)],
        sds(x.shape, BF16), row, [], 2 * x.shape[0] * layout.tile * width * weight.shape[1],
    )


def value_weight_grad(normed, dk, dv):
    width = normed.shape[2]
    return pl.pallas_call(
        value_weight_kernel,
        out_shape=sds((width, 3 * width // 2), BF16),
        in_specs=[VMEM] * 3,
        out_specs=VMEM,
        compiler_params=pltpu.CompilerParams(vmem_limit_bytes=30 * 2**20),
        cost_estimate=estimate(3 * normed.shape[0] * normed.shape[1] * width * width),
    )(normed, dk, dv)


def query_weight_grad(layout, numbers, normed, dq, dk):
    width = normed.shape[2]
    return pl.pallas_call(
        functools.partial(query_weight_kernel, layout),
        out_shape=sds((width, 3 * width // 2), BF16),
        in_specs=[SMEM, VMEM, VMEM, VMEM],
        out_specs=VMEM,
        compiler_params=pltpu.CompilerParams(vmem_limit_bytes=28 * 2**20),
        cost_estimate=estimate(2 * normed.shape[0] * normed.shape[1] * width * width),
    )(numbers, normed, dq, dk)


def swap_seq(array):
    return lax.ppermute(array, "seq", [(0, 1), (1, 0)])


def powers(size):
    return [1 << n for n in range(size.bit_length() - 1)]


def is_power(size):
    return size & (size - 1) == 0


def scatter_halving(grad, order):
    count = lax.axis_size("dp")
    index = lax.axis_index("dp")
    bits = len(powers(count))
    held_bits = list(range(bits))[::-1]
    parts = grad.reshape((2,) * bits + grad.shape[1:])
    for n in order:
        axis = held_bits.index(n)
        held_bits.remove(n)
        mine = (index >> n) & 1
        keep = lax.dynamic_index_in_dim(parts, mine, axis, keepdims=False)
        send = lax.dynamic_index_in_dim(parts, 1 - mine, axis, keepdims=False)
        got = lax.ppermute(send, "dp", [(i, i ^ (1 << n)) for i in range(count)])
        parts = (keep.astype(F32) + got.astype(F32)).astype(BF16)
    return parts


def on_device(
    tokens, cotangent, lengths, threshold, attn_gain, qkv_weight, out_weight, mlp_gain, up_weight, down_weight
):
    _, block_len, width = tokens.shape
    blocks = lax.axis_size("seq")
    dp_count = lax.axis_size("dp")
    me = lax.axis_index("seq")
    tile = pick_tile(block_len)
    owned = block_len // tile
    tiles = owned * blocks
    rows = blocks * block_len
    hid = up_weight.shape[1]
    token_own = tokens[0]
    cot_own = cotangent[0]
    attn_gain = attn_gain.reshape(1, width)
    mlp_gain = mlp_gain.reshape(1, width)
    by_tile = (owned, tile, width)

    layout = Layout(rows, lengths.shape[1], tile, owned, blocks)
    count = layout.count
    numbers = layout.chosen(lengths[0], me)
    given = layout.part(numbers, "given")

    def put(array, pieces):
        for n in range(count):
            array = lax.dynamic_update_slice_in_dim(array, pieces[n][None], given[n], 0)
        return array

    def swap_tiles(array):
        if count == 0:
            return array
        sent = jnp.stack([lax.dynamic_index_in_dim(array, given[n], 0, False) for n in range(count)])
        return put(array, swap_seq(sent))

    x_own = token_own.reshape(by_tile)
    if blocks == 2:
        x_others = swap_seq(token_own).reshape(by_tile)
    else:
        gathered = lax.all_gather(token_own, "seq", axis=0, tiled=False)
        x_others = jnp.roll(gathered, -me, axis=0)[1:].reshape(tiles - owned, tile, width)
    cot_tiles, x_others = lax.optimization_barrier((cot_own.reshape(by_tile), x_others))
    cot = swap_tiles(cot_tiles).reshape(block_len, width)
    parts = project(x_own, qkv_weight, attn_gain, tiles, 0, ())
    q_all, k_all, v_all, normed_all, x_all = project(x_others, qkv_weight, attn_gain, tiles, owned, parts)

    kept, sums = run_sums(layout, numbers, q_all, k_all)
    attended, inverse = run_forward(layout, numbers, q_all, k_all, v_all, kept)
    limit = threshold[0].astype(F32) / 1024.0
    ends = jnp.cumsum(lengths[0])
    positions = jnp.arange(rows, dtype=jnp.int32)
    passed = positions[:, None] >= ends[None, :]
    start = jnp.max(jnp.where(passed, ends[None, :], 0), axis=1)
    end = jnp.min(jnp.where(passed, rows, ends[None, :]), axis=1)
    over = jnp.maximum(4.0 / (end - start).astype(F32) * sums.reshape(rows) - limit, 0.0)
    excess = jnp.full((1, 128), jnp.sum(jnp.where(positions // block_len == me, over, 0.0)))
    hops = [("dp", bit) for bit in powers(dp_count)] + [("seq", bit) for bit in powers(blocks)]
    if not (is_power(dp_count) and is_power(blocks)):
        excess, hops = lax.psum(excess, ("seq", "dp")), []

    def hop_beside(excess, result):
        if hops:
            axis, bit = hops.pop(0)
            excess += lax.ppermute(excess, axis, [(i, i ^ bit) for i in range(lax.axis_size(axis))])
        return lax.optimization_barrier((excess, result))


    out_c, branch_c, dx, early_grads = middle(
        layout, numbers, attended, inverse, x_all, cot, out_weight, up_weight, down_weight, mlp_gain, dp_count
    )
    output = swap_tiles(out_c)
    branch = swap_tiles(branch_c)
    parts_hid = hid // width
    if early_grads.shape[0] != dp_count or early_grads.ndim != 3 or early_grads.shape[1] == width:
        down_grad = early_grads[:parts_hid].reshape(dp_count, -1, width)
        rest = early_grads[parts_hid:].reshape(parts_hid + 1, dp_count, -1, width).transpose(1, 0, 2, 3)
        early_grads = jnp.concatenate([down_grad, rest.reshape(dp_count, -1, width)], axis=1)
    early = lax.psum_scatter(early_grads, "dp", scatter_dimension=0, tiled=False)

    dq, dk, dv, totals = run_backward(layout, numbers, q_all, k_all, v_all, dx, kept)
    excess, (dk, dv, output, branch) = hop_beside(excess, (dk, dv, output, branch))
    if blocks == 2:
        far_totals = swap_seq(totals)
    else:
        far_totals = lax.all_gather(totals, "seq", axis=0, tiled=True)
    value_grad = value_weight_grad(normed_all, dk, dv)
    excess, far_totals = hop_beside(excess, far_totals)
    dq, dk = run_late(layout, numbers, q_all, k_all, far_totals, dq, dk)

    away = run_away(layout, numbers, dq, dk, dv, qkv_weight)
    if blocks == 2:
        back = swap_seq(away)
    else:
        by_block = jnp.concatenate([jnp.zeros((owned, tile, width), BF16), away]).reshape(blocks, block_len, width)
        back = lax.psum_scatter(jnp.roll(by_block, me, axis=0), "seq", scatter_dimension=0, tiled=False)
        back = back.reshape(by_tile)
    away, dq, dk = lax.optimization_barrier((away, dq, dk))
    excess, dq = hop_beside(excess, dq)
    query_grad = query_weight_grad(layout, numbers, normed_all, dq, dk)
    def over_seq(piece):
        if blocks == 2:
            return piece.astype(F32) + swap_seq(piece).astype(F32)
        return lax.psum(piece, "seq").astype(F32)

    halves = [grad.reshape(dp_count, -1, 3 * width // 2) for grad in (query_grad, value_grad)]
    if is_power(dp_count) and dp_count > 1:
        bits = list(range(len(powers(dp_count))))
        halves = [scatter_halving(halves[0], bits), scatter_halving(halves[1], bits[:1] + bits[2:] + bits[1:2])]
    else:
        halves = [lax.psum_scatter(grad, "dp", scatter_dimension=0, tiled=False) for grad in halves]
    late = jnp.concatenate(halves, axis=1)
    _, late, early = lax.optimization_barrier((back, late, early))
    qkv_piece = over_seq(late)
    early = over_seq(early)
    input_grad = run_home(layout, numbers, dq, dk, dv, qkv_weight, back, x_own, branch, attn_gain)

    part = width // dp_count
    n_down = hid // dp_count
    down_piece = early[:n_down]
    up_piece = early[n_down : 2 * n_down].reshape(hid // width, part, width).transpose(1, 0, 2).reshape(part, hid)
    out_piece = early[2 * n_down :]
    at = lax.axis_index("dp") * part

    def gain_grad(weight, weight_grad, gain):
        mine = lax.dynamic_slice_in_dim(weight, at, part).astype(F32)
        return jnp.sum(mine * weight_grad, axis=1) / lax.dynamic_slice_in_dim(gain[0], at, part)

    attn_piece = gain_grad(qkv_weight, qkv_piece, attn_gain)
    mlp_piece = gain_grad(up_weight, up_piece, mlp_gain)
    while hops:
        excess, _ = hop_beside(excess, excess)
    excess = excess[0, :1] / (dp_count * rows)
    return (
        output.reshape(1, block_len, width),
        input_grad.reshape(1, block_len, width),
        attn_piece,
        qkv_piece,
        out_piece,
        mlp_piece,
        up_piece,
        down_piece,
        excess,
    )


def solution(mesh):
    return jax.shard_map(
        on_device,
        mesh=mesh,
        in_specs=(
            P("dp", "seq", None),
            P("dp", "seq", None),
            P("dp", None),
            P(),
            P(),
            P(),
            P(),
            P(),
            P(),
            P(),
        ),
        out_specs=(
            P("dp", "seq", None),
            P("dp", "seq", None),
            P("dp"),
            P("dp", None),
            P("dp", None),
            P("dp"),
            P("dp", None),
            P("dp", None),
            P(),
        ),
        check_vma=False,
    )
```
